256 devices in a mesh: dom: 64 (over z, y, core), rel: 4 (over x).
Axes of the slice: x: 4, y: 4, z: 8, core: 2. Of those that a mesh axis runs over, the one named last changes fastest.
Arguments:
- embeddings: float32 [131072, 400], P('dom'), may hold values from -3 to 3
- rel_weight: float32 [256, 400], P('rel'), may hold values from -4 to 4
- head_row: int32 [98304], P(('dom', 'rel')), may hold values from 0 to 2047
- rel_id: int32 [98304], P(('dom', 'rel')), may hold values from 0 to 63
- tail_owner: int32 [98304, 1], P(('dom', 'rel')), may hold values from 0 to 63; in each aligned block of 384 rows (0 to 383, 384 to 767, ...) at most 12 rows name the same one
- tail_row: int32 [98304], P(('dom', 'rel')), may hold values from 0 to 2047
- neg_owner: int32 [24576, 1], P('dom'), may hold values from 0 to 63; in each aligned block of 96 rows (0 to 95, 96 to 191, ...) at most 3 rows name the same one
- neg_row: int32 [24576], P('dom'), may hold values from 0 to 2047
Outputs:
- embedding_grad: float32 [131072, 400], P('dom')
- relation_grad: float32 [256, 400], P('rel')
The draws below stay inside these ranges and needn't reach their ends.
Inputs may be any that keep to these rules, and one draw needn't show every extreme that they name: `tail_owner`: in the rows of one device no partition is named more than 12 times, and it is reached. `neg_owner`: in each aligned block of 96 rows no partition is named more than 3 times, and it is reached.
All inputs are finite; a program needn't handle non-finite values.
Results may differ from the reference program's by a relative error of at most 0.0003.
Values sent between devices are 32-bit elements; how exact they have to be, the bound alone decides.
A program may use at most 64 MiB of HBM per device.

```python
import math
import jax
import jax.numpy as jnp
import numpy as np
from jax import lax

D = 400
SPAN = 128
NEG = 128
ENT_DEV = 2048
REL_DEV = 64
SPANS = 3
EDGE_DEV = 384
NEG_DOM = 384
QUARTER = 96
CAP_T = 12
CAP_Q = 3
NENT = 131072
NRELS = 256
N_DOM = 64
N_REL = 4


def draw_embeddings(key, part):
    first_key = jax.random.fold_in(key, 0)
    values = jnp.clip(jax.random.normal(first_key, (NENT, D), jnp.float32) * 0.3, -1.5, 1.5)
    return values.astype(jnp.float32)


def plant(result, rng, least, top_value):
    spot = [jax.random.randint(jax.random.fold_in(rng, axis), (), 0, length) for axis, length in enumerate(result.shape)]
    main_axis = result.shape.index(max(result.shape))
    neighbour = spot[:main_axis] + [(spot[main_axis] + 1) % result.shape[main_axis]] + spot[main_axis + 1:]
    return result.at[tuple(spot)].set(least).at[tuple(neighbour)].set(top_value)


def block_scale(stream_key, extent, cuts, low, top_value):
    factor_of, own = 1.0, jax.random.fold_in(stream_key, 6)
    for dim, blocks in cuts:
        steps = jnp.exp(jax.random.uniform(jax.random.fold_in(own, dim), (blocks,), jnp.float32, low / len(cuts), top_value / len(cuts)))
        factor_of = factor_of * jnp.repeat(steps, extent[dim] // blocks).reshape([-1 if axis == dim else 1 for axis in range(len(extent))])
    return factor_of


def assign_block(rng, own, number, rows, number_of, top, limit, lean):
    order = jax.random.permutation(rng, number_of)
    packed, common = load_shares(number_of, rows * top, limit, lean, True), load_shares(number_of, rows * top, limit, lean, False)
    places = jnp.arange(number_of)

    def named(lengths, offset_by):
        used = int((lengths > 0).sum())
        fixed = max(1, used // 4)
        passed = fixed + (places - fixed + offset_by * (used - fixed)) % max(1, number_of - fixed)
        return jnp.zeros((number_of,), jnp.int32).at[order[jnp.where(places < fixed, places, passed)]].set(jnp.asarray(lengths, jnp.int32))

    lengths = jnp.where(number % 4 == 0, named(packed, number // 4), named(common, number - number // 4 - 1))
    mixed = jax.random.permutation(jax.random.fold_in(own, 3), number_of)
    giver, taker = mixed[0:number_of // 2 * 2:2], mixed[1:number_of // 2 * 2:2]
    room = jnp.minimum(lengths[giver] - 1, limit - lengths[taker]) // 2
    room = jnp.where((giver == order[0]) | (taker == order[0]) | (lengths[taker] == 0), 0, jnp.maximum(room, 0))
    passed = jax.random.randint(jax.random.fold_in(own, 4), (number_of // 2,), 0, 1 << 20) % (room + 1)
    lengths = lengths.at[giver].add(-passed).at[taker].add(passed)
    members = jnp.searchsorted(jnp.cumsum(lengths), jnp.arange(rows * top), side="right").astype(jnp.int32)
    grid = members.reshape(top, rows).T
    grid = grid[jax.random.permutation(jax.random.fold_in(own, 1), rows)]
    offset_by = jax.random.randint(jax.random.fold_in(own, 2), (rows, 1), 0, top)
    return jnp.take_along_axis(grid, (jnp.arange(top)[None, :] + offset_by) % top, axis=1)


def load_shares(number_of, total, most, skew, full):
    weights = [(1 << 20) // math.isqrt(rank ** skew) + 1 for rank in range(1, number_of + 1)]
    largest = most if full else min(most, max(-(-total // number_of), total * weights[0] // sum(weights)))
    least = 1 if total - largest >= number_of - 1 else 0
    holding, rest = [largest] + [least] * (number_of - 1), total - largest - least * (number_of - 1)
    while rest > 0:
        candidates = [i for i in range(1, number_of) if holding[i] < largest] or [i for i in range(1, number_of) if holding[i] < most]
        whole, remaining = sum([weights[i] for i in candidates]), rest
        for i in candidates:
            extra = min(most - holding[i], max(1, remaining * weights[i] // whole), rest)
            holding[i] = holding[i] + extra
            rest = rest - extra
    return np.array(holding)


def normal_values(rng, shape, scale, most, shards=(), kind=jnp.bfloat16):
    gain = block_scale(rng, shape, shards, -0.22, 0.18) if shards else 1.0
    entries = jax.random.normal(rng, shape, jnp.float32) * scale * gain
    return jnp.minimum(jnp.maximum(entries, -most), most).astype(kind)


def setup_inputs(seed: int = 0) -> dict:
    key_of = jax.random.split(jax.random.key(seed), 9)
    embeddings = draw_embeddings(jax.random.fold_in(key_of[8], 71), 0)
    rel_weight = normal_values(key_of[1], (NRELS, D), 1.0, 4.0, ((0, 4),), jnp.float32)
    head_row = plant(jax.random.randint(key_of[2], (N_DOM * N_REL * EDGE_DEV,), 0, ENT_DEV), jax.random.fold_in(key_of[2], 1), 0, ENT_DEV - 1).astype(jnp.int32)
    rel_id = plant(jax.random.randint(key_of[3], (N_DOM * N_REL * EDGE_DEV,), 0, REL_DEV), jax.random.fold_in(key_of[3], 1), 0, REL_DEV - 1).astype(jnp.int32)
    tail_owner_keys = jax.random.split(jax.random.fold_in(key_of[4], 1), (N_DOM * N_REL * EDGE_DEV) // EDGE_DEV)
    tail_owner_turns = jax.random.permutation(jax.random.fold_in(key_of[4], 3), (N_DOM * N_REL * EDGE_DEV) // EDGE_DEV)
    tail_owner = jax.vmap(lambda own, number: assign_block(jax.random.fold_in(key_of[4], 2), own, number, EDGE_DEV, N_DOM, 1, CAP_T, 2))(tail_owner_keys, tail_owner_turns).reshape((N_DOM * N_REL * EDGE_DEV, 1))
    tail_row = plant(jax.random.randint(key_of[5], (N_DOM * N_REL * EDGE_DEV,), 0, ENT_DEV), jax.random.fold_in(key_of[5], 1), 0, ENT_DEV - 1).astype(jnp.int32)
    neg_owner_keys = jax.random.split(jax.random.fold_in(key_of[6], 1), (N_DOM * NEG_DOM) // QUARTER)
    neg_owner_turns = jax.random.permutation(jax.random.fold_in(key_of[6], 3), (N_DOM * NEG_DOM) // QUARTER)
    neg_owner = jax.vmap(lambda own, number: assign_block(jax.random.fold_in(key_of[6], 2), own, number, QUARTER, N_DOM, 1, CAP_Q, 2))(neg_owner_keys, neg_owner_turns).reshape((N_DOM * NEG_DOM, 1))
    neg_row = plant(jax.random.randint(key_of[7], (N_DOM * NEG_DOM,), 0, ENT_DEV), jax.random.fold_in(key_of[7], 1), 0, ENT_DEV - 1).astype(jnp.int32)
    return {"embeddings": embeddings, "rel_weight": rel_weight, "head_row": head_row, "rel_id": rel_id, "tail_owner": tail_owner, "tail_row": tail_row, "neg_owner": neg_owner, "neg_row": neg_row}


def span_grads(head_emb, rel_rows, tail_emb, neg_emb):
    queries = head_emb * rel_rows
    positive = jnp.sum(queries * tail_emb, axis=1)
    scores = jnp.dot(queries, neg_emb.T, precision=lax.Precision.HIGHEST)
    row_max = jnp.maximum(positive, jnp.max(scores, axis=1))
    pos_exp = jnp.exp(positive - row_max)
    neg_exp = jnp.exp(scores - row_max[:, None])
    total = pos_exp + jnp.sum(neg_exp, axis=1)
    pos_coef = pos_exp / total - 1.0
    neg_coef = neg_exp / total[:, None]
    grad_query = pos_coef[:, None] * tail_emb + jnp.dot(neg_coef, neg_emb, precision=lax.Precision.HIGHEST)
    grad_tail = pos_coef[:, None] * queries
    grad_neg = jnp.dot(neg_coef.T, queries, precision=lax.Precision.HIGHEST)
    return grad_query * rel_rows, grad_query * head_emb, grad_tail, grad_neg


def reference(embeddings, rel_weight, head_row, rel_id, tail_owner, tail_row, neg_owner, neg_row):
    heads = head_row.reshape(N_DOM, N_REL, SPANS, SPAN)
    relations = rel_id.reshape(N_DOM, N_REL, SPANS, SPAN)
    tails = (tail_owner[:, 0] * ENT_DEV + tail_row).reshape(N_DOM, N_REL, SPANS, SPAN)
    negatives = (neg_owner[:, 0] * ENT_DEV + neg_row).reshape(N_DOM, SPANS, NEG)

    def step(carry, step_index):
        emb_grad, rel_grad = carry
        dom_index = step_index // (N_REL * SPANS)
        rel_index = (step_index // SPANS) % N_REL
        span_index = step_index % SPANS
        head_ids = heads[dom_index, rel_index, span_index] + dom_index * ENT_DEV
        rel_ids = relations[dom_index, rel_index, span_index] + rel_index * REL_DEV
        tail_ids = tails[dom_index, rel_index, span_index]
        neg_ids = negatives[dom_index, span_index]
        grad_head, grad_rel, grad_tail, grad_neg = span_grads(
            embeddings[head_ids], rel_weight[rel_ids], embeddings[tail_ids], embeddings[neg_ids])
        emb_grad = emb_grad.at[head_ids].add(grad_head)
        emb_grad = emb_grad.at[tail_ids].add(grad_tail)
        emb_grad = emb_grad.at[neg_ids].add(grad_neg)
        rel_grad = rel_grad.at[rel_ids].add(grad_rel)
        return (emb_grad, rel_grad), None

    start = (jnp.zeros(embeddings.shape, jnp.float32), jnp.zeros(rel_weight.shape, jnp.float32))
    (emb_grad, rel_grad), unused = lax.scan(step, start, jnp.arange(N_DOM * N_REL * SPANS, dtype=jnp.int32))
    return emb_grad, rel_grad
```

```python
import functools

import jax
import jax.numpy as jnp
from jax import lax
from jax.experimental import pallas as pl
from jax.experimental.pallas import tpu as pltpu
from jax.sharding import PartitionSpec as P

SPAN = 128
MAIN = 384
WIDE = 512
SLOTS = 16
CAP_T = 12
F32, BF16, I32 = jnp.float32, jnp.bfloat16, jnp.int32
MESH = pl.DeviceIdType.MESH
HIGHEST = lax.Precision.HIGHEST
NN = (((1,), (0,)), ((), ()))
NT = (((1,), (1,)), ((), ()))
TN = (((0,), (0,)), ((), ()))


def iota(shape, dim):
    return lax.broadcasted_iota(I32, shape, dim)


def parts(x, count):
    out = []
    for _ in range(count - 1):
        hi = x.astype(BF16)
        out.append(hi)
        x = x - hi.astype(F32)
    return out + [x.astype(BF16)]


def dot(a, b, dims):
    return lax.dot_general(a, b, dims, preferred_element_type=F32)


def dot_parts(onehot, values, dims=NN):
    total = dot(onehot, values[0], dims)
    for v in values[1:]:
        total = total + dot(onehot, v, dims)
    return total


def column(row):
    n = row.shape[1]
    return jnp.broadcast_to(row.astype(F32), (8, n)).T[:, 0:1].astype(I32)


def onehot(mask):
    return jnp.where(mask, 1.0, 0.0).astype(BF16)


def fold_matrix(rows, cols):
    l, m = iota((rows, cols), 0), iota((rows, cols), 1)
    return onehot((l & 15) == m)


def spread_matrix(rows, cols):
    m, l = iota((rows, cols), 0), iota((rows, cols), 1)
    return onehot((l & 15) == m)


def route_kernel(owner_ref, row_ref, ids_ref, slot_ref):
    lists = owner_ref.shape[1]
    owner = owner_ref[...]
    same = column(owner) == owner
    earlier = iota((lists, lists), 0) < iota((lists, lists), 1)
    position = jnp.sum(jnp.where(same & earlier, 1, 0), axis=0, keepdims=True)
    negative = owner >= 64
    valid = owner < 128
    position = jnp.where(negative, position + CAP_T, position)
    owner = jnp.where(negative, owner - 64, owner)
    slot_ref[...] = jnp.where(valid, owner * SLOTS + position, -1)
    peers = ids_ref.shape[0]
    left = jnp.where((iota((peers, lists), 0) == owner) & valid, (row_ref[...] + 1).astype(F32), 0.0)
    right = jnp.where(iota((128, lists), 0) == position, 1.0, 0.0)
    ids = lax.dot_general(left, right, NT, precision=HIGHEST, preferred_element_type=F32)
    ids_ref[...] = (ids + 0.5).astype(I32) - 1


def id_column(ids):
    p = ids.shape[0]
    spread = jnp.broadcast_to(ids.astype(F32)[:, None, :], (p, SLOTS, 128))
    own = iota((p, SLOTS, 128), 1) == iota((p, SLOTS, 128), 2)
    return jnp.sum(jnp.where(own, spread, 0.0), axis=2, keepdims=True).reshape(p * SLOTS, 1).astype(I32)


def split_table(et_ref, tables, copies):
    width, rows = et_ref.shape

    @pl.loop(0, width // 16)
    def _(i):
        at = pl.multiple_of(i * 16, 16)
        for t, v in zip(tables, parts(et_ref[pl.ds(at, 16), :], 3), strict=True):
            t[pl.ds(at, 16), :] = v

    for t in tables:
        tail = t[MAIN : MAIN + 16, :]
        for k in range(1, 8):
            t[MAIN + 16 * k : MAIN + 16 * (k + 1), :] = tail if copies else jnp.zeros_like(tail)


def serve_kernel(ids_ref, et_ref, out_ref, hi_ref, mid_ref, lo_ref):
    tables = (hi_ref, mid_ref, lo_ref)
    split_table(et_ref, tables, True)
    rows = et_ref.shape[1]
    group = 16

    @pl.loop(0, ids_ref.shape[0] // group)
    def _(i):
        at = pl.multiple_of(i * group, group)
        ids = id_column(ids_ref[pl.ds(at, group), :])
        hot = onehot(iota((group * SLOTS, rows), 1) == ids)
        got = dot_parts(hot, [t[...] for t in tables], NT)
        slot = iota((group, SLOTS, 128), 1)
        lane = iota((group, SLOTS, 128), 2)
        rest = got[:, MAIN:].reshape(group, SLOTS, 128)
        rest = jnp.where((lane >> 4) == (slot & 7), rest, 0.0)
        low = jnp.sum(jnp.where(slot < 8, rest, 0.0), axis=1, keepdims=True)
        high = jnp.sum(jnp.where(slot < 8, 0.0, rest), axis=1, keepdims=True)
        for k, part in enumerate((low, high, jnp.zeros_like(low))):
            main = got[:, 128 * k : 128 * (k + 1)].reshape(group, SLOTS, 128)
            out_ref[pl.ds(at, group), :, 128 * k : 128 * (k + 1)] = jnp.where(slot == SLOTS - 1, part, main)


def heads_kernel(head_ref, rel_id_ref, et_ref, rel_ref, head_out, rel_out, hi_ref, mid_ref, lo_ref):
    tables = (hi_ref, mid_ref, lo_ref)
    split_table(et_ref, tables, False)
    edges, rows = head_ref.shape[1], et_ref.shape[1]
    hot = onehot(iota((edges, rows), 1) == column(head_ref[...]))
    head_out[...] = dot_parts(hot, [t[...] for t in tables], NT)
    groups, width = rel_ref.shape
    hot_rel = onehot(iota((edges, groups), 1) == column(rel_id_ref[...]))
    got = dot_parts(hot_rel, parts(rel_ref[...], 3))
    rel_out[...] = jnp.concatenate([got, jnp.zeros((edges, WIDE - width), F32)], axis=1)


def unpack_kernel(slot_ref, recv_ref, out_ref, neg_ref):
    lists = slot_ref.shape[1]
    peers = recv_ref.shape[0]
    slot = column(slot_ref[...])
    hot = onehot(iota((lists, peers * SLOTS), 1) == slot)
    main = dot_parts(hot, parts(recv_ref[...].reshape(peers * SLOTS, MAIN), 3))
    hot_peer = onehot(iota((lists, peers), 1) == (slot >> 4))
    rest = dot_parts(hot_peer, parts(recv_ref[:, SLOTS - 1, 0:256], 3))
    rest = jnp.where((iota((lists, 256), 1) >> 4) == (slot & 15), rest, 0.0)
    fold = fold_matrix(256, 128)
    rest = sum(dot(p, fold, NN) for p in parts(rest, 3))
    out_ref[:, 0:MAIN] = main[0 : out_ref.shape[0]]
    out_ref[:, MAIN:WIDE] = rest[0 : out_ref.shape[0]]
    first, count = out_ref.shape[0], neg_ref.shape[0]
    neg_ref[:, 0:MAIN] = main[first : first + count]
    neg_ref[:, MAIN:WIDE] = rest[first : first + count]


def grads_kernel(head_ref, relrow_ref, tail_ref, neg_ref, rel_id_ref, gh_ref, gt_ref, gn_ref, gr_ref):
    edges = head_ref.shape[0]
    groups = gr_ref.shape[0]
    for c in range(edges // SPAN):
        at = slice(c * SPAN, (c + 1) * SPAN)
        head, rel, tail, neg = head_ref[at], relrow_ref[at], tail_ref[at], neg_ref[at]
        queries = head * rel
        positive = jnp.sum(queries * tail, axis=1, keepdims=True)
        scores = lax.dot_general(queries, neg, NT, precision=HIGHEST, preferred_element_type=F32)
        row_max = jnp.maximum(positive, jnp.max(scores, axis=1, keepdims=True))
        pos_exp = jnp.exp(positive - row_max)
        neg_exp = jnp.exp(scores - row_max)
        total = pos_exp + jnp.sum(neg_exp, axis=1, keepdims=True)
        pos_coef = pos_exp / total - 1.0
        neg_coef = neg_exp / total
        grad_query = pos_coef * tail + lax.dot_general(neg_coef, neg, NN, precision=HIGHEST, preferred_element_type=F32)
        gh_ref[at] = grad_query * rel
        gt_ref[at] = pos_coef * queries
        gn_ref[at] = lax.dot_general(neg_coef.T, queries, NN, precision=HIGHEST, preferred_element_type=F32)
        hot = onehot(iota((groups, SPAN), 0) == rel_id_ref[:, at])
        part = dot_parts(hot, parts(grad_query * head, 3))
        if c == 0:
            gr_ref[...] = part
        else:
            gr_ref[...] += part


def pack_kernel(slot_ref, gt_ref, gn_ref, out_ref):
    lists = slot_ref.shape[1]
    peers = out_ref.shape[0]
    edges, quarter = gt_ref.shape[0], gn_ref.shape[0]
    slot = slot_ref[...]
    values = jnp.concatenate([gt_ref[...], gn_ref[...], jnp.zeros((lists - edges - quarter, WIDE), F32)], axis=0)
    hot = onehot(iota((peers * SLOTS, lists), 0) == slot)
    main = dot_parts(hot, parts(values[:, 0:MAIN], 3)).reshape(peers, SLOTS, MAIN)
    spread = spread_matrix(128, 256)
    rest = sum(dot(p, spread, NN) for p in parts(values[:, MAIN:WIDE], 3))
    rest = jnp.where((iota((lists, 256), 1) >> 4) == (column(slot) & 15), rest, 0.0)
    hot_peer = onehot(iota((peers, lists), 0) == (slot >> 4))
    rest = dot_parts(hot_peer, parts(rest, 3))
    rest = jnp.concatenate([rest, jnp.zeros((peers, MAIN - 256), F32)], axis=1)
    last = iota((peers, SLOTS, MAIN), 1) == SLOTS - 1
    out_ref[...] = jnp.where(last, rest[:, None, :], main)


def scatter_kernel(ids_ref, recv_ref, gh_ref, head_ref, out_ref, hi_ref, lo_ref):
    peers = recv_ref.shape[0]
    slots = peers * SLOTS
    edges = gh_ref.shape[0]
    width, rows = out_ref.shape
    for b in range(0, peers, 16):
        n = 16 * SLOTS
        rest = jnp.broadcast_to(recv_ref[b : b + 16, SLOTS - 1 : SLOTS, 0:256], (16, SLOTS, 256))
        mine = (iota((16, SLOTS, 256), 2) >> 4) == iota((16, SLOTS, 256), 1)
        rest = jnp.where(mine, rest, 0.0).reshape(n, 256)
        fold = fold_matrix(256, 128)
        rest = sum(dot(p, fold, NN) for p in parts(rest, 2))
        main = recv_ref[b : b + 16].reshape(n, MAIN)
        at = slice(b * SLOTS, (b + 16) * SLOTS)
        hi, lo = parts(main.T, 2)
        hi_ref[0:MAIN, at], lo_ref[0:MAIN, at] = hi, lo
        hi, lo = parts(rest.T, 2)
        hi_ref[MAIN:WIDE, at], lo_ref[MAIN:WIDE, at] = hi, lo
    hi, lo = parts(gh_ref[...].T, 2)
    hi_ref[:, slots:], lo_ref[:, slots:] = hi, lo
    ids = jnp.concatenate([id_column(ids_ref[...]), column(head_ref[...])], axis=0)
    step = 512

    @pl.loop(0, rows // step)
    def _(i):
        at = pl.multiple_of(i * step, step)
        hot = onehot(iota((slots + edges, step), 1) + at == ids)
        got = dot(hi_ref[...], hot, NN) + dot(lo_ref[...], hot, NN)
        out_ref[:, pl.ds(at, step)] = got[0:width]


def local_call(kernel, outs, scratch=(), vmem=48, flops=0, moved=0):
    single = not isinstance(outs, (list, tuple))
    return pl.pallas_call(
        kernel,
        out_shape=outs if single else tuple(outs),
        scratch_shapes=list(scratch),
        compiler_params=pltpu.CompilerParams(vmem_limit_bytes=vmem << 20),
        cost_estimate=pl.CostEstimate(flops=flops, bytes_accessed=moved, transcendentals=0),
        name=kernel.__name__.removesuffix("_kernel"),
    )


def shape(*dims, dtype=F32):
    return jax.ShapeDtypeStruct(dims, dtype)


def greet(n, me):
    barrier = pltpu.get_barrier_semaphore()
    for k in range(1, n):
        pl.semaphore_signal(barrier, inc=1, device_id={"rel": lax.rem(me + k, n)}, device_id_type=MESH)
    pl.semaphore_wait(barrier, n - 1)


def gather_kernel(n, in_ref, out_ref, send_sem, recv_sem, own_sem):
    me = lax.axis_index("rel")
    greet(n, me)
    copies = []
    for k in range(1, n):
        copy = pltpu.make_async_remote_copy(
            in_ref, out_ref.at[me], send_sem.at[k - 1], recv_sem.at[k - 1],
            device_id={"rel": lax.rem(me + k, n)}, device_id_type=MESH)
        copy.start()
        copies.append(copy)
    own = pltpu.make_async_copy(in_ref, out_ref.at[me], own_sem)
    own.start()
    own.wait()
    for copy in copies:
        copy.wait()


def reduce_kernel(n, in_ref, out_ref, held, send_sem, recv_sem):
    me = lax.axis_index("rel")
    greet(n, me)
    copies = []
    for k in range(1, n):
        peer = lax.rem(me + k, n)
        copy = pltpu.make_async_remote_copy(
            in_ref.at[peer], held.at[k - 1], send_sem.at[k - 1], recv_sem.at[k - 1],
            device_id={"rel": peer}, device_id_type=MESH)
        copy.start()
        copies.append(copy)
    for copy in copies:
        copy.wait()
    total = in_ref[me]
    for k in range(1, n):
        total = total + held[k - 1]
    out_ref[...] = total


def all_reduce_kernel(n, x_ref, out_ref, held, sums, send_sem, recv_sem):
    width, rows = x_ref.shape
    piece, half = rows // n, width // 2
    me = lax.axis_index("rel")
    right, left, far = lax.rem(me + 1, n), lax.rem(me + 3, n), lax.rem(me + 2, n)
    barrier = pltpu.get_barrier_semaphore()
    for peer in (right, left):
        pl.semaphore_signal(barrier, inc=1, device_id={"rel": peer}, device_id_type=MESH)
    pl.semaphore_wait(barrier, 2)

    def cols(j):
        return pl.ds(pl.multiple_of(j * piece, piece), piece)

    ways = ((right, left, slice(0, half), slice(half, width)), (left, right, slice(half, width), slice(0, half)))

    def send(way, slot, src, dst):
        copy = pltpu.make_async_remote_copy(
            src, dst, send_sem.at[way, slot], recv_sem.at[way, slot], device_id={"rel": ways[way][0]}, device_id_type=MESH)
        copy.start()
        return copy

    sent = {}
    for way, (to, _, mine, other) in enumerate(ways):
        sent[way, 0] = send(way, 0, x_ref.at[mine, cols(far)], held.at[way, 0])
        sent[way, 1] = send(way, 1, x_ref.at[other, cols(to)], held.at[way, 1])
    for way, (to, _, mine, other) in enumerate(ways):
        sent[way, 0].wait_recv()
        sums[way] = x_ref[mine, cols(to)] + held[way, 0]
        sent[way, 2] = send(way, 2, sums.at[way], held.at[way, 2])
    for way in range(2):
        sent[way, 1].wait_recv()
        sent[way, 2].wait_recv()
    out_ref[0:half, cols(me)] = x_ref[0:half, cols(me)] + held[0, 2] + held[1, 1]
    out_ref[half:width, cols(me)] = x_ref[half:width, cols(me)] + held[1, 2] + held[0, 1]
    for way, (to, back, mine, other) in enumerate(ways):
        sent[way, 3] = send(way, 3, out_ref.at[mine, cols(me)], out_ref.at[mine, cols(me)])
        sent[way, 4] = send(way, 4, out_ref.at[other, cols(me)], out_ref.at[other, cols(me)])
    for way, (to, back, mine, other) in enumerate(ways):
        sent[way, 3].wait_recv()
        sent[way, 5] = send(way, 5, out_ref.at[mine, cols(back)], out_ref.at[mine, cols(back)])
    for way in range(2):
        sent[way, 4].wait_recv()
        sent[way, 5].wait_recv()
    for copy in sent.values():
        copy.wait_send()


def remote_call(kernel, n, outs, scratch, collective_id, flops, moved):
    return pl.pallas_call(
        functools.partial(kernel, n),
        out_shape=outs,
        in_specs=[pl.BlockSpec(memory_space=pltpu.VMEM)],
        out_specs=pl.BlockSpec(memory_space=pltpu.VMEM),
        scratch_shapes=scratch,
        compiler_params=pltpu.CompilerParams(
            collective_id=collective_id, has_side_effects=True, vmem_limit_bytes=40 << 20),
        cost_estimate=pl.CostEstimate(flops=flops, bytes_accessed=moved, transcendentals=0),
        name=kernel.__name__.removesuffix("_kernel"),
    )


DMA = pltpu.SemaphoreType.DMA


def body(embeddings, rel_weight, head_row, rel_id, tail_owner, tail_row, neg_owner, neg_row):
    peers, n = lax.axis_size("dom"), lax.axis_size("rel")
    me = lax.axis_index("rel")
    rows, width = embeddings.shape
    edges, negs = head_row.shape[0], neg_row.shape[0]
    groups = rel_weight.shape[0]
    quarter = negs // n
    lists = WIDE
    spare = jnp.full((lists - edges - quarter,), 255, I32)
    own_owner = lax.dynamic_slice(neg_owner[:, 0], (me * quarter,), (quarter,))
    own_row = lax.dynamic_slice(neg_row, (me * quarter,), (quarter,))
    owners = jnp.concatenate([tail_owner[:, 0], own_owner + 64, spare]).reshape(1, lists)
    rows_asked = jnp.concatenate([tail_row, own_row, spare]).reshape(1, lists)
    et = embeddings.T
    head = head_row.reshape(1, edges)
    rel = rel_id.reshape(1, edges)

    ids, slot = local_call(route_kernel, (shape(peers, 128, dtype=I32), shape(1, lists, dtype=I32)))(owners, rows_asked)
    asked = lax.all_to_all(ids.reshape(peers, 1, 128), "dom", 0, 0, tiled=True).reshape(peers, 128)
    table = pltpu.VMEM((WIDE, rows), BF16)
    block = shape(peers, SLOTS, MAIN)
    served = local_call(serve_kernel, block, [table] * 3, flops=int(7e9), moved=5 << 20)(asked, et)
    got = lax.all_to_all(served, "dom", 0, 0, tiled=True)
    head_emb, rel_rows = local_call(
        heads_kernel, (shape(edges, WIDE), shape(edges, WIDE)), [table] * 3, flops=int(3e9), moved=5 << 20
    )(head, rel, et, rel_weight)
    tail_emb, neg_part = local_call(unpack_kernel, (shape(edges, WIDE), shape(quarter, WIDE)))(slot, got)
    neg_emb = remote_call(
        gather_kernel, n, shape(n, quarter, WIDE), [DMA((n - 1,)), DMA((n - 1,)), DMA(())], 0, 0, 1 << 20
    )(neg_part).reshape(negs, WIDE)
    gh, gt, gn, gr = local_call(
        grads_kernel, (shape(edges, WIDE), shape(edges, WIDE), shape(negs, WIDE), shape(groups, WIDE))
    )(head_emb, rel_rows, tail_emb, neg_emb, rel)
    gn_sum = remote_call(
        reduce_kernel, n, shape(quarter, WIDE),
        [pltpu.VMEM((n - 1, quarter, WIDE), F32), DMA((n - 1,)), DMA((n - 1,))], 1, 0, 1 << 20
    )(gn.reshape(n, quarter, WIDE))
    back = local_call(pack_kernel, block)(slot, gt, gn_sum)
    recv = lax.all_to_all(back, "dom", 0, 0, tiled=True)
    slab = local_call(
        scatter_kernel, shape(width, rows), [pltpu.VMEM((WIDE, peers * SLOTS + edges), BF16)] * 2,
        flops=int(6e9), moved=6 << 20,
    )(asked, recv, gh, head)
    piece, half = rows // n, width // 2
    total = remote_call(
        all_reduce_kernel, n, shape(width, rows),
        [pltpu.VMEM((2, 3, half, piece), F32), pltpu.VMEM((2, half, piece), F32), DMA((2, 6)), DMA((2, 6))], 2, 0, 10 << 20
    )(slab)
    rel_parts = lax.all_to_all(gr.reshape(peers, groups // peers, WIDE), "dom", 0, 0, tiled=True)
    rel_sum = jnp.sum(rel_parts, axis=0)
    relation = lax.all_gather(rel_sum, "dom", axis=0, tiled=True)[:, 0:width]
    return (total.T, relation)


def solution(mesh):
    return jax.shard_map(
        body,
        mesh=mesh,
        in_specs=(
            P("dom", None),
            P("rel", None),
            P(("dom", "rel")),
            P(("dom", "rel")),
            P(("dom", "rel"), None),
            P(("dom", "rel")),
            P("dom", None),
            P("dom"),
        ),
        out_specs=(P("dom", None), P("rel", None)),
        check_vma=False,
    )
```

```python
import jax
import jax.numpy as jnp
from jax import lax
from jax.experimental import pallas as pl
from jax.experimental.pallas import tpu as pltpu
from jax.sharding import PartitionSpec as P

SPAN = 128
MAIN = 384
WIDE = 512
SLOTS = 16
CAP_T = 12
F32, BF16, I32 = jnp.float32, jnp.bfloat16, jnp.int32
MESH = pl.DeviceIdType.MESH
HIGHEST = lax.Precision.HIGHEST
NN = (((1,), (0,)), ((), ()))
NT = (((1,), (1,)), ((), ()))
TN = (((0,), (0,)), ((), ()))


def iota(shape, dim):
    return lax.broadcasted_iota(I32, shape, dim)


def parts(x, count):
    out = []
    for _ in range(count - 1):
        hi = x.astype(BF16)
        out.append(hi)
        x = x - hi.astype(F32)
    return out + [x.astype(BF16)]


def dot(a, b, dims):
    return lax.dot_general(a, b, dims, preferred_element_type=F32)


def dot_parts(onehot, values, dims=NN):
    total = dot(onehot, values[0], dims)
    for v in values[1:]:
        total = total + dot(onehot, v, dims)
    return total


def column(row):
    n = row.shape[1]
    return jnp.broadcast_to(row.astype(F32), (8, n)).T[:, 0:1].astype(I32)


def onehot(mask):
    return jnp.where(mask, 1.0, 0.0).astype(BF16)


def fold_matrix(rows, cols):
    l, m = iota((rows, cols), 0), iota((rows, cols), 1)
    return onehot((l & 15) == m)


def spread_matrix(rows, cols):
    m, l = iota((rows, cols), 0), iota((rows, cols), 1)
    return onehot((l & 15) == m)


def steps(i):
    j, q = lax.div(i, 8), 7 - lax.rem(i, 8)
    t, odd = lax.div(j, 2), lax.rem(j, 2)
    return (1 - odd) * (4 - t) + odd * lax.rem(5 + t, 8), lax.div(q, 2), lax.rem(q, 2)


def plus(me, i):
    dz, dy, dc = steps(i)
    z, y, c = lax.div(me, 8), lax.rem(lax.div(me, 2), 4), lax.rem(me, 2)
    return lax.rem(z + dz, 8) * 8 + lax.rem(y + dy, 4) * 2 + lax.rem(c + dc, 2)


def minus(me, i):
    dz, dy, dc = steps(i)
    z, y, c = lax.div(me, 8), lax.rem(lax.div(me, 2), 4), lax.rem(me, 2)
    return lax.rem(z + 8 - dz, 8) * 8 + lax.rem(y + 4 - dy, 4) * 2 + lax.rem(c + dc, 2)


def number(me, owner):
    z, y, c = lax.div(me, 8), lax.rem(lax.div(me, 2), 4), lax.rem(me, 2)
    dz = ((owner >> 3) - z + 8) & 7
    dz = jnp.where(dz == 0, 8, dz)
    j = jnp.where(dz <= 4, 8 - 2 * dz, 2 * dz - 9)
    dy = (((owner >> 1) & 3) - y + 4) & 3
    dc = ((owner & 1) - c + 2) & 1
    return j * 8 + 7 - (dy * 2 + dc)


def id_column(ids):
    p = ids.shape[0]
    spread = jnp.broadcast_to(ids.astype(F32), (p, SLOTS, 128))
    own = iota((p, SLOTS, 128), 1) == iota((p, SLOTS, 128), 2)
    return jnp.sum(jnp.where(own, spread, 0.0), axis=2, keepdims=True).reshape(p * SLOTS, 1).astype(I32)


GROUP = 16
CHUNKS = 3


def kernel(
    towner_ref, trow_ref, nowner_ref, nrow_ref, head_ref, rel_id_ref, rel_ref, et_hbm,
    out_ref, rel_out,
    et_ref, hi_ref, mid_ref, lo_ref, oh_ref, ids_ref, asked_ref, served_ref, fetched_ref, got_ref, negs_ref,
    head_emb, rel_rows, gh_ref, gt_ref, gn_ref, gn_held, back_ref, recv_ref, vt_hi, vt_lo, slab_ref, held_ref, sums_ref,
    gr_ref, gr_recv, gr_sum,
    et_sem, ids_send, ids_recv, serve_send, serve_recv, neg_send, neg_recv, gn_send, gn_recv, back_send, back_recv,
    gr_send, gr_got, ag_send, ag_recv, ring_send, ring_recv,
):
    peers = ids_ref.shape[0]
    others = peers - 1
    n = negs_ref.shape[0]
    me, g = lax.axis_index("dom"), lax.axis_index("rel")
    edges, negs = head_ref.shape[1], nowner_ref.shape[1]
    quarter = negs // n
    lists = WIDE
    slots = peers * SLOTS
    width, rows = et_ref.shape
    tables = (hi_ref, mid_ref, lo_ref)

    load = pltpu.make_async_copy(et_hbm, et_ref, et_sem)
    load.start()
    barrier = pltpu.get_barrier_semaphore()

    @pl.loop(0, others)
    def _(i):
        pl.semaphore_signal(barrier, inc=1, device_id={"dom": plus(me, i)}, device_id_type=MESH)

    for k in range(1, n):
        pl.semaphore_signal(barrier, inc=1, device_id={"rel": lax.rem(g + k, n)}, device_id_type=MESH)

    def mine(ref):
        return sum(jnp.where(g == q, ref[:, quarter * q : quarter * (q + 1)], 0) for q in range(n))

    spare = jnp.zeros((1, lists - edges - quarter), I32)
    owner = jnp.concatenate([towner_ref[...], mine(nowner_ref) + 64, spare + 255], axis=1)
    asked_rows = jnp.concatenate([trow_ref[...], mine(nrow_ref), spare], axis=1)
    same = column(owner) == owner
    earlier = iota((lists, lists), 0) < iota((lists, lists), 1)
    position = jnp.sum(jnp.where(same & earlier, 1.0, 0.0), axis=0, keepdims=True).astype(I32)
    negative, valid = owner >= 64, owner < 128
    position = jnp.where(negative, position + CAP_T, position)
    peer = number(me, owner & 63)
    slot = jnp.where(valid, peer * SLOTS + position, -1)
    left = jnp.where((iota((peers, lists), 0) == peer) & valid, (asked_rows + 1).astype(F32), 0.0)
    right = jnp.where(iota((128, lists), 0) == position, 1.0, 0.0)
    ids = lax.dot_general(left, right, NT, precision=HIGHEST, preferred_element_type=F32)
    ids_ref[...] = ((ids + 0.5).astype(I32) - 1)[:, None, :]

    pl.semaphore_wait(barrier, others + n - 1)

    def dom_copy(src, dst, send, recv, device):
        return pltpu.make_async_remote_copy(
            src, dst, send, recv, device_id={"dom": device}, device_id_type=MESH)

    @pl.loop(0, others)
    def _(i):
        dom_copy(ids_ref.at[i], asked_ref.at[i], ids_send, ids_recv, plus(me, i)).start()

    pltpu.make_async_copy(ids_ref.at[others], asked_ref.at[others], ids_recv).start()

    load.wait()

    @pl.loop(0, width // 16)
    def _(i):
        at = pl.multiple_of(i * 16, 16)
        for t, v in zip(tables, parts(et_ref[pl.ds(at, 16), :], 3), strict=True):
            t[pl.ds(at, 16), :] = v

    for t in tables:
        for k in range(1, 8):
            t[MAIN + 16 * k : MAIN + 16 * (k + 1), :] = t[MAIN : MAIN + 16, :]

    pltpu.make_async_copy(ids_ref, asked_ref, ids_recv).wait()

    @pl.loop(0, peers // GROUP)
    def _(b):
        at = pl.multiple_of(b * GROUP, GROUP)
        col = id_column(asked_ref[pl.ds(at, GROUP)])
        hot = onehot(iota((GROUP * SLOTS, rows), 1) == col)
        oh_ref[pl.ds(pl.multiple_of(b * GROUP * SLOTS, GROUP * SLOTS), GROUP * SLOTS), :] = hot
        got = dot_parts(hot, [t[...] for t in tables], NT)
        place = iota((GROUP, SLOTS, 128), 1)
        lane = iota((GROUP, SLOTS, 128), 2)
        rest = got[:, MAIN:].reshape(GROUP, SLOTS, 128)
        rest = jnp.where((lane >> 4) == (place & 7), rest, 0.0)
        low = jnp.sum(jnp.where(place < 8, rest, 0.0), axis=1, keepdims=True)
        high = jnp.sum(jnp.where(place < 8, 0.0, rest), axis=1, keepdims=True)
        for k, part in enumerate((low, high, jnp.zeros_like(low))):
            main = got[:, 128 * k : 128 * (k + 1)].reshape(GROUP, SLOTS, 128)
            served_ref[pl.ds(at, GROUP), :, 128 * k : 128 * (k + 1)] = jnp.where(place == SLOTS - 1, part, main)

        @pl.loop(0, GROUP)
        def _(k):
            i = b * GROUP + k

            @pl.when(i < others)
            def _():
                dom_copy(served_ref.at[i], fetched_ref.at[i], serve_send, serve_recv.at[b], minus(me, i)).start()

    last = peers // GROUP - 1
    pltpu.make_async_copy(served_ref.at[others], fetched_ref.at[others], serve_recv.at[last]).start()

    hot = onehot(iota((edges, rows), 1) == column(head_ref[...]))
    oh_ref[slots:, :] = hot
    got = dot_parts(hot, [t[...] for t in tables], NT)
    head_emb[:, 0:MAIN] = got[:, 0:MAIN]
    head_emb[:, MAIN:WIDE] = jnp.where(iota((edges, 128), 1) < width - MAIN, got[:, MAIN:WIDE], 0.0)
    groups = rel_ref.shape[0]
    hot = onehot(iota((edges, groups), 1) == column(rel_id_ref[...]))
    rel_rows[:, 0:width] = dot_parts(hot, parts(rel_ref[...], 3))
    rel_rows[:, width:WIDE] = jnp.zeros((edges, WIDE - width), F32)

    slot_col = column(slot)
    got_ref[...] = jnp.zeros_like(got_ref)

    @pl.loop(0, peers // GROUP)
    def _(b):
        at = pl.ds(pl.multiple_of(b * GROUP, GROUP), GROUP)
        pltpu.make_async_copy(served_ref.at[at], fetched_ref.at[at], serve_recv.at[b]).wait()
        hot = onehot(iota((lists, GROUP * SLOTS), 1) + b * (GROUP * SLOTS) == slot_col)
        got_ref[:, 0:MAIN] += dot_parts(hot, parts(fetched_ref[at].reshape(GROUP * SLOTS, MAIN), 3))

    hot_peer = onehot(iota((lists, peers), 1) == (slot_col >> 4))
    rest = dot_parts(hot_peer, parts(fetched_ref[:, SLOTS - 1, 0:256], 3))
    rest = jnp.where((iota((lists, 256), 1) >> 4) == (slot_col & 15), rest, 0.0)
    fold = fold_matrix(256, 128)
    got_ref[:, MAIN:WIDE] = sum(dot(p, fold, NN) for p in parts(rest, 3))

    negs_ref[g] = got_ref[edges : edges + quarter, :]

    def rel_copy(src, dst, send, recv, k):
        return pltpu.make_async_remote_copy(
            src, dst, send, recv, device_id={"rel": lax.rem(g + k, n)}, device_id_type=MESH)

    copies = [rel_copy(negs_ref.at[g], negs_ref.at[g], neg_send.at[k - 1], neg_recv.at[k - 1], k) for k in range(1, n)]
    for copy in copies:
        copy.start()
    for copy in copies:
        copy.wait_recv()
    sent = list(copies)

    def neg_rows(c):
        return negs_ref[...].reshape(negs, WIDE)[c * SPAN : (c + 1) * SPAN]

    gn_parts = []
    for c in range(edges // SPAN):
        at = slice(c * SPAN, (c + 1) * SPAN)
        head, rel, tail, neg = head_emb[at], rel_rows[at], got_ref[at], neg_rows(c)
        queries = head * rel
        positive = jnp.sum(queries * tail, axis=1, keepdims=True)
        scores = lax.dot_general(queries, neg, NT, precision=HIGHEST, preferred_element_type=F32)
        row_max = jnp.maximum(positive, jnp.max(scores, axis=1, keepdims=True))
        pos_exp = jnp.exp(positive - row_max)
        neg_exp = jnp.exp(scores - row_max)
        total = pos_exp + jnp.sum(neg_exp, axis=1, keepdims=True)
        pos_coef = pos_exp / total - 1.0
        neg_coef = neg_exp / total
        grad_query = pos_coef * tail + lax.dot_general(
            neg_coef, neg, NN, precision=HIGHEST, preferred_element_type=F32)
        gh_ref[at] = grad_query * rel
        gt_ref[at] = pos_coef * queries
        grad_neg = lax.dot_general(neg_coef.T, queries, NN, precision=HIGHEST, preferred_element_type=F32)
        first = c * SPAN
        while first < (c + 1) * SPAN:
            q, inside = divmod(first, quarter)
            count = min(quarter - inside, (c + 1) * SPAN - first)
            gn_ref[q, inside : inside + count] = grad_neg[first - c * SPAN : first - c * SPAN + count]
            first += count
        hot = onehot(iota((groups, SPAN), 0) == rel_id_ref[:, at])
        part = dot_parts(hot, parts(grad_query * head, 3))
        gn_parts.append(part)
    gr_ref[...] = sum(gn_parts)[:, None, :]

    copies = [
        rel_copy(gn_ref.at[lax.rem(g + k, n)], gn_held.at[k - 1], gn_send.at[k - 1], gn_recv.at[k - 1], k) for k in range(1, n)
    ]
    for copy in copies:
        copy.start()

    @pl.loop(0, others)
    def _(i):
        to = plus(me, i)
        dom_copy(gr_ref.at[to], gr_recv.at[i], gr_send, gr_got, to).start()

    pltpu.make_async_copy(gr_ref.at[me], gr_recv.at[others], gr_got).start()

    hot = onehot(iota((slots, lists), 0) == slot)
    hot_peer = onehot(iota((peers, lists), 0) == (slot >> 4))
    for copy in copies:
        copy.wait_recv()
    sent += copies
    grad_neg = gn_ref[g] + gn_held[0] + gn_held[1] + gn_held[2]
    values = jnp.concatenate([gt_ref[...], grad_neg, jnp.zeros((lists - edges - quarter, WIDE), F32)], axis=0)
    rest = sum(dot(p, spread_matrix(128, 256), NN) for p in parts(values[:, MAIN:WIDE], 3))
    rest = jnp.where((iota((lists, 256), 1) >> 4) == (slot_col & 15), rest, 0.0)
    rest = dot_parts(hot_peer, parts(rest, 3))
    place = iota((peers, SLOTS, 128), 1)
    for k in range(CHUNKS):
        main = dot_parts(hot, parts(values[:, 128 * k : 128 * (k + 1)], 2)).reshape(peers, SLOTS, 128)
        if k < 2:
            main = jnp.where(place == SLOTS - 1, rest[:, 128 * k : 128 * (k + 1)][:, None, :], main)
        back_ref[k] = main

        @pl.loop(0, others)
        def _(i, k=k):
            dom_copy(back_ref.at[k, i], recv_ref.at[k, i], back_send, back_recv.at[k], plus(me, i)).start()

        pltpu.make_async_copy(back_ref.at[k, others], recv_ref.at[k, others], back_recv.at[k]).start()

    piece = rows // n
    right_hand, left_hand, far = lax.rem(g + 1, n), lax.rem(g + 3, n), lax.rem(g + 2, n)
    first_row = [128 * k for k in range(CHUNKS)]
    height = [128] * (CHUNKS - 1) + [width - 128 * (CHUNKS - 1)]

    def cols(j):
        return pl.ds(pl.multiple_of(j * piece, piece), piece)

    ring = {}
    to_of, back_of = (right_hand, left_hand), (left_hand, right_hand)

    def half(k, way, mine):
        h = height[k] // 2
        low = (way == 0) == mine
        return slice(first_row[k], first_row[k] + h) if low else slice(first_row[k] + h, first_row[k] + 2 * h)

    def send(k, way, step, src, dst):
        copy = pltpu.make_async_remote_copy(
            src, dst, ring_send.at[k, way, step], ring_recv.at[k, way, step],
            device_id={"rel": to_of[way]}, device_id_type=MESH)
        copy.start()
        ring[k, way, step] = copy

    def scatter(k):
        pltpu.make_async_copy(back_ref.at[k], recv_ref.at[k], back_recv.at[k]).wait()
        values = [recv_ref[k].reshape(slots, 128).T, gh_ref[:, 128 * k : 128 * (k + 1)].T]
        vt = jnp.concatenate(values, axis=1)
        if k == CHUNKS - 1:
            rest = jnp.concatenate([recv_ref[0, :, SLOTS - 1, :], recv_ref[1, :, SLOTS - 1, :]], axis=1)
            rest = jnp.broadcast_to(rest[:, None, :], (peers, SLOTS, 256))
            own = (iota((peers, SLOTS, 256), 2) >> 4) == iota((peers, SLOTS, 256), 1)
            rest = jnp.where(own, rest, 0.0).reshape(slots, 256)
            rest = sum(dot(p, fold, NN) for p in parts(rest, 2))
            more = jnp.concatenate([rest.T[0:16], gh_ref[:, MAIN:WIDE].T[0:16]], axis=1)
            vt = jnp.concatenate([vt, more], axis=0)
        h = height[k]
        vt_hi[0:h], vt_lo[0:h] = parts(vt, 2)

        @pl.loop(0, n)
        def _(j):
            at = cols(j)
            slab_ref[first_row[k] : first_row[k] + h, at] = dot(vt_hi[0:h], oh_ref[:, at], NN) + dot(
                vt_lo[0:h], oh_ref[:, at], NN)

    def begin(k):
        h = height[k] // 2
        for way in range(2):
            send(k, way, 0, slab_ref.at[half(k, way, True), cols(far)], held_ref.at[k, way, 0, 0:h])
            send(k, way, 1, slab_ref.at[half(k, way, False), cols(to_of[way])], held_ref.at[k, way, 1, 0:h])

    def add(k):
        h = height[k] // 2
        for way in range(2):
            ring[k, way, 0].wait_recv()
            sums_ref[k, way, 0:h] = slab_ref[half(k, way, True), cols(to_of[way])] + held_ref[k, way, 0, 0:h]
            send(k, way, 2, sums_ref.at[k, way, 0:h], held_ref.at[k, way, 2, 0:h])

    def share(k):
        h = height[k] // 2
        for way in range(2):
            ring[k, way, 1].wait_recv()
            ring[k, way, 2].wait_recv()
        for way in range(2):
            at = half(k, way, True)
            out_ref[at, cols(g)] = slab_ref[at, cols(g)] + held_ref[k, way, 2, 0:h] + held_ref[k, 1 - way, 1, 0:h]
        for way in range(2):
            for step, mine_too in ((3, True), (4, False)):
                at = half(k, way, mine_too)
                send(k, way, step, out_ref.at[at, cols(g)], out_ref.at[at, cols(g)])

    def forward(k):
        for way in range(2):
            ring[k, way, 3].wait_recv()
            at = half(k, way, True)
            send(k, way, 5, out_ref.at[at, cols(back_of[way])], out_ref.at[at, cols(back_of[way])])

    scatter(0)
    begin(0)
    pltpu.make_async_copy(gr_ref, gr_recv, gr_got).wait()
    gr_sum[0] = jnp.sum(gr_recv[...], axis=0)

    @pl.loop(0, others)
    def _(i):
        dom_copy(gr_sum.at[0], rel_out.at[me], ag_send, ag_recv, plus(me, i)).start()

    pltpu.make_async_copy(gr_sum.at[0], rel_out.at[me], ag_recv).start()
    add(0)
    scatter(1)
    begin(1)
    share(0)
    add(1)
    scatter(2)
    begin(2)
    forward(0)
    share(1)
    add(2)
    forward(1)
    share(2)
    forward(2)
    for k in range(CHUNKS):
        for way in range(2):
            ring[k, way, 4].wait_recv()
            ring[k, way, 5].wait_recv()
    pltpu.make_async_copy(gr_ref, rel_out, ag_recv).wait()

    for copy in [*sent, *ring.values()]:
        copy.wait_send()
    first = pl.ds(0, others)
    pltpu.make_async_copy(ids_ref.at[first], ids_ref.at[first], ids_send).wait()
    pltpu.make_async_copy(served_ref.at[first], served_ref.at[first], serve_send).wait()
    pltpu.make_async_copy(gr_ref.at[first], gr_ref.at[first], gr_send).wait()
    pltpu.make_async_copy(gr_ref.at[first], gr_ref.at[first], ag_send).wait()
    for k in range(CHUNKS):
        pltpu.make_async_copy(back_ref.at[k, first], back_ref.at[k, first], back_send).wait()


def body(embeddings, rel_weight, head_row, rel_id, tail_owner, tail_row, neg_owner, neg_row):
    peers, n = lax.axis_size("dom"), lax.axis_size("rel")
    rows, width = embeddings.shape
    edges, negs = head_row.shape[0], neg_row.shape[0]
    groups = rel_weight.shape[0]
    quarter = negs // n
    lists = WIDE
    slots = peers * SLOTS
    tall = (width - 128 * (CHUNKS - 1)) // 2
    V, DMA = pltpu.VMEM, pltpu.SemaphoreType.DMA
    vmem, anywhere = pl.BlockSpec(memory_space=pltpu.VMEM), pl.BlockSpec(memory_space=pl.ANY)
    scratch = [
        V((width, rows), F32), V((WIDE, rows), BF16), V((WIDE, rows), BF16), V((WIDE, rows), BF16),
        V((slots + edges, rows), BF16), V((peers, 1, 128), I32), V((peers, 1, 128), I32),
        V((peers, SLOTS, MAIN), F32), V((peers, SLOTS, MAIN), F32), V((lists, WIDE), F32), V((n, quarter, WIDE), F32),
        V((edges, WIDE), F32), V((edges, WIDE), F32), V((edges, WIDE), F32), V((edges, WIDE), F32),
        V((n, quarter, WIDE), F32), V((n - 1, quarter, WIDE), F32),
        V((CHUNKS, peers, SLOTS, 128), F32), V((CHUNKS, peers, SLOTS, 128), F32),
        V((2 * tall, slots + edges), BF16), V((2 * tall, slots + edges), BF16),
        V((width, rows), F32), V((CHUNKS, 2, 3, tall, rows // n), F32), V((CHUNKS, 2, tall, rows // n), F32),
        V((groups, 1, WIDE), F32), V((peers, 1, WIDE), F32), V((1, 1, WIDE), F32),
        DMA(()), DMA(()), DMA(()), DMA(()), DMA((peers // GROUP,)), DMA((n - 1,)), DMA((n - 1,)), DMA((n - 1,)), DMA((n - 1,)),
        DMA(()), DMA((CHUNKS,)), DMA(()), DMA(()), DMA(()), DMA(()), DMA((CHUNKS, 2, 6)), DMA((CHUNKS, 2, 6)),
    ]
    total, relation = pl.pallas_call(
        kernel,
        out_shape=(jax.ShapeDtypeStruct((width, rows), F32), jax.ShapeDtypeStruct((groups, 1, WIDE), F32)),
        in_specs=[vmem] * 7 + [anywhere],
        out_specs=(vmem, vmem),
        scratch_shapes=scratch,
        compiler_params=pltpu.CompilerParams(collective_id=0, has_side_effects=True, vmem_limit_bytes=58 << 20),
        cost_estimate=pl.CostEstimate(flops=int(3e10), bytes_accessed=7 << 20, transcendentals=0),
        name="ranking_gradients",
    )(
        tail_owner.reshape(1, edges), tail_row.reshape(1, edges), neg_owner.reshape(1, negs), neg_row.reshape(1, negs),
        head_row.reshape(1, edges), rel_id.reshape(1, edges), rel_weight, embeddings.T)
    return (total.T, relation.reshape(groups, WIDE)[:, 0:width])


def solution(mesh):
    return jax.shard_map(
        body,
        mesh=mesh,
        in_specs=(
            P("dom", None),
            P("rel", None),
            P(("dom", "rel")),
            P(("dom", "rel")),
            P(("dom", "rel"), None),
            P(("dom", "rel")),
            P("dom", None),
            P("dom"),
        ),
        out_specs=(P("dom", None), P("rel", None)),
        check_vma=False,
    )
```

```python
import jax
import jax.numpy as jnp
from jax import lax
from jax.experimental import pallas as pl
from jax.experimental.pallas import tpu as pltpu
from jax.sharding import PartitionSpec as P

SPAN = 128
MAIN = 384
WIDE = 512
SLOTS = 16
CAP_T = 12
F32, BF16, I32 = jnp.float32, jnp.bfloat16, jnp.int32
MESH = pl.DeviceIdType.MESH
HIGHEST = lax.Precision.HIGHEST
NN = (((1,), (0,)), ((), ()))
NT = (((1,), (1,)), ((), ()))
TN = (((0,), (0,)), ((), ()))


def iota(shape, dim):
    return lax.broadcasted_iota(I32, shape, dim)


def parts(x, count):
    out = []
    for _ in range(count - 1):
        hi = x.astype(BF16)
        out.append(hi)
        x = x - hi.astype(F32)
    return out + [x.astype(BF16)]


def dot(a, b, dims):
    return lax.dot_general(a, b, dims, preferred_element_type=F32)


def dot_parts(onehot, values, dims=NN):
    total = dot(onehot, values[0], dims)
    for v in values[1:]:
        total = total + dot(onehot, v, dims)
    return total


def column(row):
    n = row.shape[1]
    return jnp.broadcast_to(row.astype(F32), (8, n)).T[:, 0:1].astype(I32)


def onehot(mask):
    return jnp.where(mask, 1.0, 0.0).astype(BF16)


def fold_matrix(rows, cols):
    l, m = iota((rows, cols), 0), iota((rows, cols), 1)
    return onehot((l & 15) == m)


def spread_matrix(rows, cols):
    m, l = iota((rows, cols), 0), iota((rows, cols), 1)
    return onehot((l & 15) == m)


DZ = (4, 5, 3, 6, 2, 7, 1, 0)
CHUNKS = 3


def id_column(ids, first):
    p = ids.shape[0]
    spread = jnp.broadcast_to(ids.astype(F32), (p, SLOTS, 128))
    own = iota((p, SLOTS, 128), 1) + first == iota((p, SLOTS, 128), 2)
    return jnp.sum(jnp.where(own, spread, 0.0), axis=2, keepdims=True).reshape(p * SLOTS, 1).astype(I32)


def kernel(
    towner_in, trow_in, nowner_in, nrow_in, head_in, rel_id_in, rel_in, et_in,
    out_ref, rel_out,
    towner_ref, trow_ref, nowner_ref, nrow_ref, head_ref, rel_id_ref, rel_ref, et_ref, hi_ref, mid_ref, lo_ref, oh_ref, ids_ref, line_ref, asked_ref, served_ref, fetched_ref, got_ref, negs_ref,
    head_emb, rel_rows, query_ref, gh_ref, gt_ref, gn_ref, gn_held, back_ref, recv_ref, vt_hi, vt_lo, held_ref, sums_ref,
    gr_ref, gr_recv, gr_sum, rel_recv,
    load_sem, ids_send, ids_recv, line_send, line_recv, serve_send, serve_recv, neg_send, neg_recv, gn_send, gn_recv,
    back_send, back_recv, gr_send, gr_got, ag_send, ag_recv, ring_send, ring_recv,
):
    peers = served_ref.shape[0]
    others = peers - 1
    n = negs_ref.shape[0]
    me, g = lax.axis_index("dom"), lax.axis_index("rel")
    edges, negs = head_ref.shape[0], nowner_ref.shape[1]
    quarter = negs // n
    lists = WIDE
    slots = peers * SLOTS
    width, rows = et_ref.shape
    tables = (hi_ref, mid_ref, lo_ref)
    z, y, core = lax.div(me, 8), lax.rem(lax.div(me, 2), 4), lax.rem(me, 2)
    spot = lax.rem(me, 8)
    z_plus = [lax.rem(z + d, 8) * 8 for d in DZ]
    z_minus = [lax.rem(z + 8 - d, 8) * 8 for d in DZ]

    def spot_plus(m):
        q = 7 - m
        return lax.rem(y + lax.div(q, 2), 4) * 2 + lax.rem(core + lax.rem(q, 2), 2)

    def spot_minus(m):
        q = 7 - m
        return lax.rem(y + 4 - lax.div(q, 2), 4) * 2 + lax.rem(core + lax.rem(q, 2), 2)

    def dom_copy(src, dst, send, recv, device):
        return pltpu.make_async_remote_copy(
            src, dst, send, recv, device_id={"dom": device}, device_id_type=MESH)

    def to_all(start, own):
        @pl.loop(0, 8)
        def _(m):
            for j in range(7):
                start(m * 8 + j, m, j)

            @pl.when(m < 7)
            def _():
                start(m * 8 + 7, m, 7)

        own()

    loads = [
        pltpu.make_async_copy(src, dst, load_sem.at[i])
        for i, (src, dst) in enumerate((
            (towner_in, towner_ref), (trow_in, trow_ref), (nowner_in, nowner_ref), (nrow_in, nrow_ref),
            (et_in, et_ref), (head_in, head_ref), (rel_id_in, rel_id_ref), (rel_in, rel_ref)))
    ]
    for load in loads:
        load.start()
    barrier = pltpu.get_barrier_semaphore()
    for j in range(7):
        pl.semaphore_signal(barrier, inc=1, device_id={"dom": z_plus[j] + spot}, device_id_type=MESH)
    for m in range(7):
        pl.semaphore_signal(barrier, inc=1, device_id={"dom": z * 8 + spot_plus(m)}, device_id_type=MESH)
    for k in range(1, n):
        pl.semaphore_signal(barrier, inc=1, device_id={"rel": lax.rem(g + k, n)}, device_id_type=MESH)

    for load in loads[0:4]:
        load.wait()

    def mine(row):
        return sum(jnp.where(g == q, row[:, quarter * q : quarter * (q + 1)], 0) for q in range(n))

    spare = jnp.zeros((1, lists - edges - quarter), I32)
    owner = jnp.concatenate([towner_ref[...], mine(nowner_ref[...]) + 64, spare + 255], axis=1)
    asked_rows = jnp.concatenate([trow_ref[...][None, :], mine(nrow_ref[...][None, :]), spare], axis=1)
    same = column(owner) == owner
    earlier = iota((lists, lists), 0) < iota((lists, lists), 1)
    position = jnp.sum(jnp.where(same & earlier, 1.0, 0.0), axis=0, keepdims=True).astype(I32)
    negative, valid = owner >= 64, owner < 128
    position = jnp.where(negative, position + CAP_T, position)
    owner = owner & 63
    dz = ((owner >> 3) - z + 8) & 7
    step_z = sum(jnp.where(dz == d, j, 0) for j, d in enumerate(DZ))
    dy, dc = (((owner >> 1) & 3) - y + 4) & 3, ((owner & 1) - core + 2) & 1
    slot = jnp.where(valid, ((7 - dy * 2 - dc) * 8 + step_z) * SLOTS + position, -1)
    left = jnp.where((iota((8, lists), 0) == step_z) & valid, (asked_rows + 1).astype(F32), 0.0)
    right = jnp.where(iota((128, lists), 0) == (owner & 7) * SLOTS + position, 1.0, 0.0)
    ids = lax.dot_general(left, right, NT, precision=HIGHEST, preferred_element_type=F32)
    ids_ref[...] = ((ids + 0.5).astype(I32) - 1)[:, None, :]

    pl.semaphore_wait(barrier, 14 + n - 1)
    for j in range(7):
        dom_copy(ids_ref.at[j], line_ref.at[j], ids_send, ids_recv, z_plus[j] + spot).start()
    pltpu.make_async_copy(ids_ref.at[7], line_ref.at[7], ids_recv).start()
    pltpu.make_async_copy(ids_ref, line_ref, ids_recv).wait()
    for m in range(7):
        dom_copy(line_ref, asked_ref.at[8 * m : 8 * m + 8], line_send, line_recv, z * 8 + spot_plus(m)).start()
    pltpu.make_async_copy(line_ref, asked_ref.at[56:64], line_recv).start()

    for load in loads[4:]:
        load.wait()

    @pl.loop(0, width // 16)
    def _(i):
        at = pl.multiple_of(i * 16, 16)
        for t, v in zip(tables, parts(et_ref[pl.ds(at, 16), :], 3), strict=True):
            t[pl.ds(at, 16), :] = v

    for t in tables:
        for k in range(1, 8):
            t[MAIN + 16 * k : MAIN + 16 * (k + 1), :] = t[MAIN : MAIN + 16, :]

    pltpu.make_async_copy(asked_ref, asked_ref, line_recv).wait()

    @pl.loop(0, 8)
    def _(m):
        at = pl.multiple_of(m * 8, 8)
        col = id_column(asked_ref[pl.ds(at, 8)], spot * SLOTS)
        hot = onehot(iota((8 * SLOTS, rows), 1) == col)
        oh_ref[pl.ds(pl.multiple_of(m * 8 * SLOTS, 8 * SLOTS), 8 * SLOTS), :] = hot
        got = dot_parts(hot, [t[...] for t in tables], NT)
        place = iota((8, SLOTS, 128), 1)
        lane = iota((8, SLOTS, 128), 2)
        rest = got[:, MAIN:].reshape(8, SLOTS, 128)
        rest = jnp.where((lane >> 4) == (place & 7), rest, 0.0)
        low = jnp.sum(jnp.where(place < 8, rest, 0.0), axis=1, keepdims=True)
        high = jnp.sum(jnp.where(place < 8, 0.0, rest), axis=1, keepdims=True)
        for k, part in enumerate((low, high, jnp.zeros_like(low))):
            main = got[:, 128 * k : 128 * (k + 1)].reshape(8, SLOTS, 128)
            served_ref[pl.ds(at, 8), :, 128 * k : 128 * (k + 1)] = jnp.where(place == SLOTS - 1, part, main)
        to = spot_minus(m)

        def start(i, j):
            dom_copy(served_ref.at[i], fetched_ref.at[i], serve_send, serve_recv.at[m], z_minus[j] + to).start()

        for j in range(7):
            start(m * 8 + j, j)

        @pl.when(m < 7)
        def _():
            start(m * 8 + 7, 7)

    pltpu.make_async_copy(served_ref.at[others], fetched_ref.at[others], serve_recv.at[7]).start()

    hot = onehot(iota((edges, rows), 1) == column(head_ref[...][None, :]))
    oh_ref[slots:, :] = hot
    got = dot_parts(hot, [t[...] for t in tables], NT)
    head_emb[:, 0:MAIN] = got[:, 0:MAIN]
    head_emb[:, MAIN:WIDE] = jnp.where(iota((edges, 128), 1) < width - MAIN, got[:, MAIN:WIDE], 0.0)
    groups = rel_ref.shape[0]
    hot = onehot(iota((edges, groups), 1) == column(rel_id_ref[...][None, :]))
    rel_rows[:, 0:width] = dot_parts(hot, parts(rel_ref[...], 3))
    rel_rows[:, width:WIDE] = jnp.zeros((edges, WIDE - width), F32)
    query_ref[...] = head_emb[...] * rel_rows[...]

    slot_col = column(slot)
    fold = fold_matrix(256, 128)
    got_ref[...] = jnp.zeros_like(got_ref)

    @pl.loop(0, 4)
    def _(b):
        at = pl.ds(pl.multiple_of(b * 16, 16), 16)
        for k in range(2):
            half = pl.ds(pl.multiple_of(b * 16, 16) + 8 * k, 8)
            pltpu.make_async_copy(served_ref.at[half], fetched_ref.at[half], serve_recv.at[2 * b + k]).wait()
        hot = onehot(iota((lists, 16 * SLOTS), 1) + b * (16 * SLOTS) == slot_col)
        got_ref[:, 0:MAIN] += dot_parts(hot, parts(fetched_ref[at].reshape(16 * SLOTS, MAIN), 3))

    packed = parts(fetched_ref[:, SLOTS - 1, 0:256], 3)

    def remainders(at):
        where = slot_col[at]
        count = where.shape[0]
        rest = dot_parts(onehot(iota((count, peers), 1) == (where >> 4)), packed)
        rest = jnp.where((iota((count, 256), 1) >> 4) == (where & 15), rest, 0.0)
        return sum(dot(p, fold, NN) for p in parts(rest, 3))

    own = slice(edges, edges + quarter)
    negs_ref[g, :, 0:MAIN] = got_ref[own, 0:MAIN]
    negs_ref[g, :, MAIN:WIDE] = remainders(own)

    def rel_copy(src, dst, send, recv, k):
        return pltpu.make_async_remote_copy(
            src, dst, send, recv, device_id={"rel": lax.rem(g + k, n)}, device_id_type=MESH)

    copies = [rel_copy(negs_ref.at[g], negs_ref.at[g], neg_send.at[k - 1], neg_recv.at[k - 1], k) for k in range(1, n)]
    for copy in copies:
        copy.start()
    got_ref[0:edges, MAIN:WIDE] = remainders(slice(0, edges))
    positive = jnp.sum(query_ref[...] * got_ref[0:edges, :], axis=1, keepdims=True)
    for copy in copies:
        copy.wait_recv()
    sent = list(copies)

    def neg_rows(c):
        return negs_ref[...].reshape(negs, WIDE)[c * SPAN : (c + 1) * SPAN]

    coefs = []
    for c in range(edges // SPAN):
        at = slice(c * SPAN, (c + 1) * SPAN)
        queries = query_ref[at]
        scores = lax.dot_general(queries, neg_rows(c), NT, precision=HIGHEST, preferred_element_type=F32)
        row_max = jnp.maximum(positive[at], jnp.max(scores, axis=1, keepdims=True))
        pos_exp = jnp.exp(positive[at] - row_max)
        neg_exp = jnp.exp(scores - row_max)
        total = pos_exp + jnp.sum(neg_exp, axis=1, keepdims=True)
        pos_coef = pos_exp / total - 1.0
        neg_coef = neg_exp / total
        coefs.append((pos_coef, neg_coef))
        gt_ref[at] = pos_coef * queries
        grad_neg = lax.dot_general(neg_coef.T, queries, NN, precision=HIGHEST, preferred_element_type=F32)
        first = c * SPAN
        while first < (c + 1) * SPAN:
            q, inside = divmod(first, quarter)
            count = min(quarter - inside, (c + 1) * SPAN - first)
            gn_ref[q, inside : inside + count] = grad_neg[first - c * SPAN : first - c * SPAN + count]
            first += count

    copies = [
        rel_copy(gn_ref.at[lax.rem(g + k, n)], gn_held.at[k - 1], gn_send.at[k - 1], gn_recv.at[k - 1], k) for k in range(1, n)
    ]
    for copy in copies:
        copy.start()

    def send_back(k, part, at):
        def start(i, m, j):
            dom_copy(
                back_ref.at[k, i, at], recv_ref.at[k, i, at], back_send, back_recv.at[part], z_plus[j] + spot_plus(m)).start()

        def own():
            pltpu.make_async_copy(back_ref.at[k, others, at], recv_ref.at[k, others, at], back_recv.at[part]).start()

        to_all(start, own)

    hot = onehot(iota((slots, edges), 0) == slot[:, 0:edges])
    low, high, all_rows = pl.ds(0, 8), pl.ds(8, 8), pl.ds(0, SLOTS)
    for k in range(CHUNKS):
        back_ref[k] = dot_parts(hot, parts(gt_ref[:, 128 * k : 128 * (k + 1)], 2)).reshape(peers, SLOTS, 128)
        if k == 0:
            send_back(0, 0, low)

    spread = spread_matrix(128, 256)

    def remainders_back(values, at):
        count = values.shape[0]
        rest = sum(dot(p, spread, NN) for p in parts(values, 2))
        rest = jnp.where((iota((count, 256), 1) >> 4) == (slot_col[at] & 15), rest, 0.0)
        return dot_parts(onehot(iota((peers, count), 0) == (slot[:, at] >> 4)), parts(rest, 2))

    rest = remainders_back(gt_ref[:, MAIN:WIDE], slice(0, edges))
    for copy in copies:
        copy.wait_recv()
    sent += copies
    grad_neg = gn_ref[g] + gn_held[0] + gn_held[1] + gn_held[2]
    rest = rest + remainders_back(grad_neg[:, MAIN:WIDE], own)
    line = iota((peers * 8, quarter), 0)
    hot = onehot((line >> 3) * SLOTS + 8 + (line & 7) == slot[:, own])
    last = iota((peers, 8, 128), 1) == 7
    for k in range(CHUNKS):
        more = dot_parts(hot, parts(grad_neg[:, 128 * k : 128 * (k + 1)], 2)).reshape(peers, 8, 128)
        more = back_ref[k, :, 8:SLOTS, :] + more
        if k < 2:
            more = jnp.where(last, rest[:, 128 * k : 128 * (k + 1)][:, None, :], more)
        back_ref[k, :, 8:SLOTS, :] = more
        send_back(k, k + 1, high if k == 0 else all_rows)

    gr_parts = []
    for c in range(edges // SPAN):
        at = slice(c * SPAN, (c + 1) * SPAN)
        pos_coef, neg_coef = coefs[c]
        grad_query = pos_coef * got_ref[at] + lax.dot_general(
            neg_coef, neg_rows(c), NN, precision=HIGHEST, preferred_element_type=F32)
        gh_ref[at] = grad_query * rel_rows[at]
        hot = onehot(iota((groups, SPAN), 0) == rel_id_ref[at][None, :])
        gr_parts.append(dot_parts(hot, parts(grad_query * head_emb[at], 3)))
    gr_ref[...] = sum(gr_parts)[:, None, :]

    def start_rel(i, m, j):
        to = z_plus[j] + spot_plus(m)
        dom_copy(gr_ref.at[to], gr_recv.at[i], gr_send, gr_got, to).start()

    to_all(start_rel, lambda: pltpu.make_async_copy(gr_ref.at[me], gr_recv.at[others], gr_got).start())

    slab_ref = et_ref
    piece = rows // n
    right_hand, left_hand, far = lax.rem(g + 1, n), lax.rem(g + 3, n), lax.rem(g + 2, n)
    first_row = [128 * k for k in range(CHUNKS)]
    height = [128] * (CHUNKS - 1) + [width - 128 * (CHUNKS - 1)]

    def cols(j):
        return pl.ds(pl.multiple_of(j * piece, piece), piece)

    ring = {}
    to_of, back_of = (right_hand, left_hand), (left_hand, right_hand)

    def half(k, way, mine):
        h = height[k] // 2
        low = (way == 0) == mine
        return slice(first_row[k], first_row[k] + h) if low else slice(first_row[k] + h, first_row[k] + 2 * h)

    def send(k, way, step, src, dst):
        copy = pltpu.make_async_remote_copy(
            src, dst, ring_send.at[k, way, step], ring_recv.at[k, way, step],
            device_id={"rel": to_of[way]}, device_id_type=MESH)
        copy.start()
        ring[k, way, step] = copy

    def arrived(k, part, at):
        pltpu.make_async_copy(back_ref.at[k, :, at], recv_ref.at[k, :, at], back_recv.at[part]).wait()

    def scatter(k):
        if k == 0:
            arrived(0, 0, low)
            arrived(0, 1, high)
        else:
            arrived(k, k + 1, all_rows)
        values = [recv_ref[k].reshape(slots, 128).T, gh_ref[:, 128 * k : 128 * (k + 1)].T]
        vt = jnp.concatenate(values, axis=1)
        if k == CHUNKS - 1:
            rest = jnp.concatenate([recv_ref[0, :, SLOTS - 1, :], recv_ref[1, :, SLOTS - 1, :]], axis=1)
            rest = jnp.broadcast_to(rest[:, None, :], (peers, SLOTS, 256))
            own = (iota((peers, SLOTS, 256), 2) >> 4) == iota((peers, SLOTS, 256), 1)
            rest = jnp.where(own, rest, 0.0).reshape(slots, 256)
            rest = sum(dot(p, fold, NN) for p in parts(rest, 2))
            more = jnp.concatenate([rest.T[0:16], gh_ref[:, MAIN:WIDE].T[0:16]], axis=1)
            vt = jnp.concatenate([vt, more], axis=0)
        h = height[k]
        vt_hi[0:h], vt_lo[0:h] = parts(vt, 2)

        @pl.loop(0, n)
        def _(j):
            at = cols(j)
            slab_ref[first_row[k] : first_row[k] + h, at] = dot(vt_hi[0:h], oh_ref[:, at], NN) + dot(
                vt_lo[0:h], oh_ref[:, at], NN)

    def begin(k):
        h = height[k] // 2
        for way in range(2):
            send(k, way, 0, slab_ref.at[half(k, way, True), cols(far)], held_ref.at[k, way, 0, 0:h])
        for way in range(2):
            send(k, way, 1, slab_ref.at[half(k, way, False), cols(to_of[way])], held_ref.at[k, way, 1, 0:h])

    def add(k):
        h = height[k] // 2
        for way in range(2):
            ring[k, way, 0].wait_recv()
            sums_ref[k, way, 0:h] = slab_ref[half(k, way, True), cols(to_of[way])] + held_ref[k, way, 0, 0:h]
            send(k, way, 2, sums_ref.at[k, way, 0:h], held_ref.at[k, way, 2, 0:h])

    def share(k):
        h = height[k] // 2
        for way in range(2):
            ring[k, way, 1].wait_recv()
            ring[k, way, 2].wait_recv()
        for way in range(2):
            at = half(k, way, True)
            out_ref[at, cols(g)] = slab_ref[at, cols(g)] + held_ref[k, way, 2, 0:h] + held_ref[k, 1 - way, 1, 0:h]
        for step, mine_too in ((3, True), (4, False)):
            for way in range(2):
                at = half(k, way, mine_too)
                send(k, way, step, out_ref.at[at, cols(g)], out_ref.at[at, cols(g)])

    def forward(k):
        for way in range(2):
            ring[k, way, 3].wait_recv()
            at = half(k, way, True)
            send(k, way, 5, out_ref.at[at, cols(back_of[way])], out_ref.at[at, cols(back_of[way])])

    scatter(0)
    begin(0)
    pltpu.make_async_copy(gr_ref, gr_recv, gr_got).wait()
    gr_sum[0] = jnp.sum(gr_recv[...], axis=0)

    def start_sum(i, m, j):
        dom_copy(gr_sum.at[0], rel_recv.at[me], ag_send, ag_recv, z_plus[j] + spot_plus(m)).start()

    to_all(start_sum, lambda: pltpu.make_async_copy(gr_sum.at[0], rel_recv.at[me], ag_recv).start())
    add(0)
    share(0)
    scatter(1)
    begin(1)
    forward(0)
    add(1)
    share(1)
    scatter(2)
    begin(2)
    forward(1)
    add(2)
    share(2)
    pltpu.make_async_copy(gr_ref, rel_recv, ag_recv).wait()
    rel_out[...] = rel_recv[:, 0, :][:, 0:width]
    forward(2)

    first = pl.ds(0, others)
    seven = pl.ds(0, 7)
    pltpu.make_async_copy(ids_ref.at[seven], ids_ref.at[seven], ids_send).wait()
    pltpu.make_async_copy(asked_ref.at[0:56], asked_ref.at[0:56], line_send).wait()
    pltpu.make_async_copy(served_ref.at[first], served_ref.at[first], serve_send).wait()
    pltpu.make_async_copy(gr_ref.at[first], gr_ref.at[first], gr_send).wait()
    pltpu.make_async_copy(gr_ref.at[first], gr_ref.at[first], ag_send).wait()
    for k in range(CHUNKS):
        pltpu.make_async_copy(back_ref.at[k, first], back_ref.at[k, first], back_send).wait()
    for copy in [*sent, *ring.values()]:
        copy.wait_send()
    for k in range(CHUNKS):
        for way in range(2):
            ring[k, way, 4].wait_recv()
            ring[k, way, 5].wait_recv()


def body(embeddings, rel_weight, head_row, rel_id, tail_owner, tail_row, neg_owner, neg_row):
    peers, n = lax.axis_size("dom"), lax.axis_size("rel")
    rows, width = embeddings.shape
    edges, negs = head_row.shape[0], neg_row.shape[0]
    groups = rel_weight.shape[0]
    quarter = negs // n
    lists = WIDE
    slots = peers * SLOTS
    tall = (width - 128 * (CHUNKS - 1)) // 2
    V, DMA = pltpu.VMEM, pltpu.SemaphoreType.DMA
    vmem, in_hbm = pl.BlockSpec(memory_space=pltpu.VMEM), pl.BlockSpec(memory_space=pltpu.HBM)
    scratch = [
        V((1, edges), I32), V((edges,), I32), V((1, negs), I32), V((negs,), I32), V((edges,), I32), V((edges,), I32),
        V((groups, width), F32), V((width, rows), F32), V((WIDE, rows), BF16), V((WIDE, rows), BF16), V((WIDE, rows), BF16),
        V((slots + edges, rows), BF16), V((8, 1, 128), I32), V((8, 1, 128), I32), V((peers, 1, 128), I32),
        V((peers, SLOTS, MAIN), F32), V((peers, SLOTS, MAIN), F32), V((lists, WIDE), F32), V((n, quarter, WIDE), F32),
        V((edges, WIDE), F32), V((edges, WIDE), F32), V((edges, WIDE), F32), V((edges, WIDE), F32), V((edges, WIDE), F32),
        V((n, quarter, WIDE), F32), V((n - 1, quarter, WIDE), F32),
        V((CHUNKS, peers, SLOTS, 128), F32), V((CHUNKS, peers, SLOTS, 128), F32),
        V((2 * tall, slots + edges), BF16), V((2 * tall, slots + edges), BF16),
        V((CHUNKS, 2, 3, tall, rows // n), F32), V((CHUNKS, 2, tall, rows // n), F32),
        V((groups, 1, WIDE), F32), V((peers, 1, WIDE), F32), V((1, 1, WIDE), F32), V((groups, 1, WIDE), F32),
        DMA((8,)), DMA(()), DMA(()), DMA(()), DMA(()), DMA(()), DMA((8,)), DMA((n - 1,)), DMA((n - 1,)), DMA((n - 1,)), DMA((n - 1,)),
        DMA(()), DMA((CHUNKS + 1,)), DMA(()), DMA(()), DMA(()), DMA(()), DMA((CHUNKS, 2, 6)), DMA((CHUNKS, 2, 6)),
    ]
    total, relation = pl.pallas_call(
        kernel,
        out_shape=(jax.ShapeDtypeStruct((width, rows), F32), jax.ShapeDtypeStruct((groups, width), F32)),
        in_specs=[in_hbm] * 8,
        out_specs=(vmem, vmem),
        scratch_shapes=scratch,
        compiler_params=pltpu.CompilerParams(collective_id=0, has_side_effects=True, vmem_limit_bytes=48 << 20),
        cost_estimate=pl.CostEstimate(flops=int(3e10), bytes_accessed=7 << 20, transcendentals=0),
        name="ranking_gradients",
    )(
        tail_owner.reshape(1, edges), tail_row, neg_owner.reshape(1, negs), neg_row, head_row, rel_id, rel_weight, embeddings.T)
    return (total.T, relation)


def solution(mesh):
    return jax.shard_map(
        body,
        mesh=mesh,
        in_specs=(
            P("dom", None),
            P("rel", None),
            P(("dom", "rel")),
            P(("dom", "rel")),
            P(("dom", "rel"), None),
            P(("dom", "rel")),
            P("dom", None),
            P("dom"),
        ),
        out_specs=(P("dom", None), P("rel", None)),
        check_vma=False,
    )
```

```python
import jax
import jax.numpy as jnp
from jax import lax
from jax.experimental import pallas as pl
from jax.experimental.pallas import tpu as pltpu
from jax.sharding import PartitionSpec as P

SPAN = 128
MAIN = 384
WIDE = 512
SLOTS = 16
CAP_T = 12
F32, BF16, I32 = jnp.float32, jnp.bfloat16, jnp.int32
MESH = pl.DeviceIdType.MESH
HIGHEST = lax.Precision.HIGHEST
NN = (((1,), (0,)), ((), ()))
NT = (((1,), (1,)), ((), ()))
TN = (((0,), (0,)), ((), ()))


def iota(shape, dim):
    return lax.broadcasted_iota(I32, shape, dim)


def parts(x, count):
    out = []
    for _ in range(count - 1):
        hi = x.astype(BF16)
        out.append(hi)
        x = x - hi.astype(F32)
    return out + [x.astype(BF16)]


def dot(a, b, dims):
    return lax.dot_general(a, b, dims, preferred_element_type=F32)


def dot_parts(onehot, values, dims=NN):
    total = dot(onehot, values[0], dims)
    for v in values[1:]:
        total = total + dot(onehot, v, dims)
    return total


def column(row):
    n = row.shape[1]
    return jnp.broadcast_to(row.astype(F32), (8, n)).T[:, 0:1].astype(I32)


def onehot(mask):
    return jnp.where(mask, 1.0, 0.0).astype(BF16)


def fold_matrix(rows, cols):
    l, m = iota((rows, cols), 0), iota((rows, cols), 1)
    return onehot((l & 15) == m)


def spread_matrix(rows, cols):
    m, l = iota((rows, cols), 0), iota((rows, cols), 1)
    return onehot((l & 15) == m)


DZ = (4, 5, 3, 6, 2, 7, 1, 0)
CHUNKS = 3


def id_column(ids, first):
    p = ids.shape[0]
    spread = jnp.broadcast_to(ids.astype(F32), (p, SLOTS, 128))
    own = iota((p, SLOTS, 128), 1) + first == iota((p, SLOTS, 128), 2)
    return jnp.sum(jnp.where(own, spread, 0.0), axis=2, keepdims=True).reshape(p * SLOTS, 1).astype(I32)


def kernel(
    lists_ref, rel_in, et_in,
    out_ref, rel_out,
    rel_ref, et_ref, hi_ref, mid_ref, lo_ref, oh_ref, ids_ref, line_ref, asked_ref, served_ref, fetched_ref, got_ref, negs_ref,
    head_emb, rel_rows, query_ref, gh_ref, gt_ref, gn_ref, gn_held, back_ref, recv_ref, vt_hi, vt_lo, held_ref, sums_ref,
    gr_ref, gr_recv, gr_sum, rel_recv,
    load_sem, ids_send, ids_recv, line_send, line_recv, serve_send, serve_recv, neg_send, neg_recv, gn_send, gn_recv,
    back_send, back_recv, gr_send, gr_got, ag_send, ag_recv, ring_send, ring_recv,
):
    peers = served_ref.shape[0]
    others = peers - 1
    n = negs_ref.shape[0]
    me, g = lax.axis_index("dom"), lax.axis_index("rel")
    edges = head_emb.shape[0]
    negs = (lists_ref.shape[1] - 4 * edges) // 2
    quarter = negs // n
    lists = WIDE
    slots = peers * SLOTS
    width, rows = et_ref.shape
    tables = (hi_ref, mid_ref, lo_ref)
    z, y, core = lax.div(me, 8), lax.rem(lax.div(me, 2), 4), lax.rem(me, 2)
    spot = lax.rem(me, 8)
    z_plus = [lax.rem(z + d, 8) * 8 for d in DZ]
    z_minus = [lax.rem(z + 8 - d, 8) * 8 for d in DZ]

    def spot_plus(m):
        q = 7 - m
        return lax.rem(y + lax.div(q, 2), 4) * 2 + lax.rem(core + lax.rem(q, 2), 2)

    def spot_minus(m):
        q = 7 - m
        return lax.rem(y + 4 - lax.div(q, 2), 4) * 2 + lax.rem(core + lax.rem(q, 2), 2)

    def dom_copy(src, dst, send, recv, device):
        return pltpu.make_async_remote_copy(
            src, dst, send, recv, device_id={"dom": device}, device_id_type=MESH)

    def to_all(start, own):
        @pl.loop(0, 8)
        def _(m):
            for j in range(7):
                start(m * 8 + j, m, j)

            @pl.when(m < 7)
            def _():
                start(m * 8 + 7, m, 7)

        own()

    loads = [pltpu.make_async_copy(et_in, et_ref, load_sem.at[0]), pltpu.make_async_copy(rel_in, rel_ref, load_sem.at[1])]
    for load in loads:
        load.start()
    barrier = pltpu.get_barrier_semaphore()
    for j in range(7):
        pl.semaphore_signal(barrier, inc=1, device_id={"dom": z_plus[j] + spot}, device_id_type=MESH)
    for m in range(7):
        pl.semaphore_signal(barrier, inc=1, device_id={"dom": z * 8 + spot_plus(m)}, device_id_type=MESH)
    for k in range(1, n):
        pl.semaphore_signal(barrier, inc=1, device_id={"rel": lax.rem(g + k, n)}, device_id_type=MESH)

    tail_owner, tail_row, head_row, rel_id = (lists_ref[:, edges * k : edges * (k + 1)] for k in range(4))
    neg_owner, neg_row = (lists_ref[:, 4 * edges + negs * k : 4 * edges + negs * (k + 1)] for k in range(2))

    def mine(row):
        return sum(jnp.where(g == q, row[:, quarter * q : quarter * (q + 1)], 0) for q in range(n))

    spare = jnp.zeros((1, lists - edges - quarter), I32)
    owner = jnp.concatenate([tail_owner, mine(neg_owner) + 64, spare + 255], axis=1)
    asked_rows = jnp.concatenate([tail_row, mine(neg_row), spare], axis=1)
    same = column(owner) == owner
    earlier = iota((lists, lists), 0) < iota((lists, lists), 1)
    position = jnp.sum(jnp.where(same & earlier, 1.0, 0.0), axis=0, keepdims=True).astype(I32)
    negative, valid = owner >= 64, owner < 128
    position = jnp.where(negative, position + CAP_T, position)
    owner = owner & 63
    dz = ((owner >> 3) - z + 8) & 7
    step_z = sum(jnp.where(dz == d, j, 0) for j, d in enumerate(DZ))
    dy, dc = (((owner >> 1) & 3) - y + 4) & 3, ((owner & 1) - core + 2) & 1
    slot = jnp.where(valid, ((7 - dy * 2 - dc) * 8 + step_z) * SLOTS + position, -1)
    left = jnp.where((iota((8, lists), 0) == step_z) & valid, (asked_rows + 1).astype(F32), 0.0)
    right = jnp.where(iota((128, lists), 0) == (owner & 7) * SLOTS + position, 1.0, 0.0)
    ids = lax.dot_general(left, right, NT, precision=HIGHEST, preferred_element_type=F32)
    ids_ref[...] = ((ids + 0.5).astype(I32) - 1)[:, None, :]

    pl.semaphore_wait(barrier, 14 + n - 1)
    for j in range(7):
        dom_copy(ids_ref.at[j], line_ref.at[j], ids_send, ids_recv, z_plus[j] + spot).start()
    pltpu.make_async_copy(ids_ref.at[7], line_ref.at[7], ids_recv).start()
    pltpu.make_async_copy(ids_ref, line_ref, ids_recv).wait()
    for m in range(7):
        dom_copy(line_ref, asked_ref.at[8 * m : 8 * m + 8], line_send, line_recv, z * 8 + spot_plus(m)).start()
    pltpu.make_async_copy(line_ref, asked_ref.at[56:64], line_recv).start()

    for load in loads:
        load.wait()

    @pl.loop(0, width // 16)
    def _(i):
        at = pl.multiple_of(i * 16, 16)
        for t, v in zip(tables, parts(et_ref[pl.ds(at, 16), :], 3), strict=True):
            t[pl.ds(at, 16), :] = v

    for t in tables:
        for k in range(1, 8):
            t[MAIN + 16 * k : MAIN + 16 * (k + 1), :] = t[MAIN : MAIN + 16, :]

    pltpu.make_async_copy(asked_ref, asked_ref, line_recv).wait()

    @pl.loop(0, 8)
    def _(m):
        at = pl.multiple_of(m * 8, 8)
        col = id_column(asked_ref[pl.ds(at, 8)], spot * SLOTS)
        hot = onehot(iota((8 * SLOTS, rows), 1) == col)
        oh_ref[pl.ds(pl.multiple_of(m * 8 * SLOTS, 8 * SLOTS), 8 * SLOTS), :] = hot
        got = dot_parts(hot, [t[...] for t in tables], NT)
        place = iota((8, SLOTS, 128), 1)
        lane = iota((8, SLOTS, 128), 2)
        rest = got[:, MAIN:].reshape(8, SLOTS, 128)
        rest = jnp.where((lane >> 4) == (place & 7), rest, 0.0)
        low = jnp.sum(jnp.where(place < 8, rest, 0.0), axis=1, keepdims=True)
        high = jnp.sum(jnp.where(place < 8, 0.0, rest), axis=1, keepdims=True)
        for k, part in enumerate((low, high, jnp.zeros_like(low))):
            main = got[:, 128 * k : 128 * (k + 1)].reshape(8, SLOTS, 128)
            served_ref[pl.ds(at, 8), :, 128 * k : 128 * (k + 1)] = jnp.where(place == SLOTS - 1, part, main)
        to = spot_minus(m)

        def start(i, j):
            dom_copy(served_ref.at[i], fetched_ref.at[i], serve_send, serve_recv.at[m], z_minus[j] + to).start()

        for j in range(7):
            start(m * 8 + j, j)

        @pl.when(m < 7)
        def _():
            start(m * 8 + 7, 7)

    pltpu.make_async_copy(served_ref.at[others], fetched_ref.at[others], serve_recv.at[7]).start()

    hot = onehot(iota((edges, rows), 1) == column(head_row))
    oh_ref[slots:, :] = hot
    got = dot_parts(hot, [t[...] for t in tables], NT)
    head_emb[:, 0:MAIN] = got[:, 0:MAIN]
    head_emb[:, MAIN:WIDE] = jnp.where(iota((edges, 128), 1) < width - MAIN, got[:, MAIN:WIDE], 0.0)
    groups = rel_ref.shape[0]
    hot = onehot(iota((edges, groups), 1) == column(rel_id))
    rel_rows[:, 0:width] = dot_parts(hot, parts(rel_ref[...], 3))
    rel_rows[:, width:WIDE] = jnp.zeros((edges, WIDE - width), F32)
    query_ref[...] = head_emb[...] * rel_rows[...]

    slot_col = column(slot)
    fold = fold_matrix(256, 128)
    got_ref[...] = jnp.zeros_like(got_ref)

    @pl.loop(0, 4)
    def _(b):
        at = pl.ds(pl.multiple_of(b * 16, 16), 16)
        for k in range(2):
            half = pl.ds(pl.multiple_of(b * 16, 16) + 8 * k, 8)
            pltpu.make_async_copy(served_ref.at[half], fetched_ref.at[half], serve_recv.at[2 * b + k]).wait()
        hot = onehot(iota((lists, 16 * SLOTS), 1) + b * (16 * SLOTS) == slot_col)
        got_ref[:, 0:MAIN] += dot_parts(hot, parts(fetched_ref[at].reshape(16 * SLOTS, MAIN), 3))

    packed = parts(fetched_ref[:, SLOTS - 1, 0:256], 3)

    def remainders(at):
        where = slot_col[at]
        count = where.shape[0]
        rest = dot_parts(onehot(iota((count, peers), 1) == (where >> 4)), packed)
        rest = jnp.where((iota((count, 256), 1) >> 4) == (where & 15), rest, 0.0)
        return sum(dot(p, fold, NN) for p in parts(rest, 3))

    own = slice(edges, edges + quarter)
    negs_ref[g, :, 0:MAIN] = got_ref[own, 0:MAIN]
    negs_ref[g, :, MAIN:WIDE] = remainders(own)

    def rel_copy(src, dst, send, recv, k):
        return pltpu.make_async_remote_copy(
            src, dst, send, recv, device_id={"rel": lax.rem(g + k, n)}, device_id_type=MESH)

    copies = [rel_copy(negs_ref.at[g], negs_ref.at[g], neg_send.at[k - 1], neg_recv.at[k - 1], k) for k in range(1, n)]
    for copy in copies:
        copy.start()
    got_ref[0:edges, MAIN:WIDE] = remainders(slice(0, edges))
    positive = jnp.sum(query_ref[...] * got_ref[0:edges, :], axis=1, keepdims=True)
    for copy in copies:
        copy.wait_recv()
    sent = list(copies)

    def neg_rows(c):
        return negs_ref[...].reshape(negs, WIDE)[c * SPAN : (c + 1) * SPAN]

    coefs = []
    for c in range(edges // SPAN):
        at = slice(c * SPAN, (c + 1) * SPAN)
        queries = query_ref[at]
        scores = lax.dot_general(queries, neg_rows(c), NT, precision=HIGHEST, preferred_element_type=F32)
        row_max = jnp.maximum(positive[at], jnp.max(scores, axis=1, keepdims=True))
        pos_exp = jnp.exp(positive[at] - row_max)
        neg_exp = jnp.exp(scores - row_max)
        total = pos_exp + jnp.sum(neg_exp, axis=1, keepdims=True)
        pos_coef = pos_exp / total - 1.0
        neg_coef = neg_exp / total
        coefs.append((pos_coef, neg_coef))
        gt_ref[at] = pos_coef * queries
        grad_neg = lax.dot_general(neg_coef.T, queries, NN, precision=HIGHEST, preferred_element_type=F32)
        first = c * SPAN
        while first < (c + 1) * SPAN:
            q, inside = divmod(first, quarter)
            count = min(quarter - inside, (c + 1) * SPAN - first)
            gn_ref[q, inside : inside + count] = grad_neg[first - c * SPAN : first - c * SPAN + count]
            first += count

    copies = [
        rel_copy(gn_ref.at[lax.rem(g + k, n)], gn_held.at[k - 1], gn_send.at[k - 1], gn_recv.at[k - 1], k) for k in range(1, n)
    ]
    for copy in copies:
        copy.start()

    def send_back(k, part, at):
        def start(i, m, j):
            dom_copy(
                back_ref.at[k, i, at], recv_ref.at[k, i, at], back_send, back_recv.at[part], z_plus[j] + spot_plus(m)).start()

        def own():
            pltpu.make_async_copy(back_ref.at[k, others, at], recv_ref.at[k, others, at], back_recv.at[part]).start()

        to_all(start, own)

    hot = onehot(iota((slots, edges), 0) == slot[:, 0:edges])
    low, high, all_rows = pl.ds(0, 8), pl.ds(8, 8), pl.ds(0, SLOTS)
    for k in range(CHUNKS):
        back_ref[k] = dot_parts(hot, parts(gt_ref[:, 128 * k : 128 * (k + 1)], 2)).reshape(peers, SLOTS, 128)
        if k == 0:
            send_back(0, 0, low)

    spread = spread_matrix(128, 256)

    def remainders_back(values, at):
        count = values.shape[0]
        rest = sum(dot(p, spread, NN) for p in parts(values, 2))
        rest = jnp.where((iota((count, 256), 1) >> 4) == (slot_col[at] & 15), rest, 0.0)
        return dot_parts(onehot(iota((peers, count), 0) == (slot[:, at] >> 4)), parts(rest, 2))

    rest = remainders_back(gt_ref[:, MAIN:WIDE], slice(0, edges))
    for copy in copies:
        copy.wait_recv()
    sent += copies
    grad_neg = gn_ref[g] + gn_held[0] + gn_held[1] + gn_held[2]
    rest = rest + remainders_back(grad_neg[:, MAIN:WIDE], own)
    line = iota((peers * 8, quarter), 0)
    hot = onehot((line >> 3) * SLOTS + 8 + (line & 7) == slot[:, own])
    last = iota((peers, 8, 128), 1) == 7
    for k in range(CHUNKS):
        more = dot_parts(hot, parts(grad_neg[:, 128 * k : 128 * (k + 1)], 2)).reshape(peers, 8, 128)
        more = back_ref[k, :, 8:SLOTS, :] + more
        if k < 2:
            more = jnp.where(last, rest[:, 128 * k : 128 * (k + 1)][:, None, :], more)
        back_ref[k, :, 8:SLOTS, :] = more
        send_back(k, k + 1, high if k == 0 else all_rows)

    gr_parts = []
    for c in range(edges // SPAN):
        at = slice(c * SPAN, (c + 1) * SPAN)
        pos_coef, neg_coef = coefs[c]
        grad_query = pos_coef * got_ref[at] + lax.dot_general(
            neg_coef, neg_rows(c), NN, precision=HIGHEST, preferred_element_type=F32)
        gh_ref[at] = grad_query * rel_rows[at]
        hot = onehot(iota((groups, SPAN), 0) == rel_id[:, at])
        gr_parts.append(dot_parts(hot, parts(grad_query * head_emb[at], 3)))
    gr_ref[...] = sum(gr_parts)[:, None, :]

    def start_rel(i, m, j):
        to = z_plus[j] + spot_plus(m)
        dom_copy(gr_ref.at[to], gr_recv.at[i], gr_send, gr_got, to).start()

    to_all(start_rel, lambda: pltpu.make_async_copy(gr_ref.at[me], gr_recv.at[others], gr_got).start())

    slab_ref = et_ref
    piece = rows // n
    right_hand, left_hand, far = lax.rem(g + 1, n), lax.rem(g + 3, n), lax.rem(g + 2, n)
    first_row = [128 * k for k in range(CHUNKS)]
    height = [128] * (CHUNKS - 1) + [width - 128 * (CHUNKS - 1)]

    def cols(j):
        return pl.ds(pl.multiple_of(j * piece, piece), piece)

    ring = {}
    to_of, back_of = (right_hand, left_hand), (left_hand, right_hand)

    def half(k, way, mine):
        h = height[k] // 2
        low = (way == 0) == mine
        return slice(first_row[k], first_row[k] + h) if low else slice(first_row[k] + h, first_row[k] + 2 * h)

    def send(k, way, step, src, dst):
        copy = pltpu.make_async_remote_copy(
            src, dst, ring_send.at[k, way, step], ring_recv.at[k, way, step],
            device_id={"rel": to_of[way]}, device_id_type=MESH)
        copy.start()
        ring[k, way, step] = copy

    def arrived(k, part, at):
        pltpu.make_async_copy(back_ref.at[k, :, at], recv_ref.at[k, :, at], back_recv.at[part]).wait()

    def scatter(k):
        if k == 0:
            arrived(0, 0, low)
            arrived(0, 1, high)
        else:
            arrived(k, k + 1, all_rows)
        values = [recv_ref[k].reshape(slots, 128).T, gh_ref[:, 128 * k : 128 * (k + 1)].T]
        vt = jnp.concatenate(values, axis=1)
        if k == CHUNKS - 1:
            rest = jnp.concatenate([recv_ref[0, :, SLOTS - 1, :], recv_ref[1, :, SLOTS - 1, :]], axis=1)
            rest = jnp.broadcast_to(rest[:, None, :], (peers, SLOTS, 256))
            own = (iota((peers, SLOTS, 256), 2) >> 4) == iota((peers, SLOTS, 256), 1)
            rest = jnp.where(own, rest, 0.0).reshape(slots, 256)
            rest = sum(dot(p, fold, NN) for p in parts(rest, 2))
            more = jnp.concatenate([rest.T[0:16], gh_ref[:, MAIN:WIDE].T[0:16]], axis=1)
            vt = jnp.concatenate([vt, more], axis=0)
        h = height[k]
        vt_hi[0:h], vt_lo[0:h] = parts(vt, 2)

        @pl.loop(0, n)
        def _(j):
            at = cols(j)
            slab_ref[first_row[k] : first_row[k] + h, at] = dot(vt_hi[0:h], oh_ref[:, at], NN) + dot(
                vt_lo[0:h], oh_ref[:, at], NN)

    def begin(k):
        h = height[k] // 2
        for way in range(2):
            send(k, way, 0, slab_ref.at[half(k, way, True), cols(far)], held_ref.at[k, way, 0, 0:h])
        for way in range(2):
            send(k, way, 1, slab_ref.at[half(k, way, False), cols(to_of[way])], held_ref.at[k, way, 1, 0:h])

    def add(k):
        h = height[k] // 2
        for way in range(2):
            ring[k, way, 0].wait_recv()
            sums_ref[k, way, 0:h] = slab_ref[half(k, way, True), cols(to_of[way])] + held_ref[k, way, 0, 0:h]
            send(k, way, 2, sums_ref.at[k, way, 0:h], held_ref.at[k, way, 2, 0:h])

    def share(k):
        h = height[k] // 2
        for way in range(2):
            ring[k, way, 1].wait_recv()
            ring[k, way, 2].wait_recv()
        for way in range(2):
            at = half(k, way, True)
            out_ref[at, cols(g)] = slab_ref[at, cols(g)] + held_ref[k, way, 2, 0:h] + held_ref[k, 1 - way, 1, 0:h]
        for step, mine_too in ((3, True), (4, False)):
            for way in range(2):
                at = half(k, way, mine_too)
                send(k, way, step, out_ref.at[at, cols(g)], out_ref.at[at, cols(g)])

    def forward(k):
        for way in range(2):
            ring[k, way, 3].wait_recv()
            at = half(k, way, True)
            send(k, way, 5, out_ref.at[at, cols(back_of[way])], out_ref.at[at, cols(back_of[way])])

    scatter(0)
    begin(0)
    add(0)
    share(0)
    scatter(1)
    begin(1)
    forward(0)
    add(1)
    share(1)
    scatter(2)
    begin(2)
    forward(1)
    pltpu.make_async_copy(gr_ref, gr_recv, gr_got).wait()
    gr_sum[0] = jnp.sum(gr_recv[...], axis=0)

    def start_sum(i, m, j):
        dom_copy(gr_sum.at[0], rel_recv.at[me], ag_send, ag_recv, z_plus[j] + spot_plus(m)).start()

    to_all(start_sum, lambda: pltpu.make_async_copy(gr_sum.at[0], rel_recv.at[me], ag_recv).start())
    add(2)
    share(2)
    pltpu.make_async_copy(gr_ref, rel_recv, ag_recv).wait()
    rel_out[...] = rel_recv[:, 0, :][:, 0:width]
    forward(2)

    first = pl.ds(0, others)
    seven = pl.ds(0, 7)
    pltpu.make_async_copy(ids_ref.at[seven], ids_ref.at[seven], ids_send).wait()
    pltpu.make_async_copy(asked_ref.at[0:56], asked_ref.at[0:56], line_send).wait()
    pltpu.make_async_copy(served_ref.at[first], served_ref.at[first], serve_send).wait()
    pltpu.make_async_copy(gr_ref.at[first], gr_ref.at[first], gr_send).wait()
    pltpu.make_async_copy(gr_ref.at[first], gr_ref.at[first], ag_send).wait()
    for k in range(CHUNKS):
        pltpu.make_async_copy(back_ref.at[k, first], back_ref.at[k, first], back_send).wait()
    for copy in [*sent, *ring.values()]:
        copy.wait_send()
    for k in range(CHUNKS):
        for way in range(2):
            ring[k, way, 4].wait_recv()
            ring[k, way, 5].wait_recv()


def body(embeddings, rel_weight, head_row, rel_id, tail_owner, tail_row, neg_owner, neg_row):
    peers, n = lax.axis_size("dom"), lax.axis_size("rel")
    rows, width = embeddings.shape
    edges, negs = head_row.shape[0], neg_row.shape[0]
    groups = rel_weight.shape[0]
    quarter = negs // n
    lists = WIDE
    slots = peers * SLOTS
    tall = (width - 128 * (CHUNKS - 1)) // 2
    lists_of = [a.reshape(1, a.shape[0]) for a in (tail_owner, tail_row, head_row, rel_id, neg_owner, neg_row)]
    ends = [sum(a.shape[1] for a in lists_of[: k + 1]) for k in range(len(lists_of))]
    joined = sum(
        jnp.pad(a, ((0, 0), (end - a.shape[1], ends[-1] - end))) for a, end in zip(lists_of, ends, strict=True))
    V, DMA = pltpu.VMEM, pltpu.SemaphoreType.DMA
    vmem, in_hbm = pl.BlockSpec(memory_space=pltpu.VMEM), pl.BlockSpec(memory_space=pltpu.HBM)
    scratch = [
        V((groups, width), F32), V((width, rows), F32), V((WIDE, rows), BF16), V((WIDE, rows), BF16), V((WIDE, rows), BF16),
        V((slots + edges, rows), BF16), V((8, 1, 128), I32), V((8, 1, 128), I32), V((peers, 1, 128), I32),
        V((peers, SLOTS, MAIN), F32), V((peers, SLOTS, MAIN), F32), V((lists, WIDE), F32), V((n, quarter, WIDE), F32),
        V((edges, WIDE), F32), V((edges, WIDE), F32), V((edges, WIDE), F32), V((edges, WIDE), F32), V((edges, WIDE), F32),
        V((n, quarter, WIDE), F32), V((n - 1, quarter, WIDE), F32),
        V((CHUNKS, peers, SLOTS, 128), F32), V((CHUNKS, peers, SLOTS, 128), F32),
        V((2 * tall, slots + edges), BF16), V((2 * tall, slots + edges), BF16),
        V((CHUNKS, 2, 3, tall, rows // n), F32), V((CHUNKS, 2, tall, rows // n), F32),
        V((groups, 1, WIDE), F32), V((peers, 1, WIDE), F32), V((1, 1, WIDE), F32), V((groups, 1, WIDE), F32),
        DMA((2,)), DMA(()), DMA(()), DMA(()), DMA(()), DMA(()), DMA((8,)), DMA((n - 1,)), DMA((n - 1,)), DMA((n - 1,)), DMA((n - 1,)),
        DMA(()), DMA((CHUNKS + 1,)), DMA(()), DMA(()), DMA(()), DMA(()), DMA((CHUNKS, 2, 6)), DMA((CHUNKS, 2, 6)),
    ]
    total, relation = pl.pallas_call(
        kernel,
        out_shape=(jax.ShapeDtypeStruct((width, rows), F32), jax.ShapeDtypeStruct((groups, width), F32)),
        in_specs=[vmem, in_hbm, in_hbm],
        out_specs=(vmem, vmem),
        scratch_shapes=scratch,
        compiler_params=pltpu.CompilerParams(collective_id=0, has_side_effects=True, vmem_limit_bytes=48 << 20),
        cost_estimate=pl.CostEstimate(flops=int(3e10), bytes_accessed=7 << 20, transcendentals=0),
        name="ranking_gradients",
    )(joined, rel_weight, embeddings.T)
    return (total.T, relation)


def solution(mesh):
    return jax.shard_map(
        body,
        mesh=mesh,
        in_specs=(
            P("dom", None),
            P("rel", None),
            P(("dom", "rel")),
            P(("dom", "rel")),
            P(("dom", "rel"), None),
            P(("dom", "rel")),
            P("dom", None),
            P("dom"),
        ),
        out_specs=(P("dom", None), P("rel", None)),
        check_vma=False,
    )
```

```python
import jax
import jax.numpy as jnp
from jax import lax
from jax.experimental import pallas as pl
from jax.experimental.pallas import tpu as pltpu
from jax.sharding import PartitionSpec as P

SPAN = 128
MAIN = 384
WIDE = 512
SLOTS = 16
CAP_T = 12
F32, BF16, I32 = jnp.float32, jnp.bfloat16, jnp.int32
MESH = pl.DeviceIdType.MESH
HIGHEST = lax.Precision.HIGHEST
NN = (((1,), (0,)), ((), ()))
NT = (((1,), (1,)), ((), ()))
TN = (((0,), (0,)), ((), ()))


def iota(shape, dim):
    return lax.broadcasted_iota(I32, shape, dim)


def parts(x, count):
    out = []
    for _ in range(count - 1):
        hi = x.astype(BF16)
        out.append(hi)
        x = x - hi.astype(F32)
    return out + [x.astype(BF16)]


def dot(a, b, dims):
    return lax.dot_general(a, b, dims, preferred_element_type=F32)


def dot_parts(onehot, values, dims=NN):
    total = dot(onehot, values[0], dims)
    for v in values[1:]:
        total = total + dot(onehot, v, dims)
    return total


def column(row):
    n = row.shape[1]
    return jnp.broadcast_to(row.astype(F32), (8, n)).T[:, 0:1].astype(I32)


def onehot(mask):
    return jnp.where(mask, 1.0, 0.0).astype(BF16)


def fold_matrix(rows, cols):
    l, m = iota((rows, cols), 0), iota((rows, cols), 1)
    return onehot((l & 15) == m)


def spread_matrix(rows, cols):
    m, l = iota((rows, cols), 0), iota((rows, cols), 1)
    return onehot((l & 15) == m)


DZ = (4, 5, 3, 6, 2, 7, 1, 0)
CHUNKS = 3


def id_column(ids, first):
    p = ids.shape[0]
    spread = jnp.broadcast_to(ids.astype(F32), (p, SLOTS, 128))
    own = iota((p, SLOTS, 128), 1) + first == iota((p, SLOTS, 128), 2)
    return jnp.sum(jnp.where(own, spread, 0.0), axis=2, keepdims=True).reshape(p * SLOTS, 1).astype(I32)


def kernel(
    lists_ref, towner_ref, nowner_ref, rel_in, et_in,
    out_ref, rel_out,
    rel_ref, et_ref, hi_ref, mid_ref, lo_ref, oh_ref, ids_ref, line_ref, asked_ref, served_ref, fetched_ref, got_ref, negs_ref,
    head_emb, rel_rows, query_ref, gh_ref, gt_ref, gn_ref, gn_held, gn_sums, back_ref, recv_ref, vt_hi, vt_lo, held_ref, sums_ref,
    gr_ref, gr_recv, gr_sum, rel_recv,
    load_sem, ids_send, ids_recv, line_send, line_recv, serve_send, high_recv, serve_recv, neg_send, neg_recv, gn_send, gn_recv,
    back_send, back_recv, gr_send, gr_got, ag_send, ag_recv, ring_send, ring_recv,
):
    peers = served_ref.shape[0]
    others = peers - 1
    n = negs_ref.shape[0]
    me, g = lax.axis_index("dom"), lax.axis_index("rel")
    edges = head_emb.shape[0]
    negs = nowner_ref.shape[1]
    quarter = negs // n
    lists = WIDE
    slots = peers * SLOTS
    width, rows = et_ref.shape
    tables = (hi_ref, mid_ref, lo_ref)
    z, y, core = lax.div(me, 8), lax.rem(lax.div(me, 2), 4), lax.rem(me, 2)
    spot = lax.rem(me, 8)
    z_plus = [lax.rem(z + d, 8) * 8 for d in DZ]
    z_minus = [lax.rem(z + 8 - d, 8) * 8 for d in DZ]

    def spot_plus(m):
        q = 7 - m
        return lax.rem(y + lax.div(q, 2), 4) * 2 + lax.rem(core + lax.rem(q, 2), 2)

    def spot_minus(m):
        q = 7 - m
        return lax.rem(y + 4 - lax.div(q, 2), 4) * 2 + lax.rem(core + lax.rem(q, 2), 2)

    def dom_copy(src, dst, send, recv, device):
        return pltpu.make_async_remote_copy(
            src, dst, send, recv, device_id={"dom": device}, device_id_type=MESH)

    low, high, all_rows = pl.ds(0, 8), pl.ds(8, 8), pl.ds(0, SLOTS)

    def to_all(start, own):
        @pl.loop(0, 8)
        def _(m):
            for j in range(7):
                start(m * 8 + j, m, j)

            @pl.when(m < 7)
            def _():
                start(m * 8 + 7, m, 7)

        own()

    loads = [pltpu.make_async_copy(et_in, et_ref, load_sem.at[0]), pltpu.make_async_copy(rel_in, rel_ref, load_sem.at[1])]
    for load in loads:
        load.start()
    barrier = pltpu.get_barrier_semaphore()
    for j in range(7):
        pl.semaphore_signal(barrier, inc=1, device_id={"dom": z_plus[j] + spot}, device_id_type=MESH)
    for m in range(7):
        pl.semaphore_signal(barrier, inc=1, device_id={"dom": z * 8 + spot_plus(m)}, device_id_type=MESH)
    for k in range(1, n):
        pl.semaphore_signal(barrier, inc=1, device_id={"rel": lax.rem(g + k, n)}, device_id_type=MESH)

    tail_row, head_row, rel_id = (lists_ref[:, edges * k : edges * (k + 1)] for k in range(3))
    neg_row = lists_ref[:, 3 * edges : 3 * edges + negs]

    def mine(row):
        return sum(jnp.where(g == q, row[:, quarter * q : quarter * (q + 1)], 0) for q in range(n))

    spare = jnp.zeros((1, lists - edges - quarter), I32)
    owner = jnp.concatenate([towner_ref[...], mine(nowner_ref[...]) + 64, spare + 255], axis=1)
    asked_rows = jnp.concatenate([tail_row, mine(neg_row), spare], axis=1)
    same = column(owner) == owner
    earlier = iota((lists, lists), 0) < iota((lists, lists), 1)
    position = jnp.sum(jnp.where(same & earlier, 1.0, 0.0), axis=0, keepdims=True).astype(I32)
    negative, valid = owner >= 64, owner < 128
    position = jnp.where(negative, position + CAP_T, position)
    owner = owner & 63
    dz = ((owner >> 3) - z + 8) & 7
    step_z = sum(jnp.where(dz == d, j, 0) for j, d in enumerate(DZ))
    dy, dc = (((owner >> 1) & 3) - y + 4) & 3, ((owner & 1) - core + 2) & 1
    slot = jnp.where(valid, ((7 - dy * 2 - dc) * 8 + step_z) * SLOTS + position, -1)
    left = jnp.where((iota((8, lists), 0) == step_z) & valid, (asked_rows + 1).astype(F32), 0.0)
    right = jnp.where(iota((128, lists), 0) == (owner & 7) * SLOTS + position, 1.0, 0.0)
    ids = lax.dot_general(left, right, NT, precision=HIGHEST, preferred_element_type=F32)
    ids_ref[...] = ((ids + 0.5).astype(I32) - 1)[:, None, :]

    pl.semaphore_wait(barrier, 14 + n - 1)
    for j in range(7):
        dom_copy(ids_ref.at[j], line_ref.at[j], ids_send, ids_recv, z_plus[j] + spot).start()
    pltpu.make_async_copy(ids_ref.at[7], line_ref.at[7], ids_recv).start()
    pltpu.make_async_copy(ids_ref, line_ref, ids_recv).wait()
    for m in range(7):
        dom_copy(line_ref, asked_ref.at[8 * m : 8 * m + 8], line_send, line_recv, z * 8 + spot_plus(m)).start()
    pltpu.make_async_copy(line_ref, asked_ref.at[56:64], line_recv).start()

    for load in loads:
        load.wait()

    @pl.loop(0, width // 16)
    def _(i):
        at = pl.multiple_of(i * 16, 16)
        for t, v in zip(tables, parts(et_ref[pl.ds(at, 16), :], 3), strict=True):
            t[pl.ds(at, 16), :] = v

    for t in tables:
        for k in range(1, 8):
            t[MAIN + 16 * k : MAIN + 16 * (k + 1), :] = t[MAIN : MAIN + 16, :]

    pltpu.make_async_copy(asked_ref, asked_ref, line_recv).wait()

    @pl.loop(0, 8)
    def _(m):
        at = pl.multiple_of(m * 8, 8)
        col = id_column(asked_ref[pl.ds(at, 8)], spot * SLOTS)
        hot = onehot(iota((8 * SLOTS, rows), 1) == col)
        oh_ref[pl.ds(pl.multiple_of(m * 8 * SLOTS, 8 * SLOTS), 8 * SLOTS), :] = hot
        got = dot_parts(hot, [t[...] for t in tables], NT)
        place = iota((8, SLOTS, 128), 1)
        lane = iota((8, SLOTS, 128), 2)
        rest = got[:, MAIN:].reshape(8, SLOTS, 128)
        rest = jnp.where((lane >> 4) == (place & 7), rest, 0.0)
        one = jnp.sum(jnp.where(place < 8, rest, 0.0), axis=1, keepdims=True)
        two = jnp.sum(jnp.where(place < 8, 0.0, rest), axis=1, keepdims=True)
        for k, part in enumerate((one, two, jnp.zeros_like(one))):
            main = got[:, 128 * k : 128 * (k + 1)].reshape(8, SLOTS, 128)
            served_ref[pl.ds(at, 8), :, 128 * k : 128 * (k + 1)] = jnp.where(place == SLOTS - 1, part, main)
        to = spot_minus(m)

        def start(i, j):
            dom_copy(served_ref.at[i, high], fetched_ref.at[i, high], serve_send, high_recv, z_minus[j] + to).start()

        for j in range(7):
            start(m * 8 + j, j)

        @pl.when(m < 7)
        def _():
            start(m * 8 + 7, 7)

    pltpu.make_async_copy(served_ref.at[others, high], fetched_ref.at[others, high], high_recv).start()

    def start_low(i, m, j):
        dom_copy(
            served_ref.at[i, low], fetched_ref.at[i, low], serve_send, serve_recv.at[m], z_minus[j] + spot_minus(m)).start()

    to_all(start_low, lambda: pltpu.make_async_copy(
        served_ref.at[others, low], fetched_ref.at[others, low], serve_recv.at[7]).start())

    hot = onehot(iota((edges, rows), 1) == column(head_row))
    oh_ref[slots:, :] = hot
    got = dot_parts(hot, [t[...] for t in tables], NT)
    head_emb[:, 0:MAIN] = got[:, 0:MAIN]
    head_emb[:, MAIN:WIDE] = jnp.where(iota((edges, 128), 1) < width - MAIN, got[:, MAIN:WIDE], 0.0)
    groups = rel_ref.shape[0]
    hot = onehot(iota((edges, groups), 1) == column(rel_id))
    rel_rows[:, 0:width] = dot_parts(hot, parts(rel_ref[...], 3))
    rel_rows[:, width:WIDE] = jnp.zeros((edges, WIDE - width), F32)
    query_ref[...] = head_emb[...] * rel_rows[...]

    slot_col = column(slot)
    fold = fold_matrix(256, 128)
    pltpu.make_async_copy(served_ref.at[:, high], fetched_ref.at[:, high], high_recv).wait()
    packed = parts(fetched_ref[:, SLOTS - 1, 0:256], 3)

    def remainders(at):
        where = slot_col[at]
        count = where.shape[0]
        rest = dot_parts(onehot(iota((count, peers), 1) == (where >> 4)), packed)
        rest = jnp.where((iota((count, 256), 1) >> 4) == (where & 15), rest, 0.0)
        return sum(dot(p, fold, NN) for p in parts(rest, 3))

    own = slice(edges, edges + quarter)
    line = iota((quarter, peers * 8), 1)
    hot = onehot((line >> 3) * SLOTS + 8 + (line & 7) == slot_col[own])
    negs_ref[g, :, 0:MAIN] = dot_parts(hot, parts(fetched_ref[:, 8:SLOTS, :].reshape(peers * 8, MAIN), 3))
    negs_ref[g, :, MAIN:WIDE] = remainders(own)

    def rel_copy(src, dst, send, recv, k):
        return pltpu.make_async_remote_copy(
            src, dst, send, recv, device_id={"rel": lax.rem(g + k, n)}, device_id_type=MESH)

    copies = [rel_copy(negs_ref.at[g], negs_ref.at[g], neg_send.at[k - 1], neg_recv.at[k - 1], k) for k in range(1, n)]
    for copy in copies:
        copy.start()
    tails = slice(0, edges)
    got_ref[:, 0:MAIN] = jnp.zeros((edges, MAIN), F32)
    got_ref[:, MAIN:WIDE] = remainders(tails)

    @pl.loop(0, 4)
    def _(b):
        at = pl.ds(pl.multiple_of(b * 16, 16), 16)
        for k in range(2):
            part = pl.ds(pl.multiple_of(b * 16, 16) + 8 * k, 8)
            pltpu.make_async_copy(served_ref.at[part, low], fetched_ref.at[part, low], serve_recv.at[2 * b + k]).wait()
        hot = onehot(iota((edges, 16 * SLOTS), 1) + b * (16 * SLOTS) == slot_col[tails])
        got_ref[:, 0:MAIN] += dot_parts(hot, parts(fetched_ref[at].reshape(16 * SLOTS, MAIN), 3))

    positive = jnp.sum(query_ref[...] * got_ref[...], axis=1, keepdims=True)
    for copy in copies:
        copy.wait_recv()
    sent = list(copies)

    def neg_rows(c):
        return negs_ref[...].reshape(negs, WIDE)[c * SPAN : (c + 1) * SPAN]

    coefs = []
    for c in range(edges // SPAN):
        at = slice(c * SPAN, (c + 1) * SPAN)
        queries = query_ref[at]
        scores = lax.dot_general(queries, neg_rows(c), NT, precision=HIGHEST, preferred_element_type=F32)
        row_max = jnp.maximum(positive[at], jnp.max(scores, axis=1, keepdims=True))
        pos_exp = jnp.exp(positive[at] - row_max)
        neg_exp = jnp.exp(scores - row_max)
        total = pos_exp + jnp.sum(neg_exp, axis=1, keepdims=True)
        pos_coef = pos_exp / total - 1.0
        neg_coef = neg_exp / total
        coefs.append((pos_coef, neg_coef))
        gt_ref[at] = pos_coef * queries
        grad_neg = lax.dot_general(neg_coef.T, queries, NN, precision=HIGHEST, preferred_element_type=F32)
        first = c * SPAN
        while first < (c + 1) * SPAN:
            q, inside = divmod(first, quarter)
            count = min(quarter - inside, (c + 1) * SPAN - first)
            gn_ref[q, inside : inside + count] = grad_neg[first - c * SPAN : first - c * SPAN + count]
            first += count

    right_hand, left_hand, far = lax.rem(g + 1, n), lax.rem(g + 3, n), lax.rem(g + 2, n)
    to_of, back_of = (right_hand, left_hand), (left_hand, right_hand)
    top, bottom = slice(0, quarter // 2), slice(quarter // 2, quarter)
    two_hops, one_hop = (top, bottom), (bottom, top)

    def gn_copy(way, step, src):
        copy = pltpu.make_async_remote_copy(
            src, gn_held.at[way, step], gn_send.at[way, step], gn_recv.at[way, step],
            device_id={"rel": to_of[way]}, device_id_type=MESH)
        copy.start()
        sent.append(copy)
        return copy

    firsts = [gn_copy(way, 0, gn_ref.at[far, two_hops[way]]) for way in range(2)]
    arrivals = [gn_copy(way, 1, gn_ref.at[to_of[way], one_hop[way]]) for way in range(2)]

    def send_back(k, part, at):
        def start(i, m, j):
            dom_copy(
                back_ref.at[k, i, at], recv_ref.at[k, i, at], back_send, back_recv.at[part], z_plus[j] + spot_plus(m)).start()

        def own():
            pltpu.make_async_copy(back_ref.at[k, others, at], recv_ref.at[k, others, at], back_recv.at[part]).start()

        to_all(start, own)

    hot = onehot(iota((slots, edges), 0) == slot[:, 0:edges])
    for k in range(CHUNKS):
        back_ref[k] = dot_parts(hot, parts(gt_ref[:, 128 * k : 128 * (k + 1)], 2)).reshape(peers, SLOTS, 128)
        if k == 0:
            send_back(0, 0, low)
            for way in range(2):
                firsts[way].wait_recv()
                gn_sums[way] = gn_ref[to_of[way], two_hops[way]] + gn_held[way, 0]
                arrivals.append(gn_copy(way, 2, gn_sums.at[way]))

    spread = spread_matrix(128, 256)

    def remainders_back(values, at):
        count = values.shape[0]
        rest = sum(dot(p, spread, NN) for p in parts(values, 2))
        rest = jnp.where((iota((count, 256), 1) >> 4) == (slot_col[at] & 15), rest, 0.0)
        return dot_parts(onehot(iota((peers, count), 0) == (slot[:, at] >> 4)), parts(rest, 2))

    rest = remainders_back(gt_ref[:, MAIN:WIDE], slice(0, edges))
    for copy in arrivals:
        copy.wait_recv()
    grad_neg = jnp.concatenate(
        [gn_ref[g, two_hops[way]] + gn_held[way, 2] + gn_held[1 - way, 1] for way in range(2)], axis=0)
    rest = rest + remainders_back(grad_neg[:, MAIN:WIDE], own)
    line = iota((peers * 8, quarter), 0)
    hot = onehot((line >> 3) * SLOTS + 8 + (line & 7) == slot[:, own])
    last = iota((peers, 8, 128), 1) == 7
    for k in range(CHUNKS):
        more = dot_parts(hot, parts(grad_neg[:, 128 * k : 128 * (k + 1)], 2)).reshape(peers, 8, 128)
        more = back_ref[k, :, 8:SLOTS, :] + more
        if k < 2:
            more = jnp.where(last, rest[:, 128 * k : 128 * (k + 1)][:, None, :], more)
        back_ref[k, :, 8:SLOTS, :] = more
        send_back(k, k + 1, high if k == 0 else all_rows)

    gr_parts = []
    for c in range(edges // SPAN):
        at = slice(c * SPAN, (c + 1) * SPAN)
        pos_coef, neg_coef = coefs[c]
        grad_query = pos_coef * got_ref[at] + lax.dot_general(
            neg_coef, neg_rows(c), NN, precision=HIGHEST, preferred_element_type=F32)
        gh_ref[at] = grad_query * rel_rows[at]
        hot = onehot(iota((groups, SPAN), 0) == rel_id[:, at])
        gr_parts.append(dot_parts(hot, parts(grad_query * head_emb[at], 3)))
    gr_ref[...] = sum(gr_parts)[:, None, :]

    def start_rel(i, m, j):
        to = z_plus[j] + spot_plus(m)
        dom_copy(gr_ref.at[to], gr_recv.at[i], gr_send, gr_got, to).start()

    to_all(start_rel, lambda: pltpu.make_async_copy(gr_ref.at[me], gr_recv.at[others], gr_got).start())

    slab_ref = et_ref
    piece = rows // n
    first_row = [128 * k for k in range(CHUNKS)]
    height = [128] * (CHUNKS - 1) + [width - 128 * (CHUNKS - 1)]

    def cols(j):
        return pl.ds(pl.multiple_of(j * piece, piece), piece)

    ring = {}

    def half(k, way, mine):
        h = height[k] // 2
        low = (way == 0) == mine
        return slice(first_row[k], first_row[k] + h) if low else slice(first_row[k] + h, first_row[k] + 2 * h)

    def send(k, way, step, src, dst):
        copy = pltpu.make_async_remote_copy(
            src, dst, ring_send.at[k, way, step], ring_recv.at[k, way, step],
            device_id={"rel": to_of[way]}, device_id_type=MESH)
        copy.start()
        ring[k, way, step] = copy

    def arrived(k, part, at):
        pltpu.make_async_copy(back_ref.at[k, :, at], recv_ref.at[k, :, at], back_recv.at[part]).wait()

    def scatter(k):
        if k == 0:
            arrived(0, 0, low)
            arrived(0, 1, high)
        else:
            arrived(k, k + 1, all_rows)
        values = [recv_ref[k].reshape(slots, 128).T, gh_ref[:, 128 * k : 128 * (k + 1)].T]
        vt = jnp.concatenate(values, axis=1)
        if k == CHUNKS - 1:
            rest = jnp.concatenate([recv_ref[0, :, SLOTS - 1, :], recv_ref[1, :, SLOTS - 1, :]], axis=1)
            rest = jnp.broadcast_to(rest[:, None, :], (peers, SLOTS, 256))
            own = (iota((peers, SLOTS, 256), 2) >> 4) == iota((peers, SLOTS, 256), 1)
            rest = jnp.where(own, rest, 0.0).reshape(slots, 256)
            rest = sum(dot(p, fold, NN) for p in parts(rest, 2))
            more = jnp.concatenate([rest.T[0:16], gh_ref[:, MAIN:WIDE].T[0:16]], axis=1)
            vt = jnp.concatenate([vt, more], axis=0)
        h = height[k]
        vt_hi[0:h], vt_lo[0:h] = parts(vt, 2)

        @pl.loop(0, n)
        def _(j):
            at = cols(j)
            slab_ref[first_row[k] : first_row[k] + h, at] = dot(vt_hi[0:h], oh_ref[:, at], NN) + dot(
                vt_lo[0:h], oh_ref[:, at], NN)

    def begin(k):
        h = height[k] // 2
        for way in range(2):
            send(k, way, 0, slab_ref.at[half(k, way, True), cols(far)], held_ref.at[k, way, 0, 0:h])
        for way in range(2):
            send(k, way, 1, slab_ref.at[half(k, way, False), cols(to_of[way])], held_ref.at[k, way, 1, 0:h])

    def add(k):
        h = height[k] // 2
        for way in range(2):
            ring[k, way, 0].wait_recv()
            sums_ref[k, way, 0:h] = slab_ref[half(k, way, True), cols(to_of[way])] + held_ref[k, way, 0, 0:h]
            send(k, way, 2, sums_ref.at[k, way, 0:h], held_ref.at[k, way, 2, 0:h])

    def share(k):
        h = height[k] // 2
        for way in range(2):
            ring[k, way, 1].wait_recv()
            ring[k, way, 2].wait_recv()
        for way in range(2):
            at = half(k, way, True)
            out_ref[at, cols(g)] = slab_ref[at, cols(g)] + held_ref[k, way, 2, 0:h] + held_ref[k, 1 - way, 1, 0:h]
        for step, mine_too in ((3, True), (4, False)):
            for way in range(2):
                at = half(k, way, mine_too)
                send(k, way, step, out_ref.at[at, cols(g)], out_ref.at[at, cols(g)])

    def forward(k):
        for way in range(2):
            ring[k, way, 3].wait_recv()
            at = half(k, way, True)
            send(k, way, 5, out_ref.at[at, cols(back_of[way])], out_ref.at[at, cols(back_of[way])])

    scatter(0)
    begin(0)
    add(0)
    share(0)
    scatter(1)
    begin(1)
    forward(0)
    add(1)
    share(1)
    scatter(2)
    begin(2)
    forward(1)
    pltpu.make_async_copy(gr_ref, gr_recv, gr_got).wait()
    gr_sum[0] = jnp.sum(gr_recv[...], axis=0)

    def start_sum(i, m, j):
        dom_copy(gr_sum.at[0], rel_recv.at[me], ag_send, ag_recv, z_plus[j] + spot_plus(m)).start()

    to_all(start_sum, lambda: pltpu.make_async_copy(gr_sum.at[0], rel_recv.at[me], ag_recv).start())
    add(2)
    share(2)
    pltpu.make_async_copy(gr_ref, rel_recv, ag_recv).wait()
    rel_out[...] = rel_recv[:, 0, :][:, 0:width]
    forward(2)

    first = pl.ds(0, others)
    seven = pl.ds(0, 7)
    pltpu.make_async_copy(ids_ref.at[seven], ids_ref.at[seven], ids_send).wait()
    pltpu.make_async_copy(asked_ref.at[0:56], asked_ref.at[0:56], line_send).wait()
    pltpu.make_async_copy(served_ref.at[first], served_ref.at[first], serve_send).wait()
    pltpu.make_async_copy(gr_ref.at[first], gr_ref.at[first], gr_send).wait()
    pltpu.make_async_copy(gr_ref.at[first], gr_ref.at[first], ag_send).wait()
    for k in range(CHUNKS):
        pltpu.make_async_copy(back_ref.at[k, first], back_ref.at[k, first], back_send).wait()
    for copy in [*sent, *ring.values()]:
        copy.wait_send()
    for k in range(CHUNKS):
        for way in range(2):
            ring[k, way, 4].wait_recv()
            ring[k, way, 5].wait_recv()


def body(embeddings, rel_weight, head_row, rel_id, tail_owner, tail_row, neg_owner, neg_row):
    peers, n = lax.axis_size("dom"), lax.axis_size("rel")
    rows, width = embeddings.shape
    edges, negs = head_row.shape[0], neg_row.shape[0]
    groups = rel_weight.shape[0]
    quarter = negs // n
    lists = WIDE
    slots = peers * SLOTS
    tall = (width - 128 * (CHUNKS - 1)) // 2
    lists_of = (tail_row, head_row, rel_id, neg_row)
    ends = [sum(a.shape[0] for a in lists_of[: k + 1]) for k in range(len(lists_of))]
    joined = sum(jnp.pad(a, (end - a.shape[0], ends[-1] - end)) for a, end in zip(lists_of, ends, strict=True))
    joined = joined.reshape(1, ends[-1])
    V, DMA = pltpu.VMEM, pltpu.SemaphoreType.DMA
    vmem, in_hbm = pl.BlockSpec(memory_space=pltpu.VMEM), pl.BlockSpec(memory_space=pltpu.HBM)
    scratch = [
        V((groups, width), F32), V((width, rows), F32), V((WIDE, rows), BF16), V((WIDE, rows), BF16), V((WIDE, rows), BF16),
        V((slots + edges, rows), BF16), V((8, 1, 128), I32), V((8, 1, 128), I32), V((peers, 1, 128), I32),
        V((peers, SLOTS, MAIN), F32), V((peers, SLOTS, MAIN), F32), V((edges, WIDE), F32), V((n, quarter, WIDE), F32),
        V((edges, WIDE), F32), V((edges, WIDE), F32), V((edges, WIDE), F32), V((edges, WIDE), F32), V((edges, WIDE), F32),
        V((n, quarter, WIDE), F32), V((2, 3, quarter // 2, WIDE), F32), V((2, quarter // 2, WIDE), F32),
        V((CHUNKS, peers, SLOTS, 128), F32), V((CHUNKS, peers, SLOTS, 128), F32),
        V((2 * tall, slots + edges), BF16), V((2 * tall, slots + edges), BF16),
        V((CHUNKS, 2, 3, tall, rows // n), F32), V((CHUNKS, 2, tall, rows // n), F32),
        V((groups, 1, WIDE), F32), V((peers, 1, WIDE), F32), V((1, 1, WIDE), F32), V((groups, 1, WIDE), F32),
        DMA((2,)), DMA(()), DMA(()), DMA(()), DMA(()), DMA(()), DMA(()), DMA((8,)), DMA((n - 1,)), DMA((n - 1,)), DMA((2, 3)), DMA((2, 3)),
        DMA(()), DMA((CHUNKS + 1,)), DMA(()), DMA(()), DMA(()), DMA(()), DMA((CHUNKS, 2, 6)), DMA((CHUNKS, 2, 6)),
    ]
    total, relation = pl.pallas_call(
        kernel,
        out_shape=(jax.ShapeDtypeStruct((width, rows), F32), jax.ShapeDtypeStruct((groups, width), F32)),
        in_specs=[vmem, vmem, vmem, in_hbm, in_hbm],
        out_specs=(vmem, vmem),
        scratch_shapes=scratch,
        compiler_params=pltpu.CompilerParams(collective_id=0, has_side_effects=True, vmem_limit_bytes=48 << 20),
        cost_estimate=pl.CostEstimate(flops=int(3e10), bytes_accessed=7 << 20, transcendentals=0),
        name="ranking_gradients",
    )(joined, tail_owner.reshape(1, edges), neg_owner.reshape(1, negs), rel_weight, embeddings.T)
    return (total.T, relation)


def solution(mesh):
    return jax.shard_map(
        body,
        mesh=mesh,
        in_specs=(
            P("dom", None),
            P("rel", None),
            P(("dom", "rel")),
            P(("dom", "rel")),
            P(("dom", "rel"), None),
            P(("dom", "rel")),
            P("dom", None),
            P("dom"),
        ),
        out_specs=(P("dom", None), P("rel", None)),
        check_vma=False,
    )
```

```python
import jax
import jax.numpy as jnp
from jax import lax
from jax.experimental import pallas as pl
from jax.experimental.pallas import tpu as pltpu
from jax.sharding import PartitionSpec as P

SPAN = 128
MAIN = 384
WIDE = 512
SLOTS = 16
CAP_T = 12
F32, BF16, I32 = jnp.float32, jnp.bfloat16, jnp.int32
MESH = pl.DeviceIdType.MESH
HIGHEST = lax.Precision.HIGHEST
NN = (((1,), (0,)), ((), ()))
NT = (((1,), (1,)), ((), ()))
TN = (((0,), (0,)), ((), ()))


def iota(shape, dim):
    return lax.broadcasted_iota(I32, shape, dim)


def parts(x, count):
    out = []
    for _ in range(count - 1):
        hi = x.astype(BF16)
        out.append(hi)
        x = x - hi.astype(F32)
    return out + [x.astype(BF16)]


def dot(a, b, dims):
    return lax.dot_general(a, b, dims, preferred_element_type=F32)


def dot_parts(onehot, values, dims=NN):
    total = dot(onehot, values[0], dims)
    for v in values[1:]:
        total = total + dot(onehot, v, dims)
    return total


def column(row):
    n = row.shape[1]
    return jnp.broadcast_to(row.astype(F32), (8, n)).T[:, 0:1].astype(I32)


def onehot(mask):
    return jnp.where(mask, 1.0, 0.0).astype(BF16)


def fold_matrix(rows, cols):
    l, m = iota((rows, cols), 0), iota((rows, cols), 1)
    return onehot((l & 15) == m)


def spread_matrix(rows, cols):
    m, l = iota((rows, cols), 0), iota((rows, cols), 1)
    return onehot((l & 15) == m)


DZ = (4, 5, 3, 6, 2, 7, 1, 0)
CHUNKS = 3


def id_column(ids, first):
    p = ids.shape[0]
    spread = jnp.broadcast_to(ids.astype(F32), (p, SLOTS, 128))
    own = iota((p, SLOTS, 128), 1) + first == iota((p, SLOTS, 128), 2)
    return jnp.sum(jnp.where(own, spread, 0.0), axis=2, keepdims=True).reshape(p * SLOTS, 1).astype(I32)


def kernel(
    lists_ref, towner_ref, nowner_ref, rel_in, et_in,
    out_ref, rel_out,
    rel_ref, et_ref, hi_ref, mid_ref, lo_ref, oh_ref, ids_ref, line_ref, asked_ref, served_ref, fetched_ref, got_ref, negs_ref,
    head_emb, rel_rows, query_ref, gh_ref, gt_ref, gn_ref, gn_held, gn_sums, back_ref, recv_ref, vt_ref, held_ref, sums_ref,
    gr_ref, gr_recv, gr_sum, rel_recv,
    load_sem, ids_send, ids_recv, line_send, line_recv, serve_send, high_recv, serve_recv, neg_send, neg_recv, gn_send, gn_recv,
    back_send, back_recv, gr_send, gr_got, ag_send, ag_recv, ring_send, ring_recv,
):
    peers = served_ref.shape[0]
    others = peers - 1
    n = negs_ref.shape[0]
    me, g = lax.axis_index("dom"), lax.axis_index("rel")
    edges = head_emb.shape[0]
    negs = nowner_ref.shape[1]
    quarter = negs // n
    lists = WIDE
    slots = peers * SLOTS
    width, rows = et_ref.shape
    tables = (hi_ref, mid_ref, lo_ref)
    z, y, core = lax.div(me, 8), lax.rem(lax.div(me, 2), 4), lax.rem(me, 2)
    spot = lax.rem(me, 8)
    z_plus = [lax.rem(z + d, 8) * 8 for d in DZ]
    z_minus = [lax.rem(z + 8 - d, 8) * 8 for d in DZ]

    def spot_plus(m):
        q = 7 - m
        return lax.rem(y + lax.div(q, 2), 4) * 2 + lax.rem(core + lax.rem(q, 2), 2)

    def spot_minus(m):
        q = 7 - m
        return lax.rem(y + 4 - lax.div(q, 2), 4) * 2 + lax.rem(core + lax.rem(q, 2), 2)

    def dom_copy(src, dst, send, recv, device):
        return pltpu.make_async_remote_copy(
            src, dst, send, recv, device_id={"dom": device}, device_id_type=MESH)

    low, high, all_rows = pl.ds(0, 8), pl.ds(8, 8), pl.ds(0, SLOTS)

    def to_all(start, own):
        @pl.loop(0, 8)
        def _(m):
            for j in range(7):
                start(m * 8 + j, m, j)

            @pl.when(m < 7)
            def _():
                start(m * 8 + 7, m, 7)

        own()

    loads = [pltpu.make_async_copy(et_in, et_ref, load_sem.at[0]), pltpu.make_async_copy(rel_in, rel_ref, load_sem.at[1])]
    for load in loads:
        load.start()
    barrier = pltpu.get_barrier_semaphore()
    for j in range(7):
        pl.semaphore_signal(barrier, inc=1, device_id={"dom": z_plus[j] + spot}, device_id_type=MESH)
    for m in range(7):
        pl.semaphore_signal(barrier, inc=1, device_id={"dom": z * 8 + spot_plus(m)}, device_id_type=MESH)
    for k in range(1, n):
        pl.semaphore_signal(barrier, inc=1, device_id={"rel": lax.rem(g + k, n)}, device_id_type=MESH)

    tail_row, head_row, rel_id = (lists_ref[edges * k : edges * (k + 1)][None, :] for k in range(3))
    neg_row = lists_ref[3 * edges : 3 * edges + negs][None, :]

    def mine(row):
        return sum(jnp.where(g == q, row[:, quarter * q : quarter * (q + 1)], 0) for q in range(n))

    spare = jnp.zeros((1, lists - edges - quarter), I32)
    owner = jnp.concatenate([towner_ref[...], mine(nowner_ref[...]) + 64, spare + 255], axis=1)
    asked_rows = jnp.concatenate([tail_row, mine(neg_row), spare], axis=1)
    same = column(owner) == owner
    earlier = iota((lists, lists), 0) < iota((lists, lists), 1)
    position = jnp.sum(jnp.where(same & earlier, 1.0, 0.0), axis=0, keepdims=True).astype(I32)
    negative, valid = owner >= 64, owner < 128
    position = jnp.where(negative, position + CAP_T, position)
    owner = owner & 63
    dz = ((owner >> 3) - z + 8) & 7
    step_z = sum(jnp.where(dz == d, j, 0) for j, d in enumerate(DZ))
    dy, dc = (((owner >> 1) & 3) - y + 4) & 3, ((owner & 1) - core + 2) & 1
    slot = jnp.where(valid, ((7 - dy * 2 - dc) * 8 + step_z) * SLOTS + position, -1)
    left = jnp.where((iota((8, lists), 0) == step_z) & valid, (asked_rows + 1).astype(F32), 0.0)
    right = jnp.where(iota((128, lists), 0) == (owner & 7) * SLOTS + position, 1.0, 0.0)
    ids = lax.dot_general(left, right, NT, precision=HIGHEST, preferred_element_type=F32)
    ids_ref[...] = ((ids + 0.5).astype(I32) - 1)[:, None, :]

    pl.semaphore_wait(barrier, 14 + n - 1)
    for j in range(7):
        dom_copy(ids_ref.at[j], line_ref.at[j], ids_send, ids_recv, z_plus[j] + spot).start()
    pltpu.make_async_copy(ids_ref.at[7], line_ref.at[7], ids_recv).start()
    for load in loads:
        load.wait()

    def split(start, stop):
        @pl.loop(start, stop)
        def _(i):
            at = pl.multiple_of(i * 16, 16)
            for t, v in zip(tables, parts(et_ref[pl.ds(at, 16), :], 3), strict=True):
                t[pl.ds(at, 16), :] = v

    split(0, width // 32)
    pltpu.make_async_copy(ids_ref, line_ref, ids_recv).wait()
    for m in range(7):
        dom_copy(line_ref, asked_ref.at[8 * m : 8 * m + 8], line_send, line_recv, z * 8 + spot_plus(m)).start()
    pltpu.make_async_copy(line_ref, asked_ref.at[56:64], line_recv).start()

    split(width // 32, width // 16)
    for t in tables:
        for k in range(1, 8):
            t[MAIN + 16 * k : MAIN + 16 * (k + 1), :] = t[MAIN : MAIN + 16, :]

    pltpu.make_async_copy(asked_ref, asked_ref, line_recv).wait()

    @pl.loop(0, 8)
    def _(m):
        at = pl.multiple_of(m * 8, 8)
        col = id_column(asked_ref[pl.ds(at, 8)], spot * SLOTS)
        hot = onehot(iota((8 * SLOTS, rows), 1) == col)
        oh_ref[pl.ds(pl.multiple_of(m * 8 * SLOTS, 8 * SLOTS), 8 * SLOTS), :] = hot
        got = dot_parts(hot, [t[...] for t in tables], NT)
        place = iota((8, SLOTS, 128), 1)
        lane = iota((8, SLOTS, 128), 2)
        rest = got[:, MAIN:].reshape(8, SLOTS, 128)
        rest = jnp.where((lane >> 4) == (place & 7), rest, 0.0)
        one = jnp.sum(jnp.where(place < 8, rest, 0.0), axis=1, keepdims=True)
        two = jnp.sum(jnp.where(place < 8, 0.0, rest), axis=1, keepdims=True)
        for k, part in enumerate((one, two, jnp.zeros_like(one))):
            main = got[:, 128 * k : 128 * (k + 1)].reshape(8, SLOTS, 128)
            served_ref[pl.ds(at, 8), :, 128 * k : 128 * (k + 1)] = jnp.where(place == SLOTS - 1, part, main)
        to = spot_minus(m)

        def start(i, j):
            dom_copy(served_ref.at[i, high], fetched_ref.at[i, high], serve_send, high_recv, z_minus[j] + to).start()

        for j in range(7):
            start(m * 8 + j, j)

        @pl.when(m < 7)
        def _():
            start(m * 8 + 7, 7)

    pltpu.make_async_copy(served_ref.at[others, high], fetched_ref.at[others, high], high_recv).start()

    def start_low(i, m, j):
        dom_copy(
            served_ref.at[i, low], fetched_ref.at[i, low], serve_send, serve_recv.at[m], z_minus[j] + spot_minus(m)).start()

    to_all(start_low, lambda: pltpu.make_async_copy(
        served_ref.at[others, low], fetched_ref.at[others, low], serve_recv.at[7]).start())

    hot = onehot(iota((edges, rows), 1) == column(head_row))
    oh_ref[slots:, :] = hot
    got = dot_parts(hot, [t[...] for t in tables], NT)
    head_emb[:, 0:MAIN] = got[:, 0:MAIN]
    head_emb[:, MAIN:WIDE] = jnp.where(iota((edges, 128), 1) < width - MAIN, got[:, MAIN:WIDE], 0.0)
    groups = rel_ref.shape[0]
    hot = onehot(iota((edges, groups), 1) == column(rel_id))
    rel_rows[:, 0:width] = dot_parts(hot, parts(rel_ref[...], 3))
    rel_rows[:, width:WIDE] = jnp.zeros((edges, WIDE - width), F32)
    query_ref[...] = head_emb[...] * rel_rows[...]

    slot_col = column(slot)
    fold = fold_matrix(256, 128)
    pltpu.make_async_copy(served_ref.at[:, high], fetched_ref.at[:, high], high_recv).wait()
    packed = parts(fetched_ref[:, SLOTS - 1, 0:256], 3)

    def remainders(at):
        where = slot_col[at]
        count = where.shape[0]
        rest = dot_parts(onehot(iota((count, peers), 1) == (where >> 4)), packed)
        rest = jnp.where((iota((count, 256), 1) >> 4) == (where & 15), rest, 0.0)
        return sum(dot(p, fold, NN) for p in parts(rest, 3))

    own = slice(edges, edges + quarter)
    line = iota((quarter, peers * 8), 1)
    hot = onehot((line >> 3) * SLOTS + 8 + (line & 7) == slot_col[own])
    negs_ref[g, :, 0:MAIN] = dot_parts(hot, parts(fetched_ref[:, 8:SLOTS, :].reshape(peers * 8, MAIN), 3))
    negs_ref[g, :, MAIN:WIDE] = remainders(own)

    def rel_copy(src, dst, send, recv, k):
        return pltpu.make_async_remote_copy(
            src, dst, send, recv, device_id={"rel": lax.rem(g + k, n)}, device_id_type=MESH)

    copies = [rel_copy(negs_ref.at[g], negs_ref.at[g], neg_send.at[k - 1], neg_recv.at[k - 1], k) for k in range(1, n)]
    for copy in copies:
        copy.start()
    tails = slice(0, edges)
    got_ref[:, 0:MAIN] = jnp.zeros((edges, MAIN), F32)
    got_ref[:, MAIN:WIDE] = remainders(tails)

    @pl.loop(0, 4)
    def _(b):
        at = pl.ds(pl.multiple_of(b * 16, 16), 16)
        for k in range(2):
            part = pl.ds(pl.multiple_of(b * 16, 16) + 8 * k, 8)
            pltpu.make_async_copy(served_ref.at[part, low], fetched_ref.at[part, low], serve_recv.at[2 * b + k]).wait()
        hot = onehot(iota((edges, 16 * SLOTS), 1) + b * (16 * SLOTS) == slot_col[tails])
        got_ref[:, 0:MAIN] += dot_parts(hot, parts(fetched_ref[at].reshape(16 * SLOTS, MAIN), 3))

    positive = jnp.sum(query_ref[...] * got_ref[...], axis=1, keepdims=True)
    for copy in copies:
        copy.wait_recv()
    sent = list(copies)

    def neg_rows(c):
        return negs_ref[...].reshape(negs, WIDE)[c * SPAN : (c + 1) * SPAN]

    coefs = []
    for c in range(edges // SPAN):
        at = slice(c * SPAN, (c + 1) * SPAN)
        queries = query_ref[at]
        scores = lax.dot_general(queries, neg_rows(c), NT, precision=HIGHEST, preferred_element_type=F32)
        row_max = jnp.maximum(positive[at], jnp.max(scores, axis=1, keepdims=True))
        pos_exp = jnp.exp(positive[at] - row_max)
        neg_exp = jnp.exp(scores - row_max)
        total = pos_exp + jnp.sum(neg_exp, axis=1, keepdims=True)
        pos_coef = pos_exp / total - 1.0
        neg_coef = neg_exp / total
        coefs.append((pos_coef, neg_coef))
        gt_ref[at] = pos_coef * queries
        grad_neg = lax.dot_general(neg_coef.T, queries, NN, precision=HIGHEST, preferred_element_type=F32)
        first = c * SPAN
        while first < (c + 1) * SPAN:
            q, inside = divmod(first, quarter)
            count = min(quarter - inside, (c + 1) * SPAN - first)
            gn_ref[q, inside : inside + count] = grad_neg[first - c * SPAN : first - c * SPAN + count]
            first += count

    right_hand, left_hand, far = lax.rem(g + 1, n), lax.rem(g + 3, n), lax.rem(g + 2, n)
    to_of, back_of = (right_hand, left_hand), (left_hand, right_hand)
    top, bottom = slice(0, quarter // 2), slice(quarter // 2, quarter)
    two_hops, one_hop = (top, bottom), (bottom, top)

    part_cols = (slice(0, 128), slice(128, WIDE))

    def gn_copy(part, way, step, src):
        copy = pltpu.make_async_remote_copy(
            src, gn_held.at[way, step, :, part_cols[part]], gn_send.at[part, way, step], gn_recv.at[part, way, step],
            device_id={"rel": to_of[way]}, device_id_type=MESH)
        copy.start()
        sent.append(copy)
        return copy

    def gn_begin(part):
        at = part_cols[part]
        two = [gn_copy(part, way, 0, gn_ref.at[far, two_hops[way], at]) for way in range(2)]
        return two, [gn_copy(part, way, 1, gn_ref.at[to_of[way], one_hop[way], at]) for way in range(2)]

    def gn_add(part, begun):
        at = part_cols[part]
        for way in range(2):
            begun[0][way].wait_recv()
            gn_sums[way, :, at] = gn_ref[to_of[way], two_hops[way], at] + gn_held[way, 0, :, at]
            begun[1].append(gn_copy(part, way, 2, gn_sums.at[way, :, at]))

    def gn_total(part, begun):
        at = part_cols[part]
        for copy in begun[1]:
            copy.wait_recv()
        return jnp.concatenate(
            [gn_ref[g, two_hops[way], at] + gn_held[way, 2, :, at] + gn_held[1 - way, 1, :, at] for way in range(2)], axis=0)

    begun = [gn_begin(0)]

    def send_back(k, part, at):
        def start(i, m, j):
            dom_copy(
                back_ref.at[k, i, at], recv_ref.at[k, i, at], back_send, back_recv.at[part], z_plus[j] + spot_plus(m)).start()

        def own():
            pltpu.make_async_copy(back_ref.at[k, others, at], recv_ref.at[k, others, at], back_recv.at[part]).start()

        to_all(start, own)

    tail_hot = onehot(iota((slots, edges), 0) == slot[:, 0:edges])

    def pack_tails(k):
        back_ref[k] = dot_parts(tail_hot, parts(gt_ref[:, 128 * k : 128 * (k + 1)], 2)).reshape(peers, SLOTS, 128)

    pack_tails(0)
    gn_add(0, begun[0])
    begun.append(gn_begin(1))
    send_back(0, 0, low)

    spread = spread_matrix(128, 256)

    def remainders_back(values, at):
        count = values.shape[0]
        rest = sum(dot(p, spread, NN) for p in parts(values, 2))
        rest = jnp.where((iota((count, 256), 1) >> 4) == (slot_col[at] & 15), rest, 0.0)
        return dot_parts(onehot(iota((peers, count), 0) == (slot[:, at] >> 4)), parts(rest, 2))

    rest = remainders_back(gt_ref[:, MAIN:WIDE], slice(0, edges))
    line = iota((peers * 8, quarter), 0)
    neg_hot = onehot((line >> 3) * SLOTS + 8 + (line & 7) == slot[:, own])
    last = iota((peers, 8, 128), 1) == 7

    def pack_rest(k, grad_neg, rest):
        more = dot_parts(neg_hot, parts(grad_neg, 2)).reshape(peers, 8, 128)
        more = back_ref[k, :, 8:SLOTS, :] + more
        if k < 2:
            more = jnp.where(last, rest[:, 128 * k : 128 * (k + 1)][:, None, :], more)
        back_ref[k, :, 8:SLOTS, :] = more
        send_back(k, k + 1, high if k == 0 else all_rows)

    pack_rest(0, gn_total(0, begun[0]), rest)
    gn_add(1, begun[1])
    pack_tails(1)
    grad_neg = gn_total(1, begun[1])
    rest = rest + remainders_back(grad_neg[:, MAIN - 128 :], own)
    pack_rest(1, grad_neg[:, 0:128], rest)

    gr_parts = []
    for c in range(edges // SPAN):
        at = slice(c * SPAN, (c + 1) * SPAN)
        pos_coef, neg_coef = coefs[c]
        grad_query = pos_coef * got_ref[at] + lax.dot_general(
            neg_coef, neg_rows(c), NN, precision=HIGHEST, preferred_element_type=F32)
        gh_ref[at] = grad_query * rel_rows[at]
        hot = onehot(iota((groups, SPAN), 0) == rel_id[:, at])
        gr_parts.append(dot_parts(hot, parts(grad_query * head_emb[at], 3)))
    gr_ref[...] = sum(gr_parts)[:, None, :]

    slab_ref = et_ref
    piece = rows // n
    first_row = [128 * k for k in range(CHUNKS)]
    height = [128] * (CHUNKS - 1) + [width - 128 * (CHUNKS - 1)]

    def cols(j):
        return pl.ds(pl.multiple_of(j * piece, piece), piece)

    ring = {}

    def half(k, way, mine):
        h = height[k] // 2
        low = (way == 0) == mine
        return slice(first_row[k], first_row[k] + h) if low else slice(first_row[k] + h, first_row[k] + 2 * h)

    def send(k, way, step, src, dst):
        copy = pltpu.make_async_remote_copy(
            src, dst, ring_send.at[k, way, step], ring_recv.at[k, way, step],
            device_id={"rel": to_of[way]}, device_id_type=MESH)
        copy.start()
        ring[k, way, step] = copy

    def arrived(k, part, at):
        pltpu.make_async_copy(back_ref.at[k, :, at], recv_ref.at[k, :, at], back_recv.at[part]).wait()

    def scatter(k):
        if k == 0:
            arrived(0, 0, low)
            arrived(0, 1, high)
        else:
            arrived(k, k + 1, all_rows)
        values = [recv_ref[k].reshape(slots, 128).T, gh_ref[:, 128 * k : 128 * (k + 1)].T]
        vt = jnp.concatenate(values, axis=1)
        if k == CHUNKS - 1:
            rest = jnp.concatenate([recv_ref[0, :, SLOTS - 1, :], recv_ref[1, :, SLOTS - 1, :]], axis=1)
            rest = jnp.broadcast_to(rest[:, None, :], (peers, SLOTS, 256))
            own = (iota((peers, SLOTS, 256), 2) >> 4) == iota((peers, SLOTS, 256), 1)
            rest = jnp.where(own, rest, 0.0).reshape(slots, 256)
            rest = sum(dot(p, fold, NN) for p in parts(rest, 2))
            more = jnp.concatenate([rest.T[0:16], gh_ref[:, MAIN:WIDE].T[0:16]], axis=1)
            vt = jnp.concatenate([vt, more], axis=0)
        h = height[k]
        vt_ref[0:h], vt_ref[h : 2 * h] = parts(vt, 2)

        @pl.loop(0, n)
        def _(j):
            at = cols(j)
            both = dot(vt_ref[0 : 2 * h], oh_ref[:, at], NN)
            slab_ref[first_row[k] : first_row[k] + h, at] = both[0:h] + both[h : 2 * h]

    def begin(k):
        h = height[k] // 2
        for way in range(2):
            send(k, way, 0, slab_ref.at[half(k, way, True), cols(far)], held_ref.at[k, way, 0, 0:h])
        for way in range(2):
            send(k, way, 1, slab_ref.at[half(k, way, False), cols(to_of[way])], held_ref.at[k, way, 1, 0:h])

    def add(k):
        h = height[k] // 2
        for way in range(2):
            ring[k, way, 0].wait_recv()
            sums_ref[k, way, 0:h] = slab_ref[half(k, way, True), cols(to_of[way])] + held_ref[k, way, 0, 0:h]
            send(k, way, 2, sums_ref.at[k, way, 0:h], held_ref.at[k, way, 2, 0:h])

    def share(k):
        h = height[k] // 2
        for way in range(2):
            ring[k, way, 1].wait_recv()
            ring[k, way, 2].wait_recv()
        for way in range(2):
            at = half(k, way, True)
            out_ref[at, cols(g)] = slab_ref[at, cols(g)] + held_ref[k, way, 2, 0:h] + held_ref[k, 1 - way, 1, 0:h]
        for step, mine_too in ((3, True), (4, False)):
            for way in range(2):
                at = half(k, way, mine_too)
                send(k, way, step, out_ref.at[at, cols(g)], out_ref.at[at, cols(g)])

    def forward(k):
        for way in range(2):
            ring[k, way, 3].wait_recv()
            at = half(k, way, True)
            send(k, way, 5, out_ref.at[at, cols(back_of[way])], out_ref.at[at, cols(back_of[way])])

    scatter(0)
    begin(0)
    pack_tails(2)
    pack_rest(2, grad_neg[:, 128:256], rest)
    add(0)
    share(0)
    scatter(1)
    begin(1)

    def start_rel(i, m, j):
        to = z_plus[j] + spot_plus(m)
        dom_copy(gr_ref.at[to], gr_recv.at[i], gr_send, gr_got, to).start()

    to_all(start_rel, lambda: pltpu.make_async_copy(gr_ref.at[me], gr_recv.at[others], gr_got).start())
    forward(0)
    add(1)
    share(1)
    scatter(2)
    begin(2)
    forward(1)
    pltpu.make_async_copy(gr_ref, gr_recv, gr_got).wait()
    gr_sum[0] = jnp.sum(gr_recv[...], axis=0)

    def start_sum(i, m, j):
        dom_copy(gr_sum.at[0], rel_recv.at[me], ag_send, ag_recv, z_plus[j] + spot_plus(m)).start()

    to_all(start_sum, lambda: pltpu.make_async_copy(gr_sum.at[0], rel_recv.at[me], ag_recv).start())
    add(2)
    share(2)
    pltpu.make_async_copy(gr_ref, rel_recv, ag_recv).wait()
    rel_out[...] = rel_recv[:, 0, :][:, 0:width]
    forward(2)

    first = pl.ds(0, others)
    seven = pl.ds(0, 7)
    pltpu.make_async_copy(ids_ref.at[seven], ids_ref.at[seven], ids_send).wait()
    pltpu.make_async_copy(asked_ref.at[0:56], asked_ref.at[0:56], line_send).wait()
    pltpu.make_async_copy(served_ref.at[first], served_ref.at[first], serve_send).wait()
    pltpu.make_async_copy(gr_ref.at[first], gr_ref.at[first], gr_send).wait()
    pltpu.make_async_copy(gr_ref.at[first], gr_ref.at[first], ag_send).wait()
    for k in range(CHUNKS):
        pltpu.make_async_copy(back_ref.at[k, first], back_ref.at[k, first], back_send).wait()
    for copy in [*sent, *ring.values()]:
        copy.wait_send()
    for k in range(CHUNKS):
        for way in range(2):
            ring[k, way, 4].wait_recv()
            ring[k, way, 5].wait_recv()


def body(embeddings, rel_weight, head_row, rel_id, tail_owner, tail_row, neg_owner, neg_row):
    peers, n = lax.axis_size("dom"), lax.axis_size("rel")
    rows, width = embeddings.shape
    edges, negs = head_row.shape[0], neg_row.shape[0]
    groups = rel_weight.shape[0]
    quarter = negs // n
    lists = WIDE
    slots = peers * SLOTS
    tall = (width - 128 * (CHUNKS - 1)) // 2
    lists_of = (tail_row, head_row, rel_id, neg_row)
    ends = [sum(a.shape[0] for a in lists_of[: k + 1]) for k in range(len(lists_of))]
    joined = sum(jnp.pad(a, (end - a.shape[0], ends[-1] - end)) for a, end in zip(lists_of, ends, strict=True))
    V, DMA = pltpu.VMEM, pltpu.SemaphoreType.DMA
    vmem, in_hbm = pl.BlockSpec(memory_space=pltpu.VMEM), pl.BlockSpec(memory_space=pltpu.HBM)
    scratch = [
        V((groups, width), F32), V((width, rows), F32), V((WIDE, rows), BF16), V((WIDE, rows), BF16), V((WIDE, rows), BF16),
        V((slots + edges, rows), BF16), V((8, 1, 128), I32), V((8, 1, 128), I32), V((peers, 1, 128), I32),
        V((peers, SLOTS, MAIN), F32), V((peers, SLOTS, MAIN), F32), V((edges, WIDE), F32), V((n, quarter, WIDE), F32),
        V((edges, WIDE), F32), V((edges, WIDE), F32), V((edges, WIDE), F32), V((edges, WIDE), F32), V((edges, WIDE), F32),
        V((n, quarter, WIDE), F32), V((2, 3, quarter // 2, WIDE), F32), V((2, quarter // 2, WIDE), F32),
        V((CHUNKS, peers, SLOTS, 128), F32), V((CHUNKS, peers, SLOTS, 128), F32),
        V((4 * tall, slots + edges), BF16),
        V((CHUNKS, 2, 3, tall, rows // n), F32), V((CHUNKS, 2, tall, rows // n), F32),
        V((groups, 1, WIDE), F32), V((peers, 1, WIDE), F32), V((1, 1, WIDE), F32), V((groups, 1, WIDE), F32),
        DMA((2,)), DMA(()), DMA(()), DMA(()), DMA(()), DMA(()), DMA(()), DMA((8,)), DMA((n - 1,)), DMA((n - 1,)), DMA((2, 2, 3)), DMA((2, 2, 3)),
        DMA(()), DMA((CHUNKS + 1,)), DMA(()), DMA(()), DMA(()), DMA(()), DMA((CHUNKS, 2, 6)), DMA((CHUNKS, 2, 6)),
    ]
    total, relation = pl.pallas_call(
        kernel,
        out_shape=(jax.ShapeDtypeStruct((width, rows), F32), jax.ShapeDtypeStruct((groups, width), F32)),
        in_specs=[vmem, vmem, vmem, in_hbm, in_hbm],
        out_specs=(vmem, vmem),
        scratch_shapes=scratch,
        compiler_params=pltpu.CompilerParams(collective_id=0, has_side_effects=True, vmem_limit_bytes=48 << 20),
        cost_estimate=pl.CostEstimate(flops=int(3e10), bytes_accessed=7 << 20, transcendentals=0),
        name="ranking_gradients",
    )(joined, tail_owner.reshape(1, edges), neg_owner.reshape(1, negs), rel_weight, embeddings.T)
    return (total.T, relation)


def solution(mesh):
    return jax.shard_map(
        body,
        mesh=mesh,
        in_specs=(
            P("dom", None),
            P("rel", None),
            P(("dom", "rel")),
            P(("dom", "rel")),
            P(("dom", "rel"), None),
            P(("dom", "rel")),
            P("dom", None),
            P("dom"),
        ),
        out_specs=(P("dom", None), P("rel", None)),
        check_vma=False,
    )
```

```python
import jax
import jax.numpy as jnp
from jax import lax
from jax.experimental import pallas as pl
from jax.experimental.pallas import tpu as pltpu
from jax.sharding import PartitionSpec as P

SPAN = 128
MAIN = 384
WIDE = 512
SLOTS = 16
CAP_T = 12
F32, BF16, I32 = jnp.float32, jnp.bfloat16, jnp.int32
MESH = pl.DeviceIdType.MESH
HIGHEST = lax.Precision.HIGHEST
NN = (((1,), (0,)), ((), ()))
NT = (((1,), (1,)), ((), ()))
TN = (((0,), (0,)), ((), ()))


def iota(shape, dim):
    return lax.broadcasted_iota(I32, shape, dim)


def parts(x, count):
    out = []
    for _ in range(count - 1):
        hi = x.astype(BF16)
        out.append(hi)
        x = x - hi.astype(F32)
    return out + [x.astype(BF16)]


def dot(a, b, dims):
    return lax.dot_general(a, b, dims, preferred_element_type=F32)


def dot_parts(onehot, values, dims=NN):
    total = dot(onehot, values[0], dims)
    for v in values[1:]:
        total = total + dot(onehot, v, dims)
    return total


def column(row):
    n = row.shape[1]
    return jnp.broadcast_to(row.astype(F32), (8, n)).T[:, 0:1].astype(I32)


def onehot(mask):
    return jnp.where(mask, 1.0, 0.0).astype(BF16)


def fold_matrix(rows, cols):
    l, m = iota((rows, cols), 0), iota((rows, cols), 1)
    return onehot((l & 15) == m)


def spread_matrix(rows, cols):
    m, l = iota((rows, cols), 0), iota((rows, cols), 1)
    return onehot((l & 15) == m)


DZ = (4, 5, 3, 6, 2, 7, 1, 0)
CHUNKS = 3


def id_column(ids, first):
    p = ids.shape[0]
    spread = jnp.broadcast_to(ids.astype(F32), (p, SLOTS, 128))
    own = iota((p, SLOTS, 128), 1) + first == iota((p, SLOTS, 128), 2)
    return jnp.sum(jnp.where(own, spread, 0.0), axis=2, keepdims=True).reshape(p * SLOTS, 1).astype(I32)


def kernel(
    lists_ref, towner_ref, nowner_ref, rel_in, et_in,
    out_ref, rel_out,
    rel_ref, et_ref, hi_ref, mid_ref, lo_ref, oh_ref, ids_ref, line_ref, asked_ref, served_ref, fetched_ref, got_ref, negs_ref,
    head_emb, rel_rows, query_ref, gh_ref, gt_ref, gn_ref, gn_held, gn_sums, back_ref, recv_ref, vt_ref, held_ref, sums_ref,
    gr_ref, gr_recv, gr_sum, rel_recv, score_ref, tail_hot, neg_hot,
    load_sem, ids_send, ids_recv, line_send, line_recv, serve_send, high_recv, serve_recv, neg_send, neg_recv, gn_send, gn_recv,
    back_send, back_recv, gr_send, gr_got, ag_send, ag_recv, ring_send, ring_recv,
):
    peers = served_ref.shape[0]
    others = peers - 1
    n = negs_ref.shape[0]
    me, g = lax.axis_index("dom"), lax.axis_index("rel")
    edges = head_emb.shape[0]
    negs = nowner_ref.shape[1]
    quarter = negs // n
    lists = WIDE
    slots = peers * SLOTS
    width, rows = et_ref.shape
    tables = (hi_ref, mid_ref, lo_ref)
    z, y, core = lax.div(me, 8), lax.rem(lax.div(me, 2), 4), lax.rem(me, 2)
    spot = lax.rem(me, 8)
    z_plus = [lax.rem(z + d, 8) * 8 for d in DZ]
    z_minus = [lax.rem(z + 8 - d, 8) * 8 for d in DZ]

    def spot_plus(m):
        q = 7 - m
        return lax.rem(y + lax.div(q, 2), 4) * 2 + lax.rem(core + lax.rem(q, 2), 2)

    def spot_minus(m):
        q = 7 - m
        return lax.rem(y + 4 - lax.div(q, 2), 4) * 2 + lax.rem(core + lax.rem(q, 2), 2)

    def dom_copy(src, dst, send, recv, device):
        return pltpu.make_async_remote_copy(
            src, dst, send, recv, device_id={"dom": device}, device_id_type=MESH)

    low, high, all_rows = pl.ds(0, 8), pl.ds(8, 8), pl.ds(0, SLOTS)

    def to_all(start, own):
        @pl.loop(0, 8)
        def _(m):
            for j in range(7):
                start(m * 8 + j, m, j)

            @pl.when(m < 7)
            def _():
                start(m * 8 + 7, m, 7)

        own()

    loads = [pltpu.make_async_copy(et_in, et_ref, load_sem.at[0]), pltpu.make_async_copy(rel_in, rel_ref, load_sem.at[1])]
    for load in loads:
        load.start()
    barrier = pltpu.get_barrier_semaphore()
    for j in range(7):
        pl.semaphore_signal(barrier, inc=1, device_id={"dom": z_plus[j] + spot}, device_id_type=MESH)
    for m in range(7):
        pl.semaphore_signal(barrier, inc=1, device_id={"dom": z * 8 + spot_plus(m)}, device_id_type=MESH)
    for k in range(1, n):
        pl.semaphore_signal(barrier, inc=1, device_id={"rel": lax.rem(g + k, n)}, device_id_type=MESH)

    tail_row, head_row, rel_id = (lists_ref[edges * k : edges * (k + 1)][None, :] for k in range(3))
    neg_row = lists_ref[3 * edges : 3 * edges + negs][None, :]

    def mine(row):
        return sum(jnp.where(g == q, row[:, quarter * q : quarter * (q + 1)], 0) for q in range(n))

    spare = jnp.zeros((1, lists - edges - quarter), I32)
    owner = jnp.concatenate([towner_ref[...], mine(nowner_ref[...]) + 64, spare + 255], axis=1)
    asked_rows = jnp.concatenate([tail_row, mine(neg_row), spare], axis=1)
    same = column(owner) == owner
    earlier = iota((lists, lists), 0) < iota((lists, lists), 1)
    position = jnp.sum(jnp.where(same & earlier, 1.0, 0.0), axis=0, keepdims=True).astype(I32)
    negative, valid = owner >= 64, owner < 128
    position = jnp.where(negative, position + CAP_T, position)
    owner = owner & 63
    dz = ((owner >> 3) - z + 8) & 7
    step_z = sum(jnp.where(dz == d, j, 0) for j, d in enumerate(DZ))
    dy, dc = (((owner >> 1) & 3) - y + 4) & 3, ((owner & 1) - core + 2) & 1
    slot = jnp.where(valid, ((7 - dy * 2 - dc) * 8 + step_z) * SLOTS + position, -1)
    left = jnp.where((iota((8, lists), 0) == step_z) & valid, (asked_rows + 1).astype(F32), 0.0)
    right = jnp.where(iota((128, lists), 0) == (owner & 7) * SLOTS + position, 1.0, 0.0)
    ids = lax.dot_general(left, right, NT, precision=HIGHEST, preferred_element_type=F32)
    ids_ref[...] = ((ids + 0.5).astype(I32) - 1)[:, None, :]

    pl.semaphore_wait(barrier, 14 + n - 1)
    for j in range(7):
        dom_copy(ids_ref.at[j], line_ref.at[j], ids_send, ids_recv, z_plus[j] + spot).start()
    pltpu.make_async_copy(ids_ref.at[7], line_ref.at[7], ids_recv).start()
    for load in loads:
        load.wait()

    def split(start, stop):
        @pl.loop(start, stop)
        def _(i):
            at = pl.multiple_of(i * 16, 16)
            for t, v in zip(tables, parts(et_ref[pl.ds(at, 16), :], 3), strict=True):
                t[pl.ds(at, 16), :] = v

    split(0, width // 32)
    pltpu.make_async_copy(ids_ref, line_ref, ids_recv).wait()
    for m in range(7):
        dom_copy(line_ref, asked_ref.at[8 * m : 8 * m + 8], line_send, line_recv, z * 8 + spot_plus(m)).start()
    pltpu.make_async_copy(line_ref, asked_ref.at[56:64], line_recv).start()

    split(width // 32, width // 16)
    for t in tables:
        for k in range(1, 8):
            t[MAIN + 16 * k : MAIN + 16 * (k + 1), :] = t[MAIN : MAIN + 16, :]

    pltpu.make_async_copy(asked_ref, asked_ref, line_recv).wait()

    @pl.loop(0, 8)
    def _(m):
        at = pl.multiple_of(m * 8, 8)
        col = id_column(asked_ref[pl.ds(at, 8)], spot * SLOTS)
        hot = onehot(iota((8 * SLOTS, rows), 1) == col)
        oh_ref[pl.ds(pl.multiple_of(m * 8 * SLOTS, 8 * SLOTS), 8 * SLOTS), :] = hot
        got = dot_parts(hot, [t[...] for t in tables], NT)
        place = iota((8, SLOTS, 128), 1)
        lane = iota((8, SLOTS, 128), 2)
        rest = got[:, MAIN:].reshape(8, SLOTS, 128)
        rest = jnp.where((lane >> 4) == (place & 7), rest, 0.0)
        one = jnp.sum(jnp.where(place < 8, rest, 0.0), axis=1, keepdims=True)
        two = jnp.sum(jnp.where(place < 8, 0.0, rest), axis=1, keepdims=True)
        for k, part in enumerate((one, two, jnp.zeros_like(one))):
            main = got[:, 128 * k : 128 * (k + 1)].reshape(8, SLOTS, 128)
            served_ref[pl.ds(at, 8), :, 128 * k : 128 * (k + 1)] = jnp.where(place == SLOTS - 1, part, main)
        to = spot_minus(m)

        def start(i, j):
            dom_copy(served_ref.at[i, high], fetched_ref.at[i, high], serve_send, high_recv, z_minus[j] + to).start()

        for j in range(7):
            start(m * 8 + j, j)

        @pl.when(m < 7)
        def _():
            start(m * 8 + 7, 7)

    pltpu.make_async_copy(served_ref.at[others, high], fetched_ref.at[others, high], high_recv).start()

    def start_low(i, m, j):
        dom_copy(
            served_ref.at[i, low], fetched_ref.at[i, low], serve_send, serve_recv.at[m], z_minus[j] + spot_minus(m)).start()

    to_all(start_low, lambda: pltpu.make_async_copy(
        served_ref.at[others, low], fetched_ref.at[others, low], serve_recv.at[7]).start())

    hot = onehot(iota((edges, rows), 1) == column(head_row))
    oh_ref[slots:, :] = hot
    got = dot_parts(hot, [t[...] for t in tables], NT)
    head_emb[:, 0:MAIN] = got[:, 0:MAIN]
    head_emb[:, MAIN:WIDE] = jnp.where(iota((edges, 128), 1) < width - MAIN, got[:, MAIN:WIDE], 0.0)
    groups = rel_ref.shape[0]
    hot = onehot(iota((edges, groups), 1) == column(rel_id))
    rel_rows[:, 0:width] = dot_parts(hot, parts(rel_ref[...], 3))
    rel_rows[:, width:WIDE] = jnp.zeros((edges, WIDE - width), F32)
    query_ref[...] = head_emb[...] * rel_rows[...]

    slot_col = column(slot)
    fold = fold_matrix(256, 128)
    pltpu.make_async_copy(served_ref.at[:, high], fetched_ref.at[:, high], high_recv).wait()
    packed = parts(fetched_ref[:, SLOTS - 1, 0:256], 3)

    def remainders(at):
        where = slot_col[at]
        count = where.shape[0]
        rest = dot_parts(onehot(iota((count, peers), 1) == (where >> 4)), packed)
        rest = jnp.where((iota((count, 256), 1) >> 4) == (where & 15), rest, 0.0)
        return sum(dot(p, fold, NN) for p in parts(rest, 3))

    own = slice(edges, edges + quarter)
    line = iota((quarter, peers * 8), 1)
    hot = onehot((line >> 3) * SLOTS + 8 + (line & 7) == slot_col[own])
    negs_ref[g, :, 0:MAIN] = dot_parts(hot, parts(fetched_ref[:, 8:SLOTS, :].reshape(peers * 8, MAIN), 3))
    negs_ref[g, :, MAIN:WIDE] = remainders(own)

    def rel_copy(src, dst, send, recv, k):
        return pltpu.make_async_remote_copy(
            src, dst, send, recv, device_id={"rel": lax.rem(g + k, n)}, device_id_type=MESH)

    copies = [rel_copy(negs_ref.at[g], negs_ref.at[g], neg_send.at[k - 1], neg_recv.at[k - 1], k) for k in range(1, n)]
    for copy in copies:
        copy.start()
    tails = slice(0, edges)
    got_ref[:, 0:MAIN] = jnp.zeros((edges, MAIN), F32)
    got_ref[:, MAIN:WIDE] = remainders(tails)

    def unpack(b):
        at = pl.ds(pl.multiple_of(b * 16, 16), 16)
        for k in range(2):
            part = pl.ds(pl.multiple_of(b * 16, 16) + 8 * k, 8)
            pltpu.make_async_copy(served_ref.at[part, low], fetched_ref.at[part, low], serve_recv.at[2 * b + k]).wait()
        hot = onehot(iota((edges, 16 * SLOTS), 1) + b * (16 * SLOTS) == slot_col[tails])
        got_ref[:, 0:MAIN] += dot_parts(hot, parts(fetched_ref[at].reshape(16 * SLOTS, MAIN), 3))

    pl.loop(0, 3)(unpack)

    for copy in copies:
        copy.wait_recv()
    sent = list(copies)

    def neg_rows(c):
        return negs_ref[...].reshape(negs, WIDE)[c * SPAN : (c + 1) * SPAN]

    for c in range(edges // SPAN):
        at = slice(c * SPAN, (c + 1) * SPAN)
        score_ref[at] = lax.dot_general(query_ref[at], neg_rows(c), NT, precision=HIGHEST, preferred_element_type=F32)
    tail_hot[...] = onehot(iota((slots, edges), 0) == slot[:, 0:edges])
    line = iota((peers * 8, quarter), 0)
    neg_hot[...] = onehot((line >> 3) * SLOTS + 8 + (line & 7) == slot[:, own])
    unpack(3)

    positive = jnp.sum(query_ref[...] * got_ref[...], axis=1, keepdims=True)
    scores = score_ref[...]
    row_max = jnp.maximum(positive, jnp.max(scores, axis=1, keepdims=True))
    pos_exp = jnp.exp(positive - row_max)
    neg_exp = jnp.exp(scores - row_max)
    total = pos_exp + jnp.sum(neg_exp, axis=1, keepdims=True)
    pos_coef = pos_exp / total - 1.0
    neg_coef = neg_exp / total
    gt_ref[...] = pos_coef * query_ref[...]
    for c in range(edges // SPAN):
        at = slice(c * SPAN, (c + 1) * SPAN)
        grad_neg = lax.dot_general(neg_coef[at].T, query_ref[at], NN, precision=HIGHEST, preferred_element_type=F32)
        first = c * SPAN
        while first < (c + 1) * SPAN:
            q, inside = divmod(first, quarter)
            count = min(quarter - inside, (c + 1) * SPAN - first)
            gn_ref[q, inside : inside + count] = grad_neg[first - c * SPAN : first - c * SPAN + count]
            first += count

    right_hand, left_hand, far = lax.rem(g + 1, n), lax.rem(g + 3, n), lax.rem(g + 2, n)
    to_of, back_of = (right_hand, left_hand), (left_hand, right_hand)
    top, bottom = slice(0, quarter // 2), slice(quarter // 2, quarter)
    two_hops, one_hop = (top, bottom), (bottom, top)

    part_cols = (slice(0, 128), slice(128, WIDE))

    def gn_copy(part, way, step, src):
        copy = pltpu.make_async_remote_copy(
            src, gn_held.at[way, step, :, part_cols[part]], gn_send.at[part, way, step], gn_recv.at[part, way, step],
            device_id={"rel": to_of[way]}, device_id_type=MESH)
        copy.start()
        sent.append(copy)
        return copy

    def gn_begin(part):
        at = part_cols[part]
        two = [gn_copy(part, way, 0, gn_ref.at[far, two_hops[way], at]) for way in range(2)]
        return two, [gn_copy(part, way, 1, gn_ref.at[to_of[way], one_hop[way], at]) for way in range(2)]

    def gn_add(part, begun):
        at = part_cols[part]
        for way in range(2):
            begun[0][way].wait_recv()
            gn_sums[way, :, at] = gn_ref[to_of[way], two_hops[way], at] + gn_held[way, 0, :, at]
            begun[1].append(gn_copy(part, way, 2, gn_sums.at[way, :, at]))

    def gn_total(part, begun):
        at = part_cols[part]
        for copy in begun[1]:
            copy.wait_recv()
        return jnp.concatenate(
            [gn_ref[g, two_hops[way], at] + gn_held[way, 2, :, at] + gn_held[1 - way, 1, :, at] for way in range(2)], axis=0)

    begun = [gn_begin(0)]

    def send_back(k, part, at):
        def start(i, m, j):
            dom_copy(
                back_ref.at[k, i, at], recv_ref.at[k, i, at], back_send, back_recv.at[part], z_plus[j] + spot_plus(m)).start()

        def own():
            pltpu.make_async_copy(back_ref.at[k, others, at], recv_ref.at[k, others, at], back_recv.at[part]).start()

        to_all(start, own)

    def pack_tails(k):
        back_ref[k] = dot_parts(tail_hot[...], parts(gt_ref[:, 128 * k : 128 * (k + 1)], 2)).reshape(peers, SLOTS, 128)

    pack_tails(0)
    send_back(0, 0, low)
    gn_add(0, begun[0])
    begun.append(gn_begin(1))

    spread = spread_matrix(128, 256)

    def remainders_back(values, at):
        count = values.shape[0]
        rest = sum(dot(p, spread, NN) for p in parts(values, 2))
        rest = jnp.where((iota((count, 256), 1) >> 4) == (slot_col[at] & 15), rest, 0.0)
        return dot_parts(onehot(iota((peers, count), 0) == (slot[:, at] >> 4)), parts(rest, 2))

    rest = remainders_back(gt_ref[:, MAIN:WIDE], slice(0, edges))
    last = iota((peers, 8, 128), 1) == 7

    def pack_rest(k, grad_neg, rest):
        more = dot_parts(neg_hot[...], parts(grad_neg, 2)).reshape(peers, 8, 128)
        more = back_ref[k, :, 8:SLOTS, :] + more
        if k < 2:
            more = jnp.where(last, rest[:, 128 * k : 128 * (k + 1)][:, None, :], more)
        back_ref[k, :, 8:SLOTS, :] = more
        send_back(k, k + 1, high if k == 0 else all_rows)

    pack_rest(0, gn_total(0, begun[0]), rest)
    gn_add(1, begun[1])
    pack_tails(1)
    grad_neg = gn_total(1, begun[1])
    rest = rest + remainders_back(grad_neg[:, MAIN - 128 :], own)
    pack_rest(1, grad_neg[:, 0:128], rest)

    gr_parts = []
    for c in range(edges // SPAN):
        at = slice(c * SPAN, (c + 1) * SPAN)
        grad_query = pos_coef[at] * got_ref[at] + lax.dot_general(
            neg_coef[at], neg_rows(c), NN, precision=HIGHEST, preferred_element_type=F32)
        gh_ref[at] = grad_query * rel_rows[at]
        hot = onehot(iota((groups, SPAN), 0) == rel_id[:, at])
        gr_parts.append(dot_parts(hot, parts(grad_query * head_emb[at], 3)))
    gr_ref[...] = sum(gr_parts)[:, None, :]

    slab_ref = et_ref
    piece = rows // n
    first_row = [128 * k for k in range(CHUNKS)]
    height = [128] * (CHUNKS - 1) + [width - 128 * (CHUNKS - 1)]

    def cols(j):
        return pl.ds(pl.multiple_of(j * piece, piece), piece)

    ring = {}

    def half(k, way, mine):
        h = height[k] // 2
        low = (way == 0) == mine
        return slice(first_row[k], first_row[k] + h) if low else slice(first_row[k] + h, first_row[k] + 2 * h)

    def send(k, way, step, src, dst):
        copy = pltpu.make_async_remote_copy(
            src, dst, ring_send.at[k, way, step], ring_recv.at[k, way, step],
            device_id={"rel": to_of[way]}, device_id_type=MESH)
        copy.start()
        ring[k, way, step] = copy

    def arrived(k, part, at):
        pltpu.make_async_copy(back_ref.at[k, :, at], recv_ref.at[k, :, at], back_recv.at[part]).wait()

    def scatter(k):
        if k == 0:
            arrived(0, 0, low)
            arrived(0, 1, high)
        else:
            arrived(k, k + 1, all_rows)
        values = [recv_ref[k].reshape(slots, 128).T, gh_ref[:, 128 * k : 128 * (k + 1)].T]
        vt = jnp.concatenate(values, axis=1)
        if k == CHUNKS - 1:
            rest = jnp.concatenate([recv_ref[0, :, SLOTS - 1, :], recv_ref[1, :, SLOTS - 1, :]], axis=1)
            rest = jnp.broadcast_to(rest[:, None, :], (peers, SLOTS, 256))
            own = (iota((peers, SLOTS, 256), 2) >> 4) == iota((peers, SLOTS, 256), 1)
            rest = jnp.where(own, rest, 0.0).reshape(slots, 256)
            rest = sum(dot(p, fold, NN) for p in parts(rest, 2))
            more = jnp.concatenate([rest.T[0:16], gh_ref[:, MAIN:WIDE].T[0:16]], axis=1)
            vt = jnp.concatenate([vt, more], axis=0)
        h = height[k]
        vt_ref[0:h], vt_ref[h : 2 * h] = parts(vt, 2)

        @pl.loop(0, n)
        def _(j):
            at = cols(j)
            both = dot(vt_ref[0 : 2 * h], oh_ref[:, at], NN)
            slab_ref[first_row[k] : first_row[k] + h, at] = both[0:h] + both[h : 2 * h]

    def begin(k):
        h = height[k] // 2
        for way in range(2):
            send(k, way, 0, slab_ref.at[half(k, way, True), cols(far)], held_ref.at[k, way, 0, 0:h])
        for way in range(2):
            send(k, way, 1, slab_ref.at[half(k, way, False), cols(to_of[way])], held_ref.at[k, way, 1, 0:h])

    def add(k):
        h = height[k] // 2
        for way in range(2):
            ring[k, way, 0].wait_recv()
            sums_ref[k, way, 0:h] = slab_ref[half(k, way, True), cols(to_of[way])] + held_ref[k, way, 0, 0:h]
            send(k, way, 2, sums_ref.at[k, way, 0:h], held_ref.at[k, way, 2, 0:h])

    def share(k):
        h = height[k] // 2
        for way in range(2):
            ring[k, way, 1].wait_recv()
            ring[k, way, 2].wait_recv()
        for way in range(2):
            at = half(k, way, True)
            out_ref[at, cols(g)] = slab_ref[at, cols(g)] + held_ref[k, way, 2, 0:h] + held_ref[k, 1 - way, 1, 0:h]
        for step, mine_too in ((3, True), (4, False)):
            for way in range(2):
                at = half(k, way, mine_too)
                send(k, way, step, out_ref.at[at, cols(g)], out_ref.at[at, cols(g)])

    def forward(k):
        for way in range(2):
            ring[k, way, 3].wait_recv()
            at = half(k, way, True)
            send(k, way, 5, out_ref.at[at, cols(back_of[way])], out_ref.at[at, cols(back_of[way])])

    scatter(0)
    begin(0)
    pack_tails(2)
    pack_rest(2, grad_neg[:, 128:256], rest)
    add(0)
    share(0)
    scatter(1)
    begin(1)

    def start_rel(i, m, j):
        to = z_plus[j] + spot_plus(m)
        dom_copy(gr_ref.at[to], gr_recv.at[i], gr_send, gr_got, to).start()

    to_all(start_rel, lambda: pltpu.make_async_copy(gr_ref.at[me], gr_recv.at[others], gr_got).start())
    forward(0)
    add(1)
    share(1)
    scatter(2)
    begin(2)
    forward(1)
    pltpu.make_async_copy(gr_ref, gr_recv, gr_got).wait()
    gr_sum[0] = jnp.sum(gr_recv[...], axis=0)

    def start_sum(i, m, j):
        dom_copy(gr_sum.at[0], rel_recv.at[me], ag_send, ag_recv, z_plus[j] + spot_plus(m)).start()

    to_all(start_sum, lambda: pltpu.make_async_copy(gr_sum.at[0], rel_recv.at[me], ag_recv).start())
    add(2)
    share(2)
    pltpu.make_async_copy(gr_ref, rel_recv, ag_recv).wait()
    rel_out[...] = rel_recv[:, 0, :][:, 0:width]
    forward(2)

    first = pl.ds(0, others)
    seven = pl.ds(0, 7)
    pltpu.make_async_copy(ids_ref.at[seven], ids_ref.at[seven], ids_send).wait()
    pltpu.make_async_copy(asked_ref.at[0:56], asked_ref.at[0:56], line_send).wait()
    pltpu.make_async_copy(served_ref.at[first], served_ref.at[first], serve_send).wait()
    pltpu.make_async_copy(gr_ref.at[first], gr_ref.at[first], gr_send).wait()
    pltpu.make_async_copy(gr_ref.at[first], gr_ref.at[first], ag_send).wait()
    for k in range(CHUNKS):
        pltpu.make_async_copy(back_ref.at[k, first], back_ref.at[k, first], back_send).wait()
    for copy in [*sent, *ring.values()]:
        copy.wait_send()
    for k in range(CHUNKS):
        for way in range(2):
            ring[k, way, 4].wait_recv()
            ring[k, way, 5].wait_recv()


def body(embeddings, rel_weight, head_row, rel_id, tail_owner, tail_row, neg_owner, neg_row):
    peers, n = lax.axis_size("dom"), lax.axis_size("rel")
    rows, width = embeddings.shape
    edges, negs = head_row.shape[0], neg_row.shape[0]
    groups = rel_weight.shape[0]
    quarter = negs // n
    lists = WIDE
    slots = peers * SLOTS
    tall = (width - 128 * (CHUNKS - 1)) // 2
    lists_of = (tail_row, head_row, rel_id, neg_row)
    ends = [sum(a.shape[0] for a in lists_of[: k + 1]) for k in range(len(lists_of))]
    joined = sum(jnp.pad(a, (end - a.shape[0], ends[-1] - end)) for a, end in zip(lists_of, ends, strict=True))
    V, DMA = pltpu.VMEM, pltpu.SemaphoreType.DMA
    vmem, in_hbm = pl.BlockSpec(memory_space=pltpu.VMEM), pl.BlockSpec(memory_space=pltpu.HBM)
    scratch = [
        V((groups, width), F32), V((width, rows), F32), V((WIDE, rows), BF16), V((WIDE, rows), BF16), V((WIDE, rows), BF16),
        V((slots + edges, rows), BF16), V((8, 1, 128), I32), V((8, 1, 128), I32), V((peers, 1, 128), I32),
        V((peers, SLOTS, MAIN), F32), V((peers, SLOTS, MAIN), F32), V((edges, WIDE), F32), V((n, quarter, WIDE), F32),
        V((edges, WIDE), F32), V((edges, WIDE), F32), V((edges, WIDE), F32), V((edges, WIDE), F32), V((edges, WIDE), F32),
        V((n, quarter, WIDE), F32), V((2, 3, quarter // 2, WIDE), F32), V((2, quarter // 2, WIDE), F32),
        V((CHUNKS, peers, SLOTS, 128), F32), V((CHUNKS, peers, SLOTS, 128), F32),
        V((4 * tall, slots + edges), BF16),
        V((CHUNKS, 2, 3, tall, rows // n), F32), V((CHUNKS, 2, tall, rows // n), F32),
        V((groups, 1, WIDE), F32), V((peers, 1, WIDE), F32), V((1, 1, WIDE), F32), V((groups, 1, WIDE), F32),
        V((edges, SPAN), F32), V((slots, edges), BF16), V((peers * 8, quarter), BF16),
        DMA((2,)), DMA(()), DMA(()), DMA(()), DMA(()), DMA(()), DMA(()), DMA((8,)), DMA((n - 1,)), DMA((n - 1,)), DMA((2, 2, 3)), DMA((2, 2, 3)),
        DMA(()), DMA((CHUNKS + 1,)), DMA(()), DMA(()), DMA(()), DMA(()), DMA((CHUNKS, 2, 6)), DMA((CHUNKS, 2, 6)),
    ]
    total, relation = pl.pallas_call(
        kernel,
        out_shape=(jax.ShapeDtypeStruct((width, rows), F32), jax.ShapeDtypeStruct((groups, width), F32)),
        in_specs=[vmem, vmem, vmem, in_hbm, in_hbm],
        out_specs=(vmem, vmem),
        scratch_shapes=scratch,
        compiler_params=pltpu.CompilerParams(collective_id=0, has_side_effects=True, vmem_limit_bytes=48 << 20),
        cost_estimate=pl.CostEstimate(flops=int(3e10), bytes_accessed=7 << 20, transcendentals=0),
        name="ranking_gradients",
    )(joined, tail_owner.reshape(1, edges), neg_owner.reshape(1, negs), rel_weight, embeddings.T)
    return (total.T, relation)


def solution(mesh):
    return jax.shard_map(
        body,
        mesh=mesh,
        in_specs=(
            P("dom", None),
            P("rel", None),
            P(("dom", "rel")),
            P(("dom", "rel")),
            P(("dom", "rel"), None),
            P(("dom", "rel")),
            P("dom", None),
            P("dom"),
        ),
        out_specs=(P("dom", None), P("rel", None)),
        check_vma=False,
    )
```

```python
import jax
import jax.numpy as jnp
from jax import lax
from jax.experimental import pallas as pl
from jax.experimental.pallas import tpu as pltpu
from jax.sharding import PartitionSpec as P

SPAN = 128
MAIN = 384
WIDE = 512
SLOTS = 16
CAP_T = 12
F32, BF16, I32 = jnp.float32, jnp.bfloat16, jnp.int32
MESH = pl.DeviceIdType.MESH
HIGHEST = lax.Precision.HIGHEST
NN = (((1,), (0,)), ((), ()))
NT = (((1,), (1,)), ((), ()))
TN = (((0,), (0,)), ((), ()))


def iota(shape, dim):
    return lax.broadcasted_iota(I32, shape, dim)


def parts(x, count):
    out = []
    for _ in range(count - 1):
        hi = x.astype(BF16)
        out.append(hi)
        x = x - hi.astype(F32)
    return out + [x.astype(BF16)]


def dot(a, b, dims):
    return lax.dot_general(a, b, dims, preferred_element_type=F32)


def dot_parts(onehot, values, dims=NN):
    total = dot(onehot, values[0], dims)
    for v in values[1:]:
        total = total + dot(onehot, v, dims)
    return total


def column(row):
    n = row.shape[1]
    return jnp.broadcast_to(row.astype(F32), (8, n)).T[:, 0:1].astype(I32)


def onehot(mask):
    return jnp.where(mask, 1.0, 0.0).astype(BF16)


def fold_matrix(rows, cols):
    l, m = iota((rows, cols), 0), iota((rows, cols), 1)
    return onehot((l & 15) == m)


def spread_matrix(rows, cols):
    m, l = iota((rows, cols), 0), iota((rows, cols), 1)
    return onehot((l & 15) == m)


DZ = (4, 5, 3, 6, 2, 7, 1, 0)
CHUNKS = 3


def id_column(ids, first):
    p = ids.shape[0]
    spread = jnp.broadcast_to(ids.astype(F32), (p, SLOTS, 128))
    own = iota((p, SLOTS, 128), 1) + first == iota((p, SLOTS, 128), 2)
    return jnp.sum(jnp.where(own, spread, 0.0), axis=2, keepdims=True).reshape(p * SLOTS, 1).astype(I32)


def kernel(
    lists_ref, towner_ref, nowner_ref, rel_in, et_in,
    out_ref, rel_out,
    rel_ref, et_ref, hi_ref, mid_ref, lo_ref, oh_ref, ids_ref, line_ref, asked_ref, served_ref, fetched_ref, got_ref, negs_ref,
    head_emb, rel_rows, query_ref, gh_ref, gt_ref, gn_ref, gn_held, gn_sums, back_ref, recv_ref, vt_ref, held_ref, sums_ref,
    gr_ref, gr_recv, gr_sum, rel_recv, score_ref, tail_hot, neg_hot,
    load_sem, ids_send, ids_recv, line_send, line_recv, serve_send, high_recv, serve_recv, neg_send, neg_recv, gn_send, gn_recv,
    back_send, back_recv, gr_send, gr_got, ag_send, ag_recv, ring_send, ring_recv,
):
    peers = served_ref.shape[0]
    others = peers - 1
    n = negs_ref.shape[0]
    me, g = lax.axis_index("dom"), lax.axis_index("rel")
    edges = head_emb.shape[0]
    negs = nowner_ref.shape[1]
    quarter = negs // n
    lists = WIDE
    slots = peers * SLOTS
    width, rows = et_ref.shape
    tables = (hi_ref, mid_ref, lo_ref)
    z, y, core = lax.div(me, 8), lax.rem(lax.div(me, 2), 4), lax.rem(me, 2)
    spot = lax.rem(me, 8)
    z_plus = [lax.rem(z + d, 8) * 8 for d in DZ]
    z_minus = [lax.rem(z + 8 - d, 8) * 8 for d in DZ]

    def spot_plus(m):
        q = 7 - m
        return lax.rem(y + lax.div(q, 2), 4) * 2 + lax.rem(core + lax.rem(q, 2), 2)

    def spot_minus(m):
        q = 7 - m
        return lax.rem(y + 4 - lax.div(q, 2), 4) * 2 + lax.rem(core + lax.rem(q, 2), 2)

    def dom_copy(src, dst, send, recv, device):
        return pltpu.make_async_remote_copy(
            src, dst, send, recv, device_id={"dom": device}, device_id_type=MESH)

    low, high, all_rows = pl.ds(0, 8), pl.ds(8, 8), pl.ds(0, SLOTS)

    def to_all(start, own):
        @pl.loop(0, 8)
        def _(m):
            for j in range(7):
                start(m * 8 + j, m, j)

            @pl.when(m < 7)
            def _():
                start(m * 8 + 7, m, 7)

        own()

    loads = [pltpu.make_async_copy(et_in, et_ref, load_sem.at[0]), pltpu.make_async_copy(rel_in, rel_ref, load_sem.at[1])]
    for load in loads:
        load.start()
    barrier = pltpu.get_barrier_semaphore()
    for j in range(7):
        pl.semaphore_signal(barrier, inc=1, device_id={"dom": z_plus[j] + spot}, device_id_type=MESH)
    for m in range(7):
        pl.semaphore_signal(barrier, inc=1, device_id={"dom": z * 8 + spot_plus(m)}, device_id_type=MESH)
    for k in range(1, n):
        pl.semaphore_signal(barrier, inc=1, device_id={"rel": lax.rem(g + k, n)}, device_id_type=MESH)

    tail_row, head_row, rel_id = (lists_ref[edges * k : edges * (k + 1)][None, :] for k in range(3))
    neg_row = lists_ref[3 * edges : 3 * edges + negs][None, :]

    def mine(row):
        return sum(jnp.where(g == q, row[:, quarter * q : quarter * (q + 1)], 0) for q in range(n))

    spare = jnp.zeros((1, lists - edges - quarter), I32)
    owner = jnp.concatenate([towner_ref[...], mine(nowner_ref[...]) + 64, spare + 255], axis=1)
    asked_rows = jnp.concatenate([tail_row, mine(neg_row), spare], axis=1)
    same = column(owner) == owner
    earlier = iota((lists, lists), 0) < iota((lists, lists), 1)
    position = jnp.sum(jnp.where(same & earlier, 1.0, 0.0), axis=0, keepdims=True).astype(I32)
    negative, valid = owner >= 64, owner < 128
    position = jnp.where(negative, position + CAP_T, position)
    owner = owner & 63
    dz = ((owner >> 3) - z + 8) & 7
    step_z = sum(jnp.where(dz == d, j, 0) for j, d in enumerate(DZ))
    dy, dc = (((owner >> 1) & 3) - y + 4) & 3, ((owner & 1) - core + 2) & 1
    slot = jnp.where(valid, ((7 - dy * 2 - dc) * 8 + step_z) * SLOTS + position, -1)
    left = jnp.where((iota((8, lists), 0) == step_z) & valid, (asked_rows + 1).astype(F32), 0.0)
    right = jnp.where(iota((128, lists), 0) == (owner & 7) * SLOTS + position, 1.0, 0.0)
    ids = lax.dot_general(left, right, NT, precision=HIGHEST, preferred_element_type=F32)
    ids_ref[...] = ((ids + 0.5).astype(I32) - 1)[:, None, :]

    pl.semaphore_wait(barrier, 14 + n - 1)
    for j in range(7):
        dom_copy(ids_ref.at[j], line_ref.at[j], ids_send, ids_recv, z_plus[j] + spot).start()
    pltpu.make_async_copy(ids_ref.at[7], line_ref.at[7], ids_recv).start()
    for load in loads:
        load.wait()

    def split(start, stop):
        @pl.loop(start, stop)
        def _(i):
            at = pl.multiple_of(i * 16, 16)
            for t, v in zip(tables, parts(et_ref[pl.ds(at, 16), :], 3), strict=True):
                t[pl.ds(at, 16), :] = v

    split(0, width // 32)
    pltpu.make_async_copy(ids_ref, line_ref, ids_recv).wait()
    for m in range(7):
        dom_copy(line_ref, asked_ref.at[8 * m : 8 * m + 8], line_send, line_recv, z * 8 + spot_plus(m)).start()
    pltpu.make_async_copy(line_ref, asked_ref.at[56:64], line_recv).start()

    split(width // 32, width // 16)
    for t in tables:
        for k in range(1, 8):
            t[MAIN + 16 * k : MAIN + 16 * (k + 1), :] = t[MAIN : MAIN + 16, :]

    pltpu.make_async_copy(asked_ref, asked_ref, line_recv).wait()

    @pl.loop(0, 8)
    def _(m):
        at = pl.multiple_of(m * 8, 8)
        col = id_column(asked_ref[pl.ds(at, 8)], spot * SLOTS)
        hot = onehot(iota((8 * SLOTS, rows), 1) == col)
        oh_ref[pl.ds(pl.multiple_of(m * 8 * SLOTS, 8 * SLOTS), 8 * SLOTS), :] = hot
        got = dot_parts(hot, [t[...] for t in tables], NT)
        place = iota((8, SLOTS, 128), 1)
        lane = iota((8, SLOTS, 128), 2)
        rest = got[:, MAIN:].reshape(8, SLOTS, 128)
        rest = jnp.where((lane >> 4) == (place & 7), rest, 0.0)
        one = jnp.sum(jnp.where(place < 8, rest, 0.0), axis=1, keepdims=True)
        two = jnp.sum(jnp.where(place < 8, 0.0, rest), axis=1, keepdims=True)
        for k, part in enumerate((one, two, jnp.zeros_like(one))):
            main = got[:, 128 * k : 128 * (k + 1)].reshape(8, SLOTS, 128)
            served_ref[pl.ds(at, 8), :, 128 * k : 128 * (k + 1)] = jnp.where(place == SLOTS - 1, part, main)
        to = spot_minus(m)

        def start(i, j):
            dom_copy(served_ref.at[i, high], fetched_ref.at[i, high], serve_send, high_recv, z_minus[j] + to).start()

        for j in range(7):
            start(m * 8 + j, j)

        @pl.when(m < 7)
        def _():
            start(m * 8 + 7, 7)

    pltpu.make_async_copy(served_ref.at[others, high], fetched_ref.at[others, high], high_recv).start()

    def start_low(i, m, j):
        dom_copy(
            served_ref.at[i, low], fetched_ref.at[i, low], serve_send, serve_recv.at[m], z_minus[j] + spot_minus(m)).start()

    to_all(start_low, lambda: pltpu.make_async_copy(
        served_ref.at[others, low], fetched_ref.at[others, low], serve_recv.at[7]).start())

    hot = onehot(iota((edges, rows), 1) == column(head_row))
    oh_ref[slots:, :] = hot
    got = dot_parts(hot, [t[...] for t in tables], NT)
    head_emb[:, 0:MAIN] = got[:, 0:MAIN]
    head_emb[:, MAIN:WIDE] = jnp.where(iota((edges, 128), 1) < width - MAIN, got[:, MAIN:WIDE], 0.0)
    groups = rel_ref.shape[0]
    hot = onehot(iota((edges, groups), 1) == column(rel_id))
    rel_rows[:, 0:width] = dot_parts(hot, parts(rel_ref[...], 3))
    rel_rows[:, width:WIDE] = jnp.zeros((edges, WIDE - width), F32)
    query_ref[...] = head_emb[...] * rel_rows[...]

    slot_col = column(slot)
    fold = fold_matrix(256, 128)
    pltpu.make_async_copy(served_ref.at[:, high], fetched_ref.at[:, high], high_recv).wait()
    packed = parts(fetched_ref[:, SLOTS - 1, 0:256], 3)

    def remainders(at):
        where = slot_col[at]
        count = where.shape[0]
        rest = dot_parts(onehot(iota((count, peers), 1) == (where >> 4)), packed)
        rest = jnp.where((iota((count, 256), 1) >> 4) == (where & 15), rest, 0.0)
        return sum(dot(p, fold, NN) for p in parts(rest, 3))

    own = slice(edges, edges + quarter)
    line = iota((quarter, peers * 8), 1)
    hot = onehot((line >> 3) * SLOTS + 8 + (line & 7) == slot_col[own])
    negs_ref[g, :, 0:MAIN] = dot_parts(hot, parts(fetched_ref[:, 8:SLOTS, :].reshape(peers * 8, MAIN), 3))
    negs_ref[g, :, MAIN:WIDE] = remainders(own)

    def rel_copy(src, dst, send, recv, k):
        return pltpu.make_async_remote_copy(
            src, dst, send, recv, device_id={"rel": lax.rem(g + k, n)}, device_id_type=MESH)

    copies = [rel_copy(negs_ref.at[g], negs_ref.at[g], neg_send.at[k - 1], neg_recv.at[k - 1], k) for k in range(1, n)]
    for copy in copies:
        copy.start()
    tails = slice(0, edges)
    got_ref[:, 0:MAIN] = jnp.zeros((edges, MAIN), F32)
    got_ref[:, MAIN:WIDE] = remainders(tails)

    def unpack(b):
        at = pl.ds(pl.multiple_of(b * 16, 16), 16)
        for k in range(2):
            part = pl.ds(pl.multiple_of(b * 16, 16) + 8 * k, 8)
            pltpu.make_async_copy(served_ref.at[part, low], fetched_ref.at[part, low], serve_recv.at[2 * b + k]).wait()
        hot = onehot(iota((edges, 16 * SLOTS), 1) + b * (16 * SLOTS) == slot_col[tails])
        got_ref[:, 0:MAIN] += dot_parts(hot, parts(fetched_ref[at].reshape(16 * SLOTS, MAIN), 3))

    pl.loop(0, 3)(unpack)

    for copy in copies:
        copy.wait_recv()
    sent = list(copies)

    def neg_rows(c):
        return negs_ref[...].reshape(negs, WIDE)[c * SPAN : (c + 1) * SPAN]

    for c in range(edges // SPAN):
        at = slice(c * SPAN, (c + 1) * SPAN)
        score_ref[at] = lax.dot_general(query_ref[at], neg_rows(c), NT, precision=HIGHEST, preferred_element_type=F32)
    tail_hot[...] = onehot(iota((slots, edges), 0) == slot[:, 0:edges])
    line = iota((peers * 8, quarter), 0)
    neg_hot[...] = onehot((line >> 3) * SLOTS + 8 + (line & 7) == slot[:, own])
    unpack(3)

    positive = jnp.sum(query_ref[...] * got_ref[...], axis=1, keepdims=True)
    scores = score_ref[...]
    row_max = jnp.maximum(positive, jnp.max(scores, axis=1, keepdims=True))
    pos_exp = jnp.exp(positive - row_max)
    neg_exp = jnp.exp(scores - row_max)
    total = pos_exp + jnp.sum(neg_exp, axis=1, keepdims=True)
    pos_coef = pos_exp / total - 1.0
    neg_coef = neg_exp / total
    turned = [neg_coef[c * SPAN : (c + 1) * SPAN].T for c in range(edges // SPAN)]

    def neg_grads(at):
        for c in range(edges // SPAN):
            queries = query_ref[c * SPAN : (c + 1) * SPAN, at]
            grad_neg = lax.dot_general(turned[c], queries, NN, precision=HIGHEST, preferred_element_type=F32)
            first = c * SPAN
            while first < (c + 1) * SPAN:
                q, inside = divmod(first, quarter)
                count = min(quarter - inside, (c + 1) * SPAN - first)
                gn_ref[q, inside : inside + count, at] = grad_neg[first - c * SPAN : first - c * SPAN + count]
                first += count

    right_hand, left_hand, far = lax.rem(g + 1, n), lax.rem(g + 3, n), lax.rem(g + 2, n)
    to_of, back_of = (right_hand, left_hand), (left_hand, right_hand)
    top, bottom = slice(0, quarter // 2), slice(quarter // 2, quarter)
    two_hops, one_hop = (top, bottom), (bottom, top)

    part_cols = (slice(0, 128), slice(128, WIDE))

    def gn_copy(part, way, step, src):
        copy = pltpu.make_async_remote_copy(
            src, gn_held.at[way, step, :, part_cols[part]], gn_send.at[part, way, step], gn_recv.at[part, way, step],
            device_id={"rel": to_of[way]}, device_id_type=MESH)
        copy.start()
        sent.append(copy)
        return copy

    def gn_begin(part):
        at = part_cols[part]
        two = [gn_copy(part, way, 0, gn_ref.at[far, two_hops[way], at]) for way in range(2)]
        return two, [gn_copy(part, way, 1, gn_ref.at[to_of[way], one_hop[way], at]) for way in range(2)]

    def gn_add(part, begun):
        at = part_cols[part]
        for way in range(2):
            begun[0][way].wait_recv()
            gn_sums[way, :, at] = gn_ref[to_of[way], two_hops[way], at] + gn_held[way, 0, :, at]
            begun[1].append(gn_copy(part, way, 2, gn_sums.at[way, :, at]))

    def gn_total(part, begun):
        at = part_cols[part]
        for copy in begun[1]:
            copy.wait_recv()
        return jnp.concatenate(
            [gn_ref[g, two_hops[way], at] + gn_held[way, 2, :, at] + gn_held[1 - way, 1, :, at] for way in range(2)], axis=0)

    neg_grads(part_cols[0])
    begun = [gn_begin(0)]
    gt_ref[...] = pos_coef * query_ref[...]

    def send_back(k, part, at):
        def start(i, m, j):
            dom_copy(
                back_ref.at[k, i, at], recv_ref.at[k, i, at], back_send, back_recv.at[part], z_plus[j] + spot_plus(m)).start()

        def own():
            pltpu.make_async_copy(back_ref.at[k, others, at], recv_ref.at[k, others, at], back_recv.at[part]).start()

        to_all(start, own)

    def pack_tails(k):
        back_ref[k] = dot_parts(tail_hot[...], parts(gt_ref[:, 128 * k : 128 * (k + 1)], 2)).reshape(peers, SLOTS, 128)

    pack_tails(0)
    send_back(0, 0, low)
    neg_grads(part_cols[1])
    gn_add(0, begun[0])
    begun.append(gn_begin(1))

    spread = spread_matrix(128, 256)

    def remainders_back(values, at):
        count = values.shape[0]
        rest = sum(dot(p, spread, NN) for p in parts(values, 2))
        rest = jnp.where((iota((count, 256), 1) >> 4) == (slot_col[at] & 15), rest, 0.0)
        return dot_parts(onehot(iota((peers, count), 0) == (slot[:, at] >> 4)), parts(rest, 2))

    rest = remainders_back(gt_ref[:, MAIN:WIDE], slice(0, edges))
    last = iota((peers, 8, 128), 1) == 7

    def pack_rest(k, grad_neg, rest):
        more = dot_parts(neg_hot[...], parts(grad_neg, 2)).reshape(peers, 8, 128)
        more = back_ref[k, :, 8:SLOTS, :] + more
        if k < 2:
            more = jnp.where(last, rest[:, 128 * k : 128 * (k + 1)][:, None, :], more)
        back_ref[k, :, 8:SLOTS, :] = more
        send_back(k, k + 1, high if k == 0 else all_rows)

    pack_rest(0, gn_total(0, begun[0]), rest)
    gn_add(1, begun[1])
    pack_tails(1)
    grad_neg = gn_total(1, begun[1])
    rest = rest + remainders_back(grad_neg[:, MAIN - 128 :], own)
    pack_rest(1, grad_neg[:, 0:128], rest)

    gr_parts = []
    for c in range(edges // SPAN):
        at = slice(c * SPAN, (c + 1) * SPAN)
        grad_query = pos_coef[at] * got_ref[at] + lax.dot_general(
            neg_coef[at], neg_rows(c), NN, precision=HIGHEST, preferred_element_type=F32)
        gh_ref[at] = grad_query * rel_rows[at]
        hot = onehot(iota((groups, SPAN), 0) == rel_id[:, at])
        gr_parts.append(dot_parts(hot, parts(grad_query * head_emb[at], 3)))
    gr_ref[...] = sum(gr_parts)[:, None, :]

    slab_ref = et_ref
    piece = rows // n
    first_row = [128 * k for k in range(CHUNKS)]
    height = [128] * (CHUNKS - 1) + [width - 128 * (CHUNKS - 1)]

    def cols(j):
        return pl.ds(pl.multiple_of(j * piece, piece), piece)

    ring = {}

    def half(k, way, mine):
        h = height[k] // 2
        low = (way == 0) == mine
        return slice(first_row[k], first_row[k] + h) if low else slice(first_row[k] + h, first_row[k] + 2 * h)

    def send(k, way, step, src, dst):
        copy = pltpu.make_async_remote_copy(
            src, dst, ring_send.at[k, way, step], ring_recv.at[k, way, step],
            device_id={"rel": to_of[way]}, device_id_type=MESH)
        copy.start()
        ring[k, way, step] = copy

    def arrived(k, part, at):
        pltpu.make_async_copy(back_ref.at[k, :, at], recv_ref.at[k, :, at], back_recv.at[part]).wait()

    def scatter(k):
        if k == 0:
            arrived(0, 0, low)
            arrived(0, 1, high)
        else:
            arrived(k, k + 1, all_rows)
        values = [recv_ref[k].reshape(slots, 128).T, gh_ref[:, 128 * k : 128 * (k + 1)].T]
        vt = jnp.concatenate(values, axis=1)
        if k == CHUNKS - 1:
            rest = jnp.concatenate([recv_ref[0, :, SLOTS - 1, :], recv_ref[1, :, SLOTS - 1, :]], axis=1)
            rest = jnp.broadcast_to(rest[:, None, :], (peers, SLOTS, 256))
            own = (iota((peers, SLOTS, 256), 2) >> 4) == iota((peers, SLOTS, 256), 1)
            rest = jnp.where(own, rest, 0.0).reshape(slots, 256)
            rest = sum(dot(p, fold, NN) for p in parts(rest, 2))
            more = jnp.concatenate([rest.T[0:16], gh_ref[:, MAIN:WIDE].T[0:16]], axis=1)
            vt = jnp.concatenate([vt, more], axis=0)
        h = height[k]
        vt_ref[0:h], vt_ref[h : 2 * h] = parts(vt, 2)

        @pl.loop(0, n)
        def _(j):
            at = cols(j)
            both = dot(vt_ref[0 : 2 * h], oh_ref[:, at], NN)
            slab_ref[first_row[k] : first_row[k] + h, at] = both[0:h] + both[h : 2 * h]

    def begin(k):
        h = height[k] // 2
        for way in range(2):
            send(k, way, 0, slab_ref.at[half(k, way, True), cols(far)], held_ref.at[k, way, 0, 0:h])
        for way in range(2):
            send(k, way, 1, slab_ref.at[half(k, way, False), cols(to_of[way])], held_ref.at[k, way, 1, 0:h])

    def add(k):
        h = height[k] // 2
        for way in range(2):
            ring[k, way, 0].wait_recv()
            sums_ref[k, way, 0:h] = slab_ref[half(k, way, True), cols(to_of[way])] + held_ref[k, way, 0, 0:h]
            send(k, way, 2, sums_ref.at[k, way, 0:h], held_ref.at[k, way, 2, 0:h])

    def share(k):
        h = height[k] // 2
        for way in range(2):
            ring[k, way, 1].wait_recv()
            ring[k, way, 2].wait_recv()
        for way in range(2):
            at = half(k, way, True)
            out_ref[at, cols(g)] = slab_ref[at, cols(g)] + held_ref[k, way, 2, 0:h] + held_ref[k, 1 - way, 1, 0:h]
        for step, mine_too in ((3, True), (4, False)):
            for way in range(2):
                at = half(k, way, mine_too)
                send(k, way, step, out_ref.at[at, cols(g)], out_ref.at[at, cols(g)])

    def forward(k):
        for way in range(2):
            ring[k, way, 3].wait_recv()
            at = half(k, way, True)
            send(k, way, 5, out_ref.at[at, cols(back_of[way])], out_ref.at[at, cols(back_of[way])])

    scatter(0)
    begin(0)
    pack_tails(2)
    pack_rest(2, grad_neg[:, 128:256], rest)
    add(0)
    share(0)
    scatter(1)
    begin(1)

    def start_rel(i, m, j):
        to = z_plus[j] + spot_plus(m)
        dom_copy(gr_ref.at[to], gr_recv.at[i], gr_send, gr_got, to).start()

    to_all(start_rel, lambda: pltpu.make_async_copy(gr_ref.at[me], gr_recv.at[others], gr_got).start())
    forward(0)
    add(1)
    share(1)
    scatter(2)
    begin(2)
    forward(1)
    pltpu.make_async_copy(gr_ref, gr_recv, gr_got).wait()
    gr_sum[0] = jnp.sum(gr_recv[...], axis=0)

    def start_sum(i, m, j):
        dom_copy(gr_sum.at[0], rel_recv.at[me], ag_send, ag_recv, z_plus[j] + spot_plus(m)).start()

    to_all(start_sum, lambda: pltpu.make_async_copy(gr_sum.at[0], rel_recv.at[me], ag_recv).start())
    add(2)
    share(2)
    pltpu.make_async_copy(gr_ref, rel_recv, ag_recv).wait()
    rel_out[...] = rel_recv[:, 0, :][:, 0:width]
    forward(2)

    first = pl.ds(0, others)
    seven = pl.ds(0, 7)
    pltpu.make_async_copy(ids_ref.at[seven], ids_ref.at[seven], ids_send).wait()
    pltpu.make_async_copy(asked_ref.at[0:56], asked_ref.at[0:56], line_send).wait()
    pltpu.make_async_copy(served_ref.at[first], served_ref.at[first], serve_send).wait()
    pltpu.make_async_copy(gr_ref.at[first], gr_ref.at[first], gr_send).wait()
    pltpu.make_async_copy(gr_ref.at[first], gr_ref.at[first], ag_send).wait()
    for k in range(CHUNKS):
        pltpu.make_async_copy(back_ref.at[k, first], back_ref.at[k, first], back_send).wait()
    for copy in [*sent, *ring.values()]:
        copy.wait_send()
    for k in range(CHUNKS):
        for way in range(2):
            ring[k, way, 4].wait_recv()
            ring[k, way, 5].wait_recv()


def body(embeddings, rel_weight, head_row, rel_id, tail_owner, tail_row, neg_owner, neg_row):
    peers, n = lax.axis_size("dom"), lax.axis_size("rel")
    rows, width = embeddings.shape
    edges, negs = head_row.shape[0], neg_row.shape[0]
    groups = rel_weight.shape[0]
    quarter = negs // n
    lists = WIDE
    slots = peers * SLOTS
    tall = (width - 128 * (CHUNKS - 1)) // 2
    lists_of = (tail_row, head_row, rel_id, neg_row)
    ends = [sum(a.shape[0] for a in lists_of[: k + 1]) for k in range(len(lists_of))]
    joined = sum(jnp.pad(a, (end - a.shape[0], ends[-1] - end)) for a, end in zip(lists_of, ends, strict=True))
    V, DMA = pltpu.VMEM, pltpu.SemaphoreType.DMA
    vmem, in_hbm = pl.BlockSpec(memory_space=pltpu.VMEM), pl.BlockSpec(memory_space=pltpu.HBM)
    scratch = [
        V((groups, width), F32), V((width, rows), F32), V((WIDE, rows), BF16), V((WIDE, rows), BF16), V((WIDE, rows), BF16),
        V((slots + edges, rows), BF16), V((8, 1, 128), I32), V((8, 1, 128), I32), V((peers, 1, 128), I32),
        V((peers, SLOTS, MAIN), F32), V((peers, SLOTS, MAIN), F32), V((edges, WIDE), F32), V((n, quarter, WIDE), F32),
        V((edges, WIDE), F32), V((edges, WIDE), F32), V((edges, WIDE), F32), V((edges, WIDE), F32), V((edges, WIDE), F32),
        V((n, quarter, WIDE), F32), V((2, 3, quarter // 2, WIDE), F32), V((2, quarter // 2, WIDE), F32),
        V((CHUNKS, peers, SLOTS, 128), F32), V((CHUNKS, peers, SLOTS, 128), F32),
        V((4 * tall, slots + edges), BF16),
        V((CHUNKS, 2, 3, tall, rows // n), F32), V((CHUNKS, 2, tall, rows // n), F32),
        V((groups, 1, WIDE), F32), V((peers, 1, WIDE), F32), V((1, 1, WIDE), F32), V((groups, 1, WIDE), F32),
        V((edges, SPAN), F32), V((slots, edges), BF16), V((peers * 8, quarter), BF16),
        DMA((2,)), DMA(()), DMA(()), DMA(()), DMA(()), DMA(()), DMA(()), DMA((8,)), DMA((n - 1,)), DMA((n - 1,)), DMA((2, 2, 3)), DMA((2, 2, 3)),
        DMA(()), DMA((CHUNKS + 1,)), DMA(()), DMA(()), DMA(()), DMA(()), DMA((CHUNKS, 2, 6)), DMA((CHUNKS, 2, 6)),
    ]
    total, relation = pl.pallas_call(
        kernel,
        out_shape=(jax.ShapeDtypeStruct((width, rows), F32), jax.ShapeDtypeStruct((groups, width), F32)),
        in_specs=[vmem, vmem, vmem, in_hbm, in_hbm],
        out_specs=(vmem, vmem),
        scratch_shapes=scratch,
        compiler_params=pltpu.CompilerParams(collective_id=0, has_side_effects=True, vmem_limit_bytes=48 << 20),
        cost_estimate=pl.CostEstimate(flops=int(3e10), bytes_accessed=7 << 20, transcendentals=0),
        name="ranking_gradients",
    )(joined, tail_owner.reshape(1, edges), neg_owner.reshape(1, negs), rel_weight, embeddings.T)
    return (total.T, relation)


def solution(mesh):
    return jax.shard_map(
        body,
        mesh=mesh,
        in_specs=(
            P("dom", None),
            P("rel", None),
            P(("dom", "rel")),
            P(("dom", "rel")),
            P(("dom", "rel"), None),
            P(("dom", "rel")),
            P("dom", None),
            P("dom"),
        ),
        out_specs=(P("dom", None), P("rel", None)),
        check_vma=False,
    )
```
